256 devices in a mesh: dp: 4 (over x), expert: 64 (over z, y, core).
Axes of the slice: x: 4, y: 4, z: 8, core: 2. Of those that a mesh axis runs over, the one named last changes fastest.
Arguments:
- tokens: bfloat16 [2, 16384, 3584], P(None, ('dp', 'expert')), may hold values from -6 to 6
- expert_ids: int32 [2, 16384, 1], P(None, ('dp', 'expert')), may hold values from 0 to 31; in each aligned block of 64 rows (0 to 63, 64 to 127, ..., all dimensions but the last counted through in order) at most 3 rows name the same one
- gate_values: float32 [2, 16384, 1], P(None, ('dp', 'expert')), may hold values from 0.2 to 1
- w_gate: bfloat16 [3584, 32768], P('dp', 'expert'), may hold values from -0.09375 to 0.09375
- w_up: bfloat16 [3584, 32768], P('dp', 'expert'), may hold values from -0.09375 to 0.09375
- w_down: bfloat16 [32768, 3584], P('expert', 'dp'), may hold values from -0.1875 to 0.1875
- cotangent: bfloat16 [2, 16384, 3584], P(None, ('dp', 'expert')), may hold values from -6 to 6
Outputs:
- layer_out: bfloat16 [2, 16384, 3584], P(None, ('dp', 'expert'))
- tokens_grad: bfloat16 [2, 16384, 3584], P(None, ('dp', 'expert'))
- grad_gate: bfloat16 [3584, 32768], P('dp', 'expert')
- grad_up: bfloat16 [3584, 32768], P('dp', 'expert')
- grad_down: bfloat16 [32768, 3584], P('expert', 'dp')
The draws below stay inside these ranges and needn't reach their ends.
Inputs may be any that keep to these rules, and one draw needn't show every extreme that they name: `expert_ids`: of the 64 tokens of one device in one micro-batch, at most 3 name the same expert, and in some micro-batch of some device exactly 3 do.
All inputs are finite; a program needn't handle non-finite values.
Results may differ from the reference program's by a relative error of at most 0.013.
Values may be sent and summed in bfloat16 or wider, within the bound.
No kernel may reach another device: no remote copies, remote signals or barrier semaphores. Data moves between devices by JAX's collectives and lax.ppermute only.
A program may use at most 128 MiB of HBM per device.

```python
import math
import jax
import jax.numpy as jnp
import numpy as np
from jax import lax

D = 3584
FF_WIN = 1024
SHARDS = 2
TOP = 1
MB = 2
TOK_MB = 64
EXPERTS = 32
CAP = 3
REPLICA_ROWS = 4096
TOKENS = 16384
N_DP = 4
N_EXPERT = 64


def shard_levels(own_key, shape, split, low, largest):
    factor_of = 1.0
    for dim, blocks in split:
        heights = jax.random.uniform(jax.random.fold_in(jax.random.fold_in(own_key, 6), dim), (blocks,), jnp.float32, low / len(split), largest / len(split))
        factor_of = factor_of * jnp.repeat(jnp.exp(heights), shape[dim] // blocks).reshape((-1,) + (1,) * (len(shape) - 1 - dim))
    return factor_of


def deal_out(stream_key, own, number, rows, count, top, reach, slope):
    sequence = jax.random.permutation(stream_key, count)
    heavy_load, usual = load_shares(count, rows * top, reach, slope, True), load_shares(count, rows * top, reach, slope, False)
    places = jnp.arange(count)

    def named(sizes, rotation):
        used = int((sizes > 0).sum())
        fixed = max(1, used // 4)
        passed = fixed + (places - fixed + rotation * (used - fixed)) % max(1, count - fixed)
        return jnp.zeros((count,), jnp.int32).at[sequence[jnp.where(places < fixed, places, passed)]].set(jnp.asarray(sizes, jnp.int32))

    sizes = jnp.where(number % 4 == 0, named(heavy_load, number // 4), named(usual, number - number // 4 - 1))
    mixed = jax.random.permutation(jax.random.fold_in(own, 3), count)
    giver, taker = mixed[0:count // 2 * 2:2], mixed[1:count // 2 * 2:2]
    slack = jnp.minimum(sizes[giver] - 1, reach - sizes[taker]) // 2
    slack = jnp.where((giver == sequence[0]) | (taker == sequence[0]) | (sizes[taker] == 0), 0, jnp.maximum(slack, 0))
    passed = jax.random.randint(jax.random.fold_in(own, 4), (count // 2,), 0, 1 << 20) % (slack + 1)
    sizes = sizes.at[giver].add(-passed).at[taker].add(passed)
    labels = jnp.searchsorted(jnp.cumsum(sizes), jnp.arange(rows * top), side="right").astype(jnp.int32)
    listing = labels.reshape(top, rows).T
    listing = listing[jax.random.permutation(jax.random.fold_in(own, 1), rows)]
    rotation = jax.random.randint(jax.random.fold_in(own, 2), (rows, 1), 0, top)
    return jnp.take_along_axis(listing, (jnp.arange(top)[None, :] + rotation) % top, axis=1)


def load_shares(count, total, most, slope, full):
    weights = [(1 << 20) // math.isqrt(standing ** slope) + 1 for standing in range(1, count + 1)]
    largest = most if full else min(most, max(-(-total // count), total * weights[0] // sum(weights)))
    least = 1 if total - largest >= count - 1 else 0
    holding, surplus = [largest] + [least] * (count - 1), total - largest - least * (count - 1)
    while surplus > 0:
        candidates = [i for i in range(1, count) if holding[i] < largest] or [i for i in range(1, count) if holding[i] < most]
        pool, left = sum([weights[i] for i in candidates]), surplus
        for i in candidates:
            more = min(most - holding[i], max(1, left * weights[i] // pool), surplus)
            holding[i] = holding[i] + more
            surplus = surplus - more
    return np.array(holding)


def bell_draw(own_key, dims, deviation, limit, shards=(), held_as=jnp.bfloat16):
    factor_of = shard_levels(own_key, dims, shards, -0.22, 0.18) if shards else 1.0
    array = jax.random.normal(own_key, dims, jnp.float32) * deviation * factor_of
    return jnp.minimum(jnp.maximum(array, -limit), limit).astype(held_as)


def setup_inputs(seed: int = 0) -> dict:
    key_of = jax.random.split(jax.random.key(seed), 8)
    tokens = bell_draw(key_of[0], (MB, TOKENS, D), 1.0, 6.0, ((1, 256),))
    expert_ids_keys = jax.random.split(jax.random.fold_in(key_of[1], 1), MB * TOKENS // TOK_MB)
    expert_ids_turns = jax.random.permutation(jax.random.fold_in(key_of[1], 3), MB * TOKENS // TOK_MB)
    expert_ids = jax.vmap(lambda own, number: deal_out(jax.random.fold_in(key_of[1], 2), own, number, TOK_MB, EXPERTS, TOP, CAP, 2))(expert_ids_keys, expert_ids_turns).reshape((MB, TOKENS, TOP))
    gate_values = jnp.clip(0.2 + 0.8 * jax.random.uniform(key_of[2], (MB, TOKENS, TOP), jnp.float32) ** shard_levels(key_of[2], (MB, TOKENS, TOP), ((1, 256),), -0.2, 0.2), 0.2, 1.0)
    w_gate = bell_draw(key_of[3], (D, EXPERTS * FF_WIN), D ** -0.5, 0.09375, ((0, 4), (1, 64)))
    w_up = bell_draw(key_of[4], (D, EXPERTS * FF_WIN), D ** -0.5, 0.09375, ((0, 4), (1, 64)))
    w_down = bell_draw(key_of[5], (EXPERTS * FF_WIN, D), FF_WIN ** -0.5, 0.1875, ((0, 64), (1, 4)))
    cotangent = bell_draw(key_of[6], (MB, TOKENS, D), 1.0, 6.0, ((1, 256),))
    return dict(tokens=tokens, expert_ids=expert_ids, gate_values=gate_values, w_gate=w_gate, w_up=w_up, w_down=w_down, cotangent=cotangent)


def positions(expert_block):
    onehot = (expert_block[:, :, None] == jnp.arange(EXPERTS, dtype=jnp.int32)[None, None, :]).astype(jnp.int32)
    earlier = jnp.cumsum(onehot, axis=1) - onehot
    slot_index = jnp.sum(earlier * onehot, axis=2).astype(jnp.int32)
    source = jnp.arange(N_EXPERT, dtype=jnp.int32)[:, None]
    return (source * CAP + slot_index).reshape(-1).astype(jnp.int32)


def one_expert(packed):
    token_rows, slopes, gate_w, up_w, down_w = packed
    share_width = FF_WIN // SHARDS
    pre_gate = jnp.dot(token_rows, gate_w, preferred_element_type=jnp.float32)
    pre_up = jnp.dot(token_rows, up_w, preferred_element_type=jnp.float32)
    sigmoid_gate = jax.nn.sigmoid(pre_gate)
    silu_gate = pre_gate * sigmoid_gate
    hidden = (silu_gate * pre_up).astype(jnp.bfloat16)
    down_shares = down_w.reshape(SHARDS, share_width, D).astype(jnp.float32)
    hidden_shares = hidden.reshape(-1, SHARDS, share_width).astype(jnp.float32)
    partial_value = jnp.einsum("rqh,qhd->rqd", hidden_shares, down_shares, precision=lax.Precision.HIGHEST).astype(jnp.bfloat16)
    back_hidden = lax.dot_general(slopes, down_w, (((1,), (1,)), ((), ())), preferred_element_type=jnp.float32)
    slope_gate = sigmoid_gate * (1.0 + pre_gate * (1.0 - sigmoid_gate))
    grad_pre_gate = (back_hidden * pre_up * slope_gate).astype(jnp.bfloat16)
    grad_pre_up = (back_hidden * silu_gate).astype(jnp.bfloat16)
    gate_shares = gate_w.T.reshape(SHARDS, share_width, D).astype(jnp.float32)
    up_shares = up_w.T.reshape(SHARDS, share_width, D).astype(jnp.float32)
    from_gate = jnp.einsum("rqh,qhd->rqd", grad_pre_gate.reshape(-1, SHARDS, share_width).astype(jnp.float32), gate_shares, precision=lax.Precision.HIGHEST)
    from_up = jnp.einsum("rqh,qhd->rqd", grad_pre_up.reshape(-1, SHARDS, share_width).astype(jnp.float32), up_shares, precision=lax.Precision.HIGHEST)
    input_part = (from_gate + from_up).astype(jnp.bfloat16)
    gate_term = lax.dot_general(token_rows, grad_pre_gate, (((0,), (0,)), ((), ())), preferred_element_type=jnp.float32)
    up_term = lax.dot_general(token_rows, grad_pre_up, (((0,), (0,)), ((), ())), preferred_element_type=jnp.float32)
    down_term = lax.dot_general(hidden, slopes, (((0,), (0,)), ((), ())), preferred_element_type=jnp.float32)
    return partial_value, input_part, gate_term, up_term, down_term


def reference(tokens, expert_ids, gate_values, w_gate, w_up, w_down, cotangent):
    gate_w = w_gate.reshape(D, EXPERTS, FF_WIN).transpose(1, 0, 2)
    up_w = w_up.reshape(D, EXPERTS, FF_WIN).transpose(1, 0, 2)
    down_w = w_down.reshape(EXPERTS, FF_WIN, D)
    total_gate = jnp.zeros((EXPERTS, D, FF_WIN), jnp.float32)
    total_up = jnp.zeros((EXPERTS, D, FF_WIN), jnp.float32)
    total_down = jnp.zeros((EXPERTS, FF_WIN, D), jnp.float32)
    layer_parts = [[] for number in range(MB)]
    grad_parts = [[] for number in range(MB)]
    block_slots = N_EXPERT * CAP
    for replica in range(N_DP):
        row_start = replica * REPLICA_ROWS
        row_end = row_start + REPLICA_ROWS
        row_buffer = jnp.zeros((EXPERTS, MB * block_slots, D), jnp.bfloat16)
        slope_buffer = jnp.zeros((EXPERTS, MB * block_slots, D), jnp.bfloat16)
        routing = []
        for number in range(MB):
            token_rows = tokens[number, row_start:row_end]
            chosen = expert_ids[number, row_start:row_end, 0].astype(jnp.int32)
            weights_here = gate_values[number, row_start:row_end, 0:1].astype(jnp.float32)
            places = (positions(chosen.reshape(N_EXPERT, TOK_MB)) + number * block_slots).astype(jnp.int32)
            upstream = (weights_here * cotangent[number, row_start:row_end].astype(jnp.float32)).astype(jnp.bfloat16)
            row_buffer = row_buffer.at[chosen, places].set(token_rows.astype(jnp.bfloat16))
            slope_buffer = slope_buffer.at[chosen, places].set(upstream)
            routing.append((chosen, places, weights_here))
        partial_value, input_part, gate_term, up_term, down_term = lax.map(one_expert, (row_buffer, slope_buffer, gate_w, up_w, down_w))
        for number in range(MB):
            chosen, places, weights_here = routing[number]
            combined = jnp.sum(partial_value[chosen, places].astype(jnp.float32), axis=1).astype(jnp.bfloat16)
            combined = lax.optimization_barrier(combined).astype(jnp.float32)
            layer_parts[number].append((weights_here * combined).astype(jnp.bfloat16))
            grad_parts[number].append(jnp.sum(input_part[chosen, places].astype(jnp.float32), axis=1).astype(jnp.bfloat16))
        total_gate = total_gate + lax.optimization_barrier(gate_term.astype(jnp.bfloat16)).astype(jnp.float32)
        total_up = total_up + lax.optimization_barrier(up_term.astype(jnp.bfloat16)).astype(jnp.float32)
        total_down = total_down + lax.optimization_barrier(down_term.astype(jnp.bfloat16)).astype(jnp.float32)
    layer_out = jnp.stack([jnp.concatenate(layer_parts[number], axis=0) for number in range(MB)], axis=0)
    tokens_grad = jnp.stack([jnp.concatenate(grad_parts[number], axis=0) for number in range(MB)], axis=0)
    grad_gate = total_gate.astype(jnp.bfloat16).transpose(1, 0, 2).reshape(D, EXPERTS * FF_WIN)
    grad_up = total_up.astype(jnp.bfloat16).transpose(1, 0, 2).reshape(D, EXPERTS * FF_WIN)
    grad_down = total_down.astype(jnp.bfloat16).reshape(EXPERTS * FF_WIN, D)
    return (layer_out, tokens_grad, grad_gate, grad_up, grad_down)
```

```python
import functools

import jax
import jax.numpy as jnp
from jax import lax
from jax.experimental import pallas as pl
from jax.experimental.pallas import tpu as pltpu
from jax.sharding import PartitionSpec as P

BF = jnp.bfloat16
F32 = jnp.float32
LIMIT = 56 * 1024 * 1024


def dot(a, b):
    return jnp.dot(a, b, preferred_element_type=F32)


def dot_t(a, b):
    return lax.dot_general(a, b, (((1,), (1,)), ((), ())), preferred_element_type=F32)


def tdot(a, b):
    return lax.dot_general(a, b, (((0,), (0,)), ((), ())), preferred_element_type=F32)


def onehot(cond):
    return jnp.where(cond, 1.0, 0.0).astype(BF)


def iota(shape, dim):
    return lax.broadcasted_iota(jnp.int32, shape, dim)


def as_column(row):
    n = row.shape[1]
    return jnp.sum(jnp.where(iota((n, n), 0) == iota((n, n), 1), row, 0), axis=1, keepdims=True)


def slot_matrices(place, rows):
    n = place.shape[1]
    at = iota((rows, n), 0)
    base = place // 8 * 8
    slot = place - base
    main = onehot(at == place)
    tail = base + 6 + slot % 2
    return [
        jnp.concatenate([main, onehot((at == tail) & (slot // 2 == j))], axis=1) for j in range(3)
    ]


def pack_kernel(ids, gate, tokens, cot, out, place_out):
    n = ids.shape[1]
    half = n // 2
    q = tokens.shape[1] // 4
    earlier, later = iota((n, n), 0), iota((n, n), 1)
    same = (as_column(ids[...]) == ids[...]) & (earlier < later) & (earlier // half == later // half)
    rank = jnp.sum(jnp.where(same, 1, 0), axis=0, keepdims=True)
    place = ids[...] * 8 + iota((1, n), 1) // half * 3 + rank
    place_out[...] = place
    choose = slot_matrices(place, out.shape[0])
    weight = as_column(gate[...])
    for kind in range(2):
        def part(j):
            rows = (tokens if kind == 0 else cot)[:, j * q : (j + 1) * q]
            return rows if kind == 0 else (weight * rows.astype(F32)).astype(BF)
        last = part(3)
        for j in range(3):
            both = jnp.concatenate([part(j), last], axis=0)
            lo = (kind * 3 + j) * q
            out[:, lo : lo + q] = dot(choose[j], both).astype(BF)


def unpack_kernel(place, gate, back, layer, grad):
    n = place.shape[1]
    q = layer.shape[1] // 4
    choose = slot_matrices(place[...], back.shape[0])
    weight = as_column(gate[...])
    for kind in range(2):
        def put(j, rows):
            if kind == 0:
                layer[:, j * q : (j + 1) * q] = (weight * rows.astype(BF).astype(F32)).astype(BF)
            else:
                grad[:, j * q : (j + 1) * q] = rows.astype(BF)
        last = jnp.zeros((n, q), F32)
        for j in range(3):
            lo = (kind * 3 + j) * q
            got = tdot(choose[j], back[:, lo : lo + q])
            put(j, got[:n])
            last = last + got[n:]
        put(3, last)


def compact_matrices(rows):
    r, p = iota((rows // 8 * 6, rows), 0), iota((rows // 8 * 6, rows), 1)
    src, slot = r // 6, r % 6
    tail = src * 8 + 6 + slot % 2
    return onehot(p == src * 8 + slot), [onehot((p == tail) & (slot // 2 == j)) for j in range(3)]


def compact_kernel(own, sib, out):
    main, tails = compact_matrices(own.shape[0])
    q = out.shape[3]
    n = main.shape[0]
    for place, source in enumerate((own, sib)):
        for kind in range(2):
            last = jnp.zeros((n, q), F32)
            for j in range(3):
                lo = (kind * 3 + j) * q
                rows = source[:, lo : lo + q]
                out[j, kind, place * n : (place + 1) * n] = dot(main, rows).astype(BF)
                last = last + dot(tails[j], rows)
            out[3, kind, place * n : (place + 1) * n] = last.astype(BF)


def expand_kernel(own, sib, out):
    rows = out.shape[0]
    n = own.shape[2]
    q = own.shape[3]
    p, r = iota((rows, n), 0), iota((rows, n), 1)
    slot = r % 6
    main = onehot(p == r // 6 * 8 + slot)
    tail = r // 6 * 8 + 6 + slot % 2
    choose = [
        jnp.concatenate([main, onehot((p == tail) & (slot // 2 == j))], axis=1) for j in range(3)
    ]
    for kind in range(2):
        def total(j):
            return (own[kind, j].astype(F32) + sib[kind, j].astype(F32)).astype(BF)
        last = total(3)
        for j in range(3):
            lo = (kind * 3 + j) * q
            both = jnp.concatenate([total(j), last], axis=0)
            out[:, lo : lo + q] = dot(choose[j], both).astype(BF)


def gather_copies(pieces, buf, sem, lanes, first):
    half = pieces[3].shape[0]
    views = [
        (buf.at[0, :, lanes], 0),
        (buf.at[1, :, lanes], 1),
        (buf.at[2, :, lanes], 2),
        (buf.at[3, pl.ds(0, half), lanes], 3),
        (buf.at[3, pl.ds(half, half), lanes], 3),
    ]
    return [
        [
            pltpu.make_async_copy(piece, view, sem.at[first + n])
            for n, (piece, (view, at)) in enumerate(zip(pieces, views))
            if at == k
        ]
        for k in range(4)
    ]


SHIFTS = (0, 3, 1, 2)


def forward_kernel(x, rows, *refs):
    gate_parts, up_parts = refs[0:5], refs[5:10]
    hid, slope, silu, to_l, to_r, to_oa, to_ob = refs[10:17]
    w, t, acc, sem, tsem, ssem = refs[17:]
    me = x[0]
    n = rows.shape[2] // 2
    spots = [lax.rem(me + s, 4) for s in SHIFTS]
    width = hid.shape[1]
    gate_c = gather_copies(gate_parts, w, sem, pl.ds(0, width), 0)
    up_c = gather_copies(up_parts, w, sem, pl.ds(width, width), 5)
    row_c = [
        pltpu.make_async_copy(rows.at[spots[k], 0], t.at[k], tsem.at[k]) for k in range(4)
    ]
    for k in range(4):
        for c in [row_c[k]] + gate_c[k] + up_c[k]:
            c.start()
    h = n // 2
    slices = [
        pltpu.make_async_copy(rows.at[spots[1], :, pl.ds(0, n)], to_l, ssem.at[0]),
        pltpu.make_async_copy(rows.at[spots[2], :, pl.ds(0, n)], to_r, ssem.at[1]),
        pltpu.make_async_copy(rows.at[spots[3], :, pl.ds(0, h)], to_oa, ssem.at[2]),
        pltpu.make_async_copy(rows.at[spots[3], :, pl.ds(h, h)], to_ob, ssem.at[3]),
    ]
    for c in slices:
        c.start()
    for k in range(4):
        for c in [row_c[k]] + gate_c[k] + up_c[k]:
            c.wait()
        term = dot(t[k], w[k])
        if k == 0:
            acc[...] = term
        else:
            acc[...] += term
    pre_gate, pre_up = acc[:, :width], acc[:, width:]
    s = jax.nn.sigmoid(pre_gate)
    act = pre_gate * s
    hid[...] = (act * pre_up).astype(BF)
    silu[...] = act
    slope[...] = pre_up * (s * (1.0 + pre_gate * (1.0 - s)))
    for c in slices:
        c.wait()


def backward_kernel(x, hid, slope, silu, rows, *refs):
    gate_parts, up_parts, down_parts = refs[0:5], refs[5:10], refs[10:15]
    own, sib, grads = refs[15:18]
    w, wd, u, o, sem, dsem, usem, osem = refs[18:]
    me = x[0]
    n = rows.shape[2] // 2
    width = hid.shape[1]
    spots = [lax.rem(me + s, 4) for s in SHIFTS]
    gate_c = gather_copies(gate_parts, w, sem, pl.ds(0, width), 0)
    up_c = gather_copies(up_parts, w, sem, pl.ds(width, width), 5)
    q = u.shape[2]
    down_c = gather_copies(down_parts, wd, dsem, pl.ds(0, q), 0)
    row_c = [
        pltpu.make_async_copy(rows.at[spots[k], 1], u.at[k], usem.at[k]) for k in range(4)
    ]
    for k in range(4):
        for c in [row_c[k]] + down_c[k]:
            c.start()
    for k in range(4):
        for c in gate_c[k] + up_c[k]:
            c.start()
    sent = []

    def emit(kind, k, value):
        o[kind, k] = value.astype(BF)
        for number, target in enumerate((own, sib)):
            c = pltpu.make_async_copy(
                o.at[kind, k, pl.ds(number * n, n)],
                target.at[kind, spots[k]],
                osem.at[(kind * 4 + k) * 2 + number],
            )
            c.start()
            sent.append(c)

    back = jnp.zeros(hid.shape, F32)
    for k in range(4):
        for c in [row_c[k]] + down_c[k]:
            c.wait()
        back = back + dot_t(u[k], wd[k])
        emit(0, k, dot(hid[...], wd[k]))
    grads[:, 0:width] = hid[...]
    grads[:, width : 2 * width] = (back * slope[...]).astype(BF)
    grads[:, 2 * width :] = (back * silu[...]).astype(BF)
    for k in range(4):
        for c in gate_c[k] + up_c[k]:
            c.wait()
        emit(1, k, dot_t(grads[:, width:], w[k]))
    for c in sent:
        c.wait()


def weight_kernel(x, rows, *refs):
    mine, theirs = refs[0:4], refs[4:8]
    parts = refs[8:13]
    d_gate, d_up, d_down = refs[13:16]
    t, g, tsem, gsem = refs[16:]
    n = rows.shape[2] // 2
    h = n // 2
    width = d_gate.shape[1]
    copies = [pltpu.make_async_copy(rows.at[x[0]], t.at[:, pl.ds(0, 2 * n)], tsem.at[8])]
    for number, group in enumerate((mine, theirs)):
        base = number * n
        spots = [
            (1, base, n),
            (2, base, n),
            (3, base, h),
            (3, base + h, h),
        ]
        for i, (piece, (k, start, size)) in enumerate(zip(group, spots)):
            copies.append(
                pltpu.make_async_copy(
                    piece, t.at[:, pl.ds(k * 2 * n + start, size)], tsem.at[number * 4 + i]
                )
            )
    spots = [(0, 2 * n), (2 * n, 2 * n), (4 * n, 2 * n), (6 * n, n), (7 * n, n)]
    for i, (piece, (start, size)) in enumerate(zip(parts, spots)):
        copies.append(pltpu.make_async_copy(piece, g.at[pl.ds(start, size)], gsem.at[i]))
    for c in copies:
        c.start()
    for c in copies:
        c.wait()
    both = tdot(t[0], g[:, width:]).astype(BF)
    d_gate[...] = both[:, :width]
    d_up[...] = both[:, width:]
    d_down[...] = tdot(g[:, :width], t[1]).astype(BF)


def vmem():
    return pl.BlockSpec(memory_space=pltpu.VMEM)


def hbm():
    return pl.BlockSpec(memory_space=pl.ANY)


def smem():
    return pl.BlockSpec(memory_space=pltpu.SMEM)


def call(kernel, outs, ins, in_specs, out_specs, scratch=(), flops=0, name=None):
    size = sum(v.size * v.dtype.itemsize for v in ins) + sum(
        v.size * v.dtype.itemsize for v in outs
    )
    return pl.pallas_call(
        kernel,
        out_shape=outs,
        in_specs=in_specs,
        out_specs=out_specs,
        scratch_shapes=list(scratch),
        compiler_params=pltpu.CompilerParams(vmem_limit_bytes=LIMIT),
        cost_estimate=pl.CostEstimate(flops=flops, bytes_accessed=size, transcendentals=0),
        name=name,
    )(*ins)


def shape(*dims, dtype=BF):
    return jax.ShapeDtypeStruct(dims, dtype)


def shift(v, k):
    n = lax.axis_size("dp")
    return lax.ppermute(v, "dp", [(i, (i + k) % n) for i in range(n)])


def sibling(v):
    return lax.ppermute(v, "expert", [(i, i ^ 1) for i in range(lax.axis_size("expert"))])


def ring(v):
    half = v.shape[0] // 2
    left, right = shift(v, 1), shift(v, -1)
    return (v, left, right, shift(left[:half], 1), shift(right[half:], -1))


def exchange(v):
    devices = lax.axis_size("expert")
    groups = [[2 * i + c for i in range(devices // 2)] for c in range(2)]
    cut = v.reshape(devices // 2, 8, v.shape[1])
    cut = lax.all_to_all(
        cut, "expert", split_axis=0, concat_axis=0, axis_index_groups=groups, tiled=True
    )
    return cut.reshape(v.shape)


def body(tokens, expert_ids, gate_values, w_gate, w_up, w_down, cotangent):
    experts = lax.axis_size("expert") // 2
    micro, toks, features = tokens.shape
    q = features // 4
    width = w_gate.shape[1]
    wire = experts * 8
    n = experts * 6
    x = lax.axis_index("dp").astype(jnp.int32).reshape(1)
    gate_parts, up_parts = ring(w_gate), ring(w_up)
    down_parts = ring(w_down)

    ids = expert_ids.reshape(1, micro * toks)
    gates = gate_values.reshape(1, micro * toks)
    packed, place = call(
        pack_kernel,
        [shape(wire, 6 * q), shape(1, micro * toks, dtype=jnp.int32)],
        [ids, gates, tokens.reshape(-1, features), cotangent.reshape(-1, features)],
        [vmem()] * 4,
        [vmem()] * 2,
        flops=2 * 6 * wire * wire * q,
        name="pack",
    )
    arrived = exchange(packed)
    arrived_sib = sibling(arrived)
    rows = call(
        compact_kernel,
        [shape(4, 2, 2 * n, q)],
        [arrived, arrived_sib],
        [vmem()] * 2,
        [vmem()],
        flops=2 * 24 * n * wire * q,
        name="compact",
    )[0]
    dma = pltpu.SemaphoreType.DMA
    hid, slope, silu, to_l, to_r, to_oa, to_ob = call(
        forward_kernel,
        [shape(2 * n, width)]
        + [shape(2 * n, width, dtype=F32)] * 2
        + [shape(2, n, q)] * 2
        + [shape(2, n // 2, q)] * 2,
        [x, rows, *gate_parts, *up_parts],
        [smem()] + [hbm()] * 11,
        [vmem()] * 3 + [hbm()] * 4,
        scratch=[
            pltpu.VMEM((4, q, 2 * width), BF),
            pltpu.VMEM((4, 2 * n, q), BF),
            pltpu.VMEM((2 * n, 2 * width), F32),
            dma((10,)),
            dma((4,)),
            dma((4,)),
        ],
        flops=4 * 2 * n * features * width,
        name="forward",
    )
    from_r, from_l = shift(to_l, -1), shift(to_r, 1)
    from_oa = shift(shift(to_oa, 1), 1)
    from_ob = shift(shift(to_ob, -1), -1)

    own, sib, grads = call(
        backward_kernel,
        [shape(2, 4, n, q)] * 2 + [shape(2 * n, 3 * width)],
        [x, hid, slope, silu, rows, *gate_parts, *up_parts, *down_parts],
        [smem()] + [vmem()] * 3 + [hbm()] * 16,
        [hbm()] * 2 + [vmem()],
        scratch=[
            pltpu.VMEM((4, q, 2 * width), BF),
            pltpu.VMEM((4, width, q), BF),
            pltpu.VMEM((4, 2 * n, q), BF),
            pltpu.VMEM((2, 4, 2 * n, q), BF),
            dma((10,)),
            dma((5,)),
            dma((4,)),
            dma((16,)),
        ],
        flops=8 * 2 * n * features * width,
        name="backward",
    )
    sent = call(
        expand_kernel,
        [shape(wire, 6 * q)],
        [own, sibling(sib)],
        [vmem()] * 2,
        [vmem()],
        flops=2 * 12 * wire * n * q,
        name="expand",
    )[0]
    came = exchange(sent)

    grad_parts = ring(grads)
    mine = (from_l, from_r, from_oa, from_ob)
    theirs = tuple(sibling(v) for v in mine)
    d_gate, d_up, d_down = call(
        weight_kernel,
        [shape(q, width)] * 2 + [shape(width, q)],
        [x, rows, *mine, *theirs, *grad_parts],
        [smem()] + [hbm()] * 14,
        [vmem()] * 3,
        scratch=[
            pltpu.VMEM((2, 8 * n, q), BF),
            pltpu.VMEM((8 * n, 3 * width), BF),
            dma((9,)),
            dma((5,)),
        ],
        flops=6 * 8 * n * q * width,
        name="weights",
    )
    layer_out, tokens_grad = call(
        unpack_kernel,
        [shape(micro * toks, features)] * 2,
        [place, gates, came],
        [vmem()] * 3,
        [vmem()] * 2,
        flops=2 * 6 * wire * wire * q,
        name="unpack",
    )
    return (
        layer_out.reshape(tokens.shape),
        tokens_grad.reshape(tokens.shape),
        d_gate,
        d_up,
        d_down,
    )


def solution(mesh):
    rows = P(None, ("dp", "expert"), None)
    return jax.shard_map(
        body,
        mesh=mesh,
        in_specs=(rows, rows, rows, P("dp", "expert"), P("dp", "expert"), P("expert", "dp"), rows),
        out_specs=(rows, rows, P("dp", "expert"), P("dp", "expert"), P("expert", "dp")),
        check_vma=False,
    )
```

```python
import functools

import jax
import jax.numpy as jnp
from jax import lax
from jax.experimental import pallas as pl
from jax.experimental.pallas import tpu as pltpu
from jax.sharding import PartitionSpec as P

BF = jnp.bfloat16
F32 = jnp.float32
LIMIT = 56 * 1024 * 1024


def dot(a, b):
    return jnp.dot(a, b, preferred_element_type=F32)


def dot_t(a, b):
    return lax.dot_general(a, b, (((1,), (1,)), ((), ())), preferred_element_type=F32)


def tdot(a, b):
    return lax.dot_general(a, b, (((0,), (0,)), ((), ())), preferred_element_type=F32)


def onehot(cond):
    return jnp.where(cond, 1.0, 0.0).astype(BF)


def iota(shape, dim):
    return lax.broadcasted_iota(jnp.int32, shape, dim)


def as_column(row):
    n = row.shape[1]
    return jnp.sum(jnp.where(iota((n, n), 0) == iota((n, n), 1), row, 0), axis=1, keepdims=True)


def slot_matrices(place, rows):
    n = place.shape[1]
    at = iota((rows, n), 0)
    base = place // 8 * 8
    slot = place - base
    main = onehot(at == place)
    tail = base + 6 + slot % 2
    return [
        jnp.concatenate([main, onehot((at == tail) & (slot // 2 == j))], axis=1) for j in range(3)
    ]


def as_row(ref):
    return jnp.concatenate([ref[m] for m in range(ref.shape[0])], axis=1)


def pack_kernel(ids_ref, gate_ref, tokens, cot, out, place_out):
    ids, gate = as_row(ids_ref), as_row(gate_ref)
    n = ids.shape[1]
    half = n // 2
    q = tokens.shape[1] // 4
    earlier, later = iota((n, n), 0), iota((n, n), 1)
    same = (as_column(ids) == ids) & (earlier < later) & (earlier // half == later // half)
    rank = jnp.sum(jnp.where(same, 1, 0), axis=0, keepdims=True)
    place = ids * 8 + iota((1, n), 1) // half * 3 + rank
    place_out[...] = place
    choose = slot_matrices(place, out.shape[0])
    weight = as_column(gate)
    for kind in range(2):
        def part(j):
            rows = (tokens if kind == 0 else cot)[:, j * q : (j + 1) * q]
            return rows if kind == 0 else (weight * rows.astype(F32)).astype(BF)
        last = part(3)
        for j in range(3):
            both = jnp.concatenate([part(j), last], axis=0)
            lo = (kind * 3 + j) * q
            out[:, lo : lo + q] = dot(choose[j], both).astype(BF)


def unpack_kernel(place, gate, back, layer, grad):
    n = place.shape[1]
    q = layer.shape[1] // 4
    choose = slot_matrices(place[...], back.shape[0])
    weight = as_column(as_row(gate))
    for kind in range(2):
        def put(j, rows):
            if kind == 0:
                layer[:, j * q : (j + 1) * q] = (weight * rows.astype(BF).astype(F32)).astype(BF)
            else:
                grad[:, j * q : (j + 1) * q] = rows.astype(BF)
        last = jnp.zeros((n, q), F32)
        for j in range(3):
            lo = (kind * 3 + j) * q
            got = tdot(choose[j], back[:, lo : lo + q])
            put(j, got[:n])
            last = last + got[n:]
        put(3, last)


def compact_matrices(rows):
    r, p = iota((rows // 8 * 6, rows), 0), iota((rows // 8 * 6, rows), 1)
    src, slot = r // 6, r % 6
    tail = src * 8 + 6 + slot % 2
    return onehot(p == src * 8 + slot), [onehot((p == tail) & (slot // 2 == j)) for j in range(3)]


def compact_kernel(own, sib, out):
    main, tails = compact_matrices(own.shape[0])
    q = out.shape[3]
    n = main.shape[0]
    for place, source in enumerate((own, sib)):
        for kind in range(2):
            last = jnp.zeros((n, q), F32)
            for j in range(3):
                lo = (kind * 3 + j) * q
                rows = source[:, lo : lo + q]
                out[j, kind, place * n : (place + 1) * n] = dot(main, rows).astype(BF)
                last = last + dot(tails[j], rows)
            out[3, kind, place * n : (place + 1) * n] = last.astype(BF)


def expand_kernel(own, own_last, sib, sib_last, out):
    rows = out.shape[0]
    n = own.shape[2]
    p, r = iota((rows, n), 0), iota((rows, n), 1)
    base, slot = r // 6 * 8, r % 6
    tail = (p == base + 6 + slot % 2) & (slot // 2 == pl.program_id(1))
    choose = jnp.concatenate([onehot(p == base + slot), onehot(tail)], axis=1)

    def total(a, b):
        return (a[0, 0].astype(F32) + b[0, 0].astype(F32)).astype(BF)

    both = jnp.concatenate([total(own, sib), total(own_last, sib_last)], axis=0)
    out[...] = dot(choose, both).astype(BF)


def gather_copies(pieces, buf, sem, lanes, first):
    half = pieces[3].shape[0]
    views = [
        (buf.at[0, :, lanes], 0),
        (buf.at[1, :, lanes], 1),
        (buf.at[2, :, lanes], 2),
        (buf.at[3, pl.ds(0, half), lanes], 3),
        (buf.at[3, pl.ds(half, half), lanes], 3),
    ]
    return [
        [
            pltpu.make_async_copy(piece, view, sem.at[first + n])
            for n, (piece, (view, at)) in enumerate(zip(pieces, views))
            if at == k
        ]
        for k in range(4)
    ]


SHIFTS = (0, 3, 1, 2)


def forward_kernel(x, rows, *refs):
    gate_parts, up_parts = refs[0:5], refs[5:10]
    hid, slope, silu, to_l, to_r, to_oa, to_ob = refs[10:17]
    w, t, u, acc, sem, tsem, usem, ssem = refs[17:]
    me = x[0]
    n = rows.shape[2] // 2
    spots = [lax.rem(me + s, 4) for s in SHIFTS]
    width = hid.shape[1]
    gate_c = gather_copies(gate_parts, w, sem, pl.ds(0, width), 0)
    up_c = gather_copies(up_parts, w, sem, pl.ds(width, width), 5)
    row_c = [
        pltpu.make_async_copy(rows.at[spots[k], 0], t.at[k], tsem.at[k]) for k in range(4)
    ]
    for k in range(4):
        for c in [row_c[k]] + gate_c[k] + up_c[k]:
            c.start()
    h = n // 2
    fetch = [
        pltpu.make_async_copy(rows.at[spots[k], 1, pl.ds(0, n)], u.at[k - 1], usem.at[k - 1])
        for k in (1, 2, 3)
    ]
    for c in fetch:
        c.start()
    slices = []
    for number, (k, lo, size, target) in enumerate(
        [(1, 0, n, to_l), (2, 0, n, to_r), (3, 0, h, to_oa), (3, h, h, to_ob)]
    ):
        for kind, source in enumerate((t.at[k], u.at[k - 1])):
            slices.append(
                pltpu.make_async_copy(
                    source.at[pl.ds(lo, size)], target.at[kind], ssem.at[number * 2 + kind]
                )
            )
    for k in range(4):
        for c in [row_c[k]] + gate_c[k] + up_c[k]:
            c.wait()
        term = dot(t[k], w[k])
        if k == 0:
            acc[...] = term
        else:
            acc[...] += term
    for c in fetch:
        c.wait()
    for c in slices:
        c.start()
    pre_gate, pre_up = acc[:, :width], acc[:, width:]
    s = jax.nn.sigmoid(pre_gate)
    act = pre_gate * s
    hid[...] = (act * pre_up).astype(BF)
    silu[...] = act
    slope[...] = pre_up * (s * (1.0 + pre_gate * (1.0 - s)))
    for c in slices:
        c.wait()


def backward_kernel(x, hid, slope, silu, rows, *refs):
    gate_parts, up_parts, down_parts = refs[0:5], refs[5:10], refs[10:15]
    own, sib, grads = refs[15:18]
    w, wd, u, o, sem, dsem, usem, osem = refs[18:]
    me = x[0]
    n = rows.shape[2] // 2
    width = hid.shape[1]
    spots = [lax.rem(me + s, 4) for s in SHIFTS]
    gate_c = gather_copies(gate_parts, w, sem, pl.ds(0, width), 0)
    up_c = gather_copies(up_parts, w, sem, pl.ds(width, width), 5)
    q = u.shape[2]
    down_c = gather_copies(down_parts, wd, dsem, pl.ds(0, q), 0)
    row_c = [
        pltpu.make_async_copy(rows.at[spots[k], 1], u.at[k], usem.at[k]) for k in range(4)
    ]
    for k in range(4):
        for c in [row_c[k]] + down_c[k]:
            c.start()
    for k in range(4):
        for c in gate_c[k] + up_c[k]:
            c.start()
    sent = []

    def emit(kind, k, value):
        o[kind, k] = value.astype(BF)
        for number, target in enumerate((own, sib)):
            c = pltpu.make_async_copy(
                o.at[kind, k, pl.ds(number * n, n)],
                target.at[kind, spots[k]],
                osem.at[(kind * 4 + k) * 2 + number],
            )
            c.start()
            sent.append(c)

    back = jnp.zeros(hid.shape, F32)
    for k in range(4):
        for c in [row_c[k]] + down_c[k]:
            c.wait()
        back = back + dot_t(u[k], wd[k])
        emit(0, k, dot(hid[...], wd[k]))
    grads[:, 0:width] = hid[...]
    grads[:, width : 2 * width] = (back * slope[...]).astype(BF)
    grads[:, 2 * width :] = (back * silu[...]).astype(BF)
    for k in range(4):
        for c in gate_c[k] + up_c[k]:
            c.wait()
        emit(1, k, dot_t(grads[:, width:], w[k]))
    for c in sent:
        c.wait()


def weight_kernel(x, rows, *refs):
    mine, theirs = refs[0:4], refs[4:8]
    parts = refs[8:13]
    d_gate, d_up, d_down = refs[13:16]
    t, g, tsem, gsem = refs[16:]
    n = rows.shape[2] // 2
    h = n // 2
    width = d_gate.shape[1]
    copies = [pltpu.make_async_copy(rows.at[x[0]], t.at[:, pl.ds(0, 2 * n)], tsem.at[8])]
    for number, group in enumerate((mine, theirs)):
        base = number * n
        spots = [
            (1, base, n),
            (2, base, n),
            (3, base, h),
            (3, base + h, h),
        ]
        for i, (piece, (k, start, size)) in enumerate(zip(group, spots)):
            copies.append(
                pltpu.make_async_copy(
                    piece, t.at[:, pl.ds(k * 2 * n + start, size)], tsem.at[number * 4 + i]
                )
            )
    spots = [(0, 2 * n), (2 * n, 2 * n), (4 * n, 2 * n), (6 * n, n), (7 * n, n)]
    for i, (piece, (start, size)) in enumerate(zip(parts, spots)):
        copies.append(pltpu.make_async_copy(piece, g.at[pl.ds(start, size)], gsem.at[i]))
    for c in copies:
        c.start()
    for c in copies:
        c.wait()
    both = tdot(t[0], g[:, width:]).astype(BF)
    d_gate[...] = both[:, :width]
    d_up[...] = both[:, width:]
    d_down[...] = tdot(g[:, :width], t[1]).astype(BF)


def vmem():
    return pl.BlockSpec(memory_space=pltpu.VMEM)


def hbm():
    return pl.BlockSpec(memory_space=pl.ANY)


def smem():
    return pl.BlockSpec(memory_space=pltpu.SMEM)


def call(kernel, outs, ins, in_specs, out_specs, scratch=(), grid=(), flops=0, name=None):
    size = flops // 512
    return pl.pallas_call(
        kernel,
        out_shape=outs,
        grid=grid,
        in_specs=in_specs,
        out_specs=out_specs,
        scratch_shapes=list(scratch),
        compiler_params=pltpu.CompilerParams(vmem_limit_bytes=LIMIT),
        cost_estimate=pl.CostEstimate(flops=flops, bytes_accessed=size, transcendentals=0),
        name=name,
    )(*ins)


def shape(*dims, dtype=BF):
    return jax.ShapeDtypeStruct(dims, dtype)


def shift(v, k):
    n = lax.axis_size("dp")
    return lax.ppermute(v, "dp", [(i, (i + k) % n) for i in range(n)])


def sibling(v):
    return lax.ppermute(v, "expert", [(i, i ^ 1) for i in range(lax.axis_size("expert"))])


def near(v):
    return (v, shift(v, 1), shift(v, -1))


def far(parts):
    half = parts[0].shape[0] // 2
    return parts + (shift(parts[1][:half], 1), shift(parts[2][half:], -1))


def ring(v):
    return far(near(v))


def after(values, *earlier):
    return lax.optimization_barrier((values, earlier))[0]


def exchange(v):
    devices = lax.axis_size("expert")
    groups = [[2 * i + c for i in range(devices // 2)] for c in range(2)]
    cut = v.reshape(devices // 2, 8, v.shape[1])
    cut = lax.all_to_all(
        cut, "expert", split_axis=0, concat_axis=0, axis_index_groups=groups, tiled=True
    )
    return cut.reshape(v.shape)


def body(tokens, expert_ids, gate_values, w_gate, w_up, w_down, cotangent):
    experts = lax.axis_size("expert") // 2
    micro, toks, features = tokens.shape
    q = features // 4
    width = w_gate.shape[1]
    wire = experts * 8
    n = experts * 6
    x = lax.axis_index("dp").astype(jnp.int32).reshape(1)
    gate_parts, w_up = lax.optimization_barrier((near(w_gate), w_up))
    gate_parts, up_parts, w_down = lax.optimization_barrier((far(gate_parts), near(w_up), w_down))

    ids = jnp.transpose(expert_ids, (0, 2, 1))
    gates = jnp.transpose(gate_values, (0, 2, 1))
    packed, place = call(
        pack_kernel,
        [shape(wire, 6 * q), shape(1, micro * toks, dtype=jnp.int32)],
        [ids, gates, tokens.reshape(-1, features), cotangent.reshape(-1, features)],
        [vmem()] * 4,
        [vmem()] * 2,
        flops=2 * 6 * wire * wire * q,
        name="pack",
    )
    arrived = exchange(packed)
    arrived, gate_parts, up_parts, down_parts = lax.optimization_barrier(
        (arrived, gate_parts, far(up_parts), near(w_down))
    )
    arrived_sib = sibling(arrived)
    rows = call(
        compact_kernel,
        [shape(4, 2, 2 * n, q)],
        [arrived, arrived_sib],
        [vmem()] * 2,
        [vmem()],
        name="compact",
    )[0]
    rows, down_parts = lax.optimization_barrier((rows, far(down_parts)))
    dma = pltpu.SemaphoreType.DMA
    hid, slope, silu, to_l, to_r, to_oa, to_ob = call(
        forward_kernel,
        [shape(2 * n, width)]
        + [shape(2 * n, width, dtype=F32)] * 2
        + [shape(2, n, q)] * 2
        + [shape(2, n // 2, q)] * 2,
        [x, rows, *gate_parts, *up_parts],
        [smem()] + [hbm()] * 11,
        [vmem()] * 3 + [hbm()] * 4,
        scratch=[
            pltpu.VMEM((4, q, 2 * width), BF),
            pltpu.VMEM((4, 2 * n, q), BF),
            pltpu.VMEM((3, n, q), BF),
            pltpu.VMEM((2 * n, 2 * width), F32),
            dma((10,)),
            dma((4,)),
            dma((3,)),
            dma((8,)),
        ],
        flops=4 * 2 * n * features * width,
        name="forward",
    )
    from_r, from_l = shift(to_l, -1), shift(to_r, 1)
    half_a, half_b = shift(to_oa, 1), shift(to_ob, -1)

    own, sib, grads = call(
        backward_kernel,
        [shape(2, 4, n, q)] * 2 + [shape(2 * n, 3 * width)],
        [x, hid, slope, silu, rows, *gate_parts, *up_parts, *down_parts],
        [smem()] + [vmem()] * 3 + [hbm()] * 16,
        [hbm()] * 2 + [vmem()],
        scratch=[
            pltpu.VMEM((4, q, 2 * width), BF),
            pltpu.VMEM((4, width, q), BF),
            pltpu.VMEM((4, 2 * n, q), BF),
            pltpu.VMEM((2, 4, 2 * n, q), BF),
            dma((10,)),
            dma((5,)),
            dma((4,)),
            dma((16,)),
        ],
        name="backward",
    )
    sib, from_l, from_r = lax.optimization_barrier((sib, from_l, from_r))
    from_sib = sibling(sib)
    sent = call(
        expand_kernel,
        [shape(wire, 6 * q)],
        [own, own, from_sib, from_sib],
        [
            pl.BlockSpec((1, 1, n, q), lambda kind, j: (kind, j, 0, 0)),
            pl.BlockSpec((1, 1, n, q), lambda kind, j: (kind, 3, 0, 0)),
        ]
        * 2,
        [pl.BlockSpec((wire, q), lambda kind, j: (0, kind * 3 + j))],
        grid=(2, 3),
        name="expand",
    )[0]
    sent, half_a, half_b = lax.optimization_barrier((sent, half_a, half_b))
    came = exchange(sent)

    from_oa, from_ob = shift(half_a, 1), shift(half_b, -1)
    grad_parts = ring(grads)
    mine = (from_l, from_r, from_oa, from_ob)
    theirs = tuple(sibling(v) for v in mine)
    d_gate, d_up, d_down = call(
        weight_kernel,
        [shape(q, width)] * 2 + [shape(width, q)],
        [x, rows, *mine, *theirs, *grad_parts],
        [smem()] + [hbm()] * 14,
        [vmem()] * 3,
        scratch=[
            pltpu.VMEM((2, 8 * n, q), BF),
            pltpu.VMEM((8 * n, 3 * width), BF),
            dma((9,)),
            dma((5,)),
        ],
        flops=6 * 8 * n * q * width,
        name="weights",
    )
    layer_out, tokens_grad = call(
        unpack_kernel,
        [shape(micro * toks, features)] * 2,
        [place, gates, came],
        [vmem()] * 3,
        [vmem()] * 2,
        flops=2 * 6 * wire * wire * q,
        name="unpack",
    )
    return (
        layer_out.reshape(tokens.shape),
        tokens_grad.reshape(tokens.shape),
        d_gate,
        d_up,
        d_down,
    )


def solution(mesh):
    rows = P(None, ("dp", "expert"), None)
    return jax.shard_map(
        body,
        mesh=mesh,
        in_specs=(rows, rows, rows, P("dp", "expert"), P("dp", "expert"), P("expert", "dp"), rows),
        out_specs=(rows, rows, P("dp", "expert"), P("dp", "expert"), P("expert", "dp")),
        check_vma=False,
    )
```

```python
import functools

import jax
import jax.numpy as jnp
from jax import lax
from jax.experimental import pallas as pl
from jax.experimental.pallas import tpu as pltpu
from jax.sharding import PartitionSpec as P

BF = jnp.bfloat16
F32 = jnp.float32
LIMIT = 56 * 1024 * 1024


def dot(a, b):
    return jnp.dot(a, b, preferred_element_type=F32)


def dot_t(a, b):
    return lax.dot_general(a, b, (((1,), (1,)), ((), ())), preferred_element_type=F32)


def tdot(a, b):
    return lax.dot_general(a, b, (((0,), (0,)), ((), ())), preferred_element_type=F32)


def onehot(cond):
    return jnp.where(cond, 1.0, 0.0).astype(BF)


def iota(shape, dim):
    return lax.broadcasted_iota(jnp.int32, shape, dim)


def as_column(row):
    n = row.shape[1]
    return jnp.sum(jnp.where(iota((n, n), 0) == iota((n, n), 1), row, 0), axis=1, keepdims=True)


def slot_matrices(place, rows):
    n = place.shape[1]
    at = iota((rows, n), 0)
    base = place // 8 * 8
    slot = place - base
    main = onehot(at == place)
    tail = base + 6 + slot % 2
    return [
        jnp.concatenate([main, onehot((at == tail) & (slot // 2 == j))], axis=1) for j in range(3)
    ]


def as_row(ref):
    return jnp.concatenate([ref[m] for m in range(ref.shape[0])], axis=1)


def as_row(ref):
    return jnp.concatenate([ref[m] for m in range(ref.shape[0])], axis=1)


def places(ids):
    n = ids.shape[1]
    half = n // 2
    earlier, later = iota((n, n), 0), iota((n, n), 1)
    same = (as_column(ids) == ids) & (earlier < later) & (earlier // half == later // half)
    rank = jnp.sum(jnp.where(same, 1, 0), axis=0, keepdims=True)
    return ids * 8 + iota((1, n), 1) // half * 3 + rank


def pack(choose, part, q, out):
    last = part(3)
    for j in range(3):
        both = jnp.concatenate([part(j), last], axis=0)
        out[:, j * q : (j + 1) * q] = dot(choose[j], both).astype(BF)


def pack_tokens(ids, tokens, out):
    q = tokens.shape[1] // 4
    choose = slot_matrices(places(as_row(ids)), out.shape[0])
    pack(choose, lambda j: tokens[:, j * q : (j + 1) * q], q, out)


def pack_upstream(ids, gate, cot, out):
    q = cot.shape[1] // 4
    choose = slot_matrices(places(as_row(ids)), out.shape[0])
    weight = as_column(as_row(gate))
    pack(choose, lambda j: (weight * cot[:, j * q : (j + 1) * q].astype(F32)).astype(BF), q, out)


def unpack(ids, back, put):
    q = back.shape[1] // 3
    choose = slot_matrices(places(as_row(ids)), back.shape[0])
    n = choose[0].shape[1] // 2
    last = jnp.zeros((n, q), F32)
    for j in range(3):
        got = tdot(choose[j], back[:, j * q : (j + 1) * q])
        put(slice(j * q, (j + 1) * q), got[:n].astype(BF))
        last = last + got[n:]
    put(slice(3 * q, 4 * q), last.astype(BF))


def unpack_layer(ids, gate, back, layer):
    weight = as_column(as_row(gate))

    def put(where, rows):
        layer[:, where] = (weight * rows.astype(F32)).astype(BF)

    unpack(ids, back, put)


def unpack_grad(ids, back, grad):
    def put(where, rows):
        grad[:, where] = rows

    unpack(ids, back, put)


def compact(own, sib, out):
    r, p = iota((own.shape[0] // 8 * 6, own.shape[0]), 0), iota((own.shape[0] // 8 * 6, own.shape[0]), 1)
    base, slot = r // 6 * 8, r % 6
    main = onehot(p == base + slot)
    tail = p == base + 6 + slot % 2
    tails = [onehot(tail & (slot // 2 == j)) for j in range(3)]
    q = out.shape[2]
    n = main.shape[0]
    for place, source in enumerate((own, sib)):
        last = jnp.zeros((n, q), F32)
        for j in range(3):
            rows = source[:, j * q : (j + 1) * q]
            out[j, place * n : (place + 1) * n] = dot(main, rows).astype(BF)
            last = last + dot(tails[j], rows)
        out[3, place * n : (place + 1) * n] = last.astype(BF)


def compact_tokens(own, sib, out):
    compact(own, sib, out)


def compact_upstream(x, own, sib, tokens, out, to_l, to_r, to_oa, to_ob, t, tsem, ssem):
    spots = [lax.rem(x[0] + s, 4) for s in SHIFTS]
    n = own.shape[0] // 8 * 6
    h = n // 2
    fetch = [
        pltpu.make_async_copy(tokens.at[spots[k], pl.ds(0, n)], t.at[k - 1], tsem.at[k - 1])
        for k in (1, 2, 3)
    ]
    for c in fetch:
        c.start()
    compact(own, sib, out)
    slices = []
    for number, (k, lo, size, target) in enumerate(
        [(1, 0, n, to_l), (2, 0, n, to_r), (3, 0, h, to_oa), (3, h, h, to_ob)]
    ):
        for kind, source in enumerate((t.at[k - 1], out.at[spots[k]])):
            slices.append(
                pltpu.make_async_copy(
                    source.at[pl.ds(lo, size)], target.at[kind], ssem.at[number * 2 + kind]
                )
            )
    for c in fetch:
        c.wait()
    for c in slices:
        c.start()
    for c in slices:
        c.wait()


def expand_kernel(own, own_last, sib, sib_last, out):
    rows = out.shape[0]
    n = own.shape[1]
    p, r = iota((rows, n), 0), iota((rows, n), 1)
    base, slot = r // 6 * 8, r % 6
    tail = (p == base + 6 + slot % 2) & (slot // 2 == pl.program_id(0))
    choose = jnp.concatenate([onehot(p == base + slot), onehot(tail)], axis=1)

    def total(a, b):
        return (a[0].astype(F32) + b[0].astype(F32)).astype(BF)

    both = jnp.concatenate([total(own, sib), total(own_last, sib_last)], axis=0)
    out[...] = dot(choose, both).astype(BF)


def gather_copies(pieces, buf, sem, lanes, first):
    half = pieces[3].shape[0]
    views = [
        (buf.at[0, :, lanes], 0),
        (buf.at[1, :, lanes], 1),
        (buf.at[2, :, lanes], 2),
        (buf.at[3, pl.ds(0, half), lanes], 3),
        (buf.at[3, pl.ds(half, half), lanes], 3),
    ]
    return [
        [
            pltpu.make_async_copy(piece, view, sem.at[first + n])
            for n, (piece, (view, at)) in enumerate(zip(pieces, views))
            if at == k
        ]
        for k in range(4)
    ]


SHIFTS = (0, 3, 1, 2)


def forward_kernel(x, rows, *refs):
    gate_parts, up_parts = refs[0:5], refs[5:10]
    hid, slope, silu = refs[10:13]
    w, t, acc, sem, tsem = refs[13:]
    width = hid.shape[1]
    gate_c = gather_copies(gate_parts, w, sem, pl.ds(0, width), 0)
    up_c = gather_copies(up_parts, w, sem, pl.ds(width, width), 5)
    row_c = [
        pltpu.make_async_copy(rows.at[lax.rem(x[0] + SHIFTS[k], 4)], t.at[k], tsem.at[k])
        for k in range(4)
    ]
    for k in range(4):
        for c in [row_c[k]] + gate_c[k] + up_c[k]:
            c.start()
    for k in range(4):
        for c in [row_c[k]] + gate_c[k] + up_c[k]:
            c.wait()
        term = dot(t[k], w[k])
        if k == 0:
            acc[...] = term
        else:
            acc[...] += term
    pre_gate, pre_up = acc[:, :width], acc[:, width:]
    s = jax.nn.sigmoid(pre_gate)
    act = pre_gate * s
    hid[...] = (act * pre_up).astype(BF)
    silu[...] = act
    slope[...] = pre_up * (s * (1.0 + pre_gate * (1.0 - s)))


def hand_out(value, k, spot, o, own, sib, sem):
    n = own.shape[1]
    o[k] = value.astype(BF)
    copies = [
        pltpu.make_async_copy(o.at[k, pl.ds(i * n, n)], target.at[spot], sem.at[k * 2 + i])
        for i, target in enumerate((own, sib))
    ]
    for c in copies:
        c.start()
    return copies


def down_kernel(x, hid, slope, silu, rows, *refs):
    down_parts = refs[0:5]
    own, sib, grads = refs[5:8]
    wd, u, o, dsem, usem, osem = refs[8:]
    width = hid.shape[1]
    spots = [lax.rem(x[0] + s, 4) for s in SHIFTS]
    down_c = gather_copies(down_parts, wd, dsem, pl.ds(0, u.shape[2]), 0)
    row_c = [pltpu.make_async_copy(rows.at[spots[k]], u.at[k], usem.at[k]) for k in range(4)]
    for k in range(4):
        for c in [row_c[k]] + down_c[k]:
            c.start()
    sent = []
    back = jnp.zeros(hid.shape, F32)
    for k in range(4):
        for c in [row_c[k]] + down_c[k]:
            c.wait()
        sent += hand_out(dot(hid[...], wd[k]), k, spots[k], o, own, sib, osem)
        back = back + dot_t(u[k], wd[k])
    grads[:, 0:width] = hid[...]
    grads[:, width : 2 * width] = (back * slope[...]).astype(BF)
    grads[:, 2 * width :] = (back * silu[...]).astype(BF)
    for c in sent:
        c.wait()


def input_kernel(x, grads, *refs):
    gate_parts, up_parts = refs[0:5], refs[5:10]
    own, sib = refs[10:12]
    w, o, sem, osem = refs[12:]
    width = w.shape[2] // 2
    gate_c = gather_copies(gate_parts, w, sem, pl.ds(0, width), 0)
    up_c = gather_copies(up_parts, w, sem, pl.ds(width, width), 5)
    for k in range(4):
        for c in gate_c[k] + up_c[k]:
            c.start()
    sent = []
    for k in range(4):
        for c in gate_c[k] + up_c[k]:
            c.wait()
        spot = lax.rem(x[0] + SHIFTS[k], 4)
        sent += hand_out(dot_t(grads[:, width:], w[k]), k, spot, o, own, sib, osem)
    for c in sent:
        c.wait()


def weight_kernel(x, tokens, upstream, *refs):
    mine, theirs = refs[0:4], refs[4:8]
    parts = refs[8:13]
    d_gate, d_up, d_down = refs[13:16]
    t, g, tsem, gsem = refs[16:]
    n = tokens.shape[1] // 2
    h = n // 2
    width = d_gate.shape[1]
    copies = [
        pltpu.make_async_copy(source.at[x[0]], t.at[kind, pl.ds(0, 2 * n)], tsem.at[8 + kind])
        for kind, source in enumerate((tokens, upstream))
    ]
    for number, group in enumerate((mine, theirs)):
        base = number * n
        spots = [
            (1, base, n),
            (2, base, n),
            (3, base, h),
            (3, base + h, h),
        ]
        for i, (piece, (k, start, size)) in enumerate(zip(group, spots)):
            copies.append(
                pltpu.make_async_copy(
                    piece, t.at[:, pl.ds(k * 2 * n + start, size)], tsem.at[number * 4 + i]
                )
            )
    spots = [(0, 2 * n), (2 * n, 2 * n), (4 * n, 2 * n), (6 * n, n), (7 * n, n)]
    for i, (piece, (start, size)) in enumerate(zip(parts, spots)):
        copies.append(pltpu.make_async_copy(piece, g.at[pl.ds(start, size)], gsem.at[i]))
    for c in copies:
        c.start()
    for c in copies:
        c.wait()
    both = tdot(t[0], g[:, width:]).astype(BF)
    d_gate[...] = both[:, :width]
    d_up[...] = both[:, width:]
    d_down[...] = tdot(g[:, :width], t[1]).astype(BF)


def vmem():
    return pl.BlockSpec(memory_space=pltpu.VMEM)


def hbm():
    return pl.BlockSpec(memory_space=pl.ANY)


def smem():
    return pl.BlockSpec(memory_space=pltpu.SMEM)


def call(kernel, outs, ins, in_specs, out_specs, scratch=(), grid=(), flops=0, name=None):
    size = flops // 512
    return pl.pallas_call(
        kernel,
        out_shape=outs,
        grid=grid,
        in_specs=in_specs,
        out_specs=out_specs,
        scratch_shapes=list(scratch),
        compiler_params=pltpu.CompilerParams(vmem_limit_bytes=LIMIT),
        cost_estimate=pl.CostEstimate(flops=flops, bytes_accessed=size, transcendentals=0),
        name=name,
    )(*ins)


def shape(*dims, dtype=BF):
    return jax.ShapeDtypeStruct(dims, dtype)


def shift(v, k):
    n = lax.axis_size("dp")
    return lax.ppermute(v, "dp", [(i, (i + k) % n) for i in range(n)])


def sibling(v):
    return lax.ppermute(v, "expert", [(i, i ^ 1) for i in range(lax.axis_size("expert"))])


def near(v):
    return (v, shift(v, 1), shift(v, -1))


def far(parts):
    half = parts[0].shape[0] // 2
    return parts + (shift(parts[1][:half], 1), shift(parts[2][half:], -1))


def ring(v):
    return far(near(v))


def exchange(v):
    devices = lax.axis_size("expert")
    groups = [[2 * i + c for i in range(devices // 2)] for c in range(2)]
    cut = v.reshape(devices // 2, 8, v.shape[1])
    cut = lax.all_to_all(
        cut, "expert", split_axis=0, concat_axis=0, axis_index_groups=groups, tiled=True
    )
    return cut.reshape(v.shape)


def body(tokens, expert_ids, gate_values, w_gate, w_up, w_down, cotangent):
    experts = lax.axis_size("expert") // 2
    micro, toks, features = tokens.shape
    q = features // 4
    width = w_gate.shape[1]
    wire = experts * 8
    n = experts * 6
    x = lax.axis_index("dp").astype(jnp.int32).reshape(1)
    gate_near, up_near = near(w_gate), near(w_up)
    down_near = near(w_down)

    ids = jnp.transpose(expert_ids, (0, 2, 1))
    gates = jnp.transpose(gate_values, (0, 2, 1))
    wire_shape, rows_shape = shape(wire, 3 * q), shape(4, 2 * n, q)
    token_rows = call(
        pack_tokens, [wire_shape], [ids, tokens.reshape(-1, features)], [vmem()] * 2, [vmem()],
        name="pack_tokens",
    )[0]
    slope_rows = call(
        pack_upstream, [wire_shape], [ids, gates, cotangent.reshape(-1, features)], [vmem()] * 3,
        [vmem()], name="pack_upstream",
    )[0]
    arrived = exchange(token_rows)
    arrived = lax.optimization_barrier((arrived, gate_near, up_near))[0]
    t_rows = call(
        compact_tokens, [rows_shape], [arrived, sibling(arrived)], [vmem()] * 2, [vmem()],
        name="compact_tokens",
    )[0]
    slope_rows, gate_near, up_near = lax.optimization_barrier((slope_rows, gate_near, up_near))
    slopes = exchange(slope_rows)
    gate_parts, up_parts = far(gate_near), far(up_near)
    slopes, gate_parts, up_parts, down_near = lax.optimization_barrier(
        (slopes, gate_parts, up_parts, down_near)
    )
    dma = pltpu.SemaphoreType.DMA
    hid, slope, silu = call(
        forward_kernel,
        [shape(2 * n, width)] + [shape(2 * n, width, dtype=F32)] * 2,
        [x, t_rows, *gate_parts, *up_parts],
        [smem()] + [hbm()] * 11,
        [vmem()] * 3,
        scratch=[
            pltpu.VMEM((4, q, 2 * width), BF),
            pltpu.VMEM((4, 2 * n, q), BF),
            pltpu.VMEM((2 * n, 2 * width), F32),
            dma((10,)),
            dma((4,)),
        ],
        flops=4 * 2 * n * features * width,
        name="forward",
    )
    u_rows, to_l, to_r, to_oa, to_ob = call(
        compact_upstream,
        [rows_shape] + [shape(2, n, q)] * 2 + [shape(2, n // 2, q)] * 2,
        [x, slopes, sibling(slopes), t_rows],
        [smem()] + [vmem()] * 2 + [hbm()],
        [vmem()] + [hbm()] * 4,
        scratch=[pltpu.VMEM((3, n, q), BF), dma((3,)), dma((8,))],
        name="compact_upstream",
    )
    down_parts = far(down_near)
    from_r, from_l = shift(to_l, -1), shift(to_r, 1)
    half_a, half_b = shift(to_oa, 1), shift(to_ob, -1)

    own_out, sib_out, grads = call(
        down_kernel,
        [shape(4, n, q)] * 2 + [shape(2 * n, 3 * width)],
        [x, hid, slope, silu, u_rows, *down_parts],
        [smem()] + [vmem()] * 3 + [hbm()] * 6,
        [hbm()] * 2 + [vmem()],
        scratch=[
            pltpu.VMEM((4, width, q), BF),
            pltpu.VMEM((4, 2 * n, q), BF),
            pltpu.VMEM((4, 2 * n, q), BF),
            dma((5,)),
            dma((4,)),
            dma((8,)),
        ],
        name="down",
    )
    own_grad, sib_grad = call(
        input_kernel,
        [shape(4, n, q)] * 2,
        [x, grads, *gate_parts, *up_parts],
        [smem()] + [vmem()] + [hbm()] * 10,
        [hbm()] * 2,
        scratch=[
            pltpu.VMEM((4, q, 2 * width), BF),
            pltpu.VMEM((4, 2 * n, q), BF),
            dma((10,)),
            dma((8,)),
        ],
        name="inputs",
    )

    def expand(own, sib, name):
        return call(
            expand_kernel,
            [wire_shape],
            [own, own, sib, sib],
            [
                pl.BlockSpec((1, n, q), lambda j: (j, 0, 0)),
                pl.BlockSpec((1, n, q), lambda j: (3, 0, 0)),
            ]
            * 2,
            [pl.BlockSpec((wire, q), lambda j: (0, j))],
            grid=(3,),
            name=name,
        )[0]

    out_wire = expand(own_out, sibling(sib_out), "expand_out")
    out_back = exchange(out_wire)
    sib_grad, from_l, from_r = lax.optimization_barrier((sib_grad, from_l, from_r))
    grad_wire = expand(own_grad, sibling(sib_grad), "expand_grad")
    grad_wire, half_a, half_b = lax.optimization_barrier((grad_wire, half_a, half_b))
    grad_back = exchange(grad_wire)

    from_oa, from_ob = shift(half_a, 1), shift(half_b, -1)
    grad_parts = ring(grads)
    mine = (from_l, from_r, from_oa, from_ob)
    theirs = tuple(sibling(v) for v in mine)
    d_gate, d_up, d_down = call(
        weight_kernel,
        [shape(q, width)] * 2 + [shape(width, q)],
        [x, t_rows, u_rows, *mine, *theirs, *grad_parts],
        [smem()] + [hbm()] * 15,
        [vmem()] * 3,
        scratch=[
            pltpu.VMEM((2, 8 * n, q), BF),
            pltpu.VMEM((8 * n, 3 * width), BF),
            dma((10,)),
            dma((5,)),
        ],
        flops=6 * 8 * n * q * width,
        name="weights",
    )
    flat = shape(micro * toks, features)
    layer_out = call(
        unpack_layer, [flat], [ids, gates, out_back], [vmem()] * 3, [vmem()], name="unpack_layer"
    )[0]
    tokens_grad = call(
        unpack_grad, [flat], [ids, grad_back], [vmem()] * 2, [vmem()], name="unpack_grad"
    )[0]
    return (
        layer_out.reshape(tokens.shape),
        tokens_grad.reshape(tokens.shape),
        d_gate,
        d_up,
        d_down,
    )


def solution(mesh):
    rows = P(None, ("dp", "expert"), None)
    return jax.shard_map(
        body,
        mesh=mesh,
        in_specs=(rows, rows, rows, P("dp", "expert"), P("dp", "expert"), P("expert", "dp"), rows),
        out_specs=(rows, rows, P("dp", "expert"), P("dp", "expert"), P("expert", "dp")),
        check_vma=False,
    )
```

```python
import functools

import jax
import jax.numpy as jnp
from jax import lax
from jax.experimental import pallas as pl
from jax.experimental.pallas import tpu as pltpu
from jax.sharding import PartitionSpec as P

BF = jnp.bfloat16
F32 = jnp.float32
LIMIT = 56 * 1024 * 1024


def dot(a, b):
    return jnp.dot(a, b, preferred_element_type=F32)


def dot_t(a, b):
    return lax.dot_general(a, b, (((1,), (1,)), ((), ())), preferred_element_type=F32)


def tdot(a, b):
    return lax.dot_general(a, b, (((0,), (0,)), ((), ())), preferred_element_type=F32)


def onehot(cond):
    return jnp.where(cond, 1.0, 0.0).astype(BF)


def iota(shape, dim):
    return lax.broadcasted_iota(jnp.int32, shape, dim)


def as_column(row):
    n = row.shape[1]
    return jnp.sum(jnp.where(iota((n, n), 0) == iota((n, n), 1), row, 0), axis=1, keepdims=True)


def slot_matrices(place, rows):
    n = place.shape[1]
    at = iota((rows, n), 0)
    base = place // 8 * 8
    slot = place - base
    main = onehot(at == place)
    tail = base + 6 + slot % 2
    return [
        jnp.concatenate([main, onehot((at == tail) & (slot // 2 == j))], axis=1) for j in range(3)
    ]


def as_row(ref):
    return jnp.concatenate([ref[m] for m in range(ref.shape[0])], axis=1)


def pack_kernel(ids_ref, gate_ref, tokens, cot, out, place_out):
    ids, gate = as_row(ids_ref), as_row(gate_ref)
    n = ids.shape[1]
    half = n // 2
    q = tokens.shape[1] // 4
    earlier, later = iota((n, n), 0), iota((n, n), 1)
    same = (as_column(ids) == ids) & (earlier < later) & (earlier // half == later // half)
    rank = jnp.sum(jnp.where(same, 1, 0), axis=0, keepdims=True)
    place = ids * 8 + iota((1, n), 1) // half * 3 + rank
    place_out[...] = place
    choose = slot_matrices(place, out.shape[0])
    weight = as_column(gate)
    for kind in range(2):
        def part(j):
            rows = (tokens if kind == 0 else cot)[:, j * q : (j + 1) * q]
            return rows if kind == 0 else (weight * rows.astype(F32)).astype(BF)
        last = part(3)
        for j in range(3):
            both = jnp.concatenate([part(j), last], axis=0)
            lo = (kind * 3 + j) * q
            out[:, lo : lo + q] = dot(choose[j], both).astype(BF)


def unpack_kernel(place, gate, back, layer, grad):
    n = place.shape[1]
    q = layer.shape[1] // 4
    choose = slot_matrices(place[...], back.shape[0])
    weight = as_column(as_row(gate))
    for kind in range(2):
        def put(j, rows):
            if kind == 0:
                layer[:, j * q : (j + 1) * q] = (weight * rows.astype(BF).astype(F32)).astype(BF)
            else:
                grad[:, j * q : (j + 1) * q] = rows.astype(BF)
        last = jnp.zeros((n, q), F32)
        for j in range(3):
            lo = (kind * 3 + j) * q
            got = tdot(choose[j], back[:, lo : lo + q])
            put(j, got[:n])
            last = last + got[n:]
        put(3, last)


def compact_matrices(rows):
    r, p = iota((rows // 8 * 6, rows), 0), iota((rows // 8 * 6, rows), 1)
    src, slot = r // 6, r % 6
    tail = src * 8 + 6 + slot % 2
    return onehot(p == src * 8 + slot), [onehot((p == tail) & (slot // 2 == j)) for j in range(3)]


def compact_kernel(own, sib, out):
    main, tails = compact_matrices(own.shape[0])
    q = out.shape[3]
    n = main.shape[0]
    for place, source in enumerate((own, sib)):
        for kind in range(2):
            last = jnp.zeros((n, q), F32)
            for j in range(3):
                lo = (kind * 3 + j) * q
                rows = source[:, lo : lo + q]
                out[j, kind, place * n : (place + 1) * n] = dot(main, rows).astype(BF)
                last = last + dot(tails[j], rows)
            out[3, kind, place * n : (place + 1) * n] = last.astype(BF)


def expand_kernel(own, own_last, sib, sib_last, out):
    rows = out.shape[0]
    n = own.shape[1]
    p, r = iota((rows, n), 0), iota((rows, n), 1)
    base, slot = r // 6 * 8, r % 6
    tail = (p == base + 6 + slot % 2) & (slot // 2 == pl.program_id(0))
    choose = jnp.concatenate([onehot(p == base + slot), onehot(tail)], axis=1)

    def total(a, b):
        return (a[0].astype(F32) + b[0].astype(F32)).astype(BF)

    both = jnp.concatenate([total(own, sib), total(own_last, sib_last)], axis=0)
    out[...] = dot(choose, both).astype(BF)


def gather_copies(pieces, buf, sem, lanes, first):
    half = pieces[3].shape[0]
    views = [
        (buf.at[0, :, lanes], 0),
        (buf.at[1, :, lanes], 1),
        (buf.at[2, :, lanes], 2),
        (buf.at[3, pl.ds(0, half), lanes], 3),
        (buf.at[3, pl.ds(half, half), lanes], 3),
    ]
    return [
        [
            pltpu.make_async_copy(piece, view, sem.at[first + n])
            for n, (piece, (view, at)) in enumerate(zip(pieces, views))
            if at == k
        ]
        for k in range(4)
    ]


SHIFTS = (0, 3, 1, 2)


def forward_kernel(x, rows, *refs):
    gate_parts, up_parts = refs[0:5], refs[5:10]
    hid, slope, silu, to_l, to_r, to_oa, to_ob = refs[10:17]
    w, t, u, acc, sem, tsem, usem, ssem = refs[17:]
    me = x[0]
    n = rows.shape[2] // 2
    spots = [lax.rem(me + s, 4) for s in SHIFTS]
    width = hid.shape[1]
    gate_c = gather_copies(gate_parts, w, sem, pl.ds(0, width), 0)
    up_c = gather_copies(up_parts, w, sem, pl.ds(width, width), 5)
    row_c = [
        pltpu.make_async_copy(rows.at[spots[k], 0], t.at[k], tsem.at[k]) for k in range(4)
    ]
    for k in range(4):
        for c in [row_c[k]] + gate_c[k] + up_c[k]:
            c.start()
    h = n // 2
    fetch = [
        pltpu.make_async_copy(rows.at[spots[k], 1, pl.ds(0, n)], u.at[k - 1], usem.at[k - 1])
        for k in (1, 2, 3)
    ]
    for c in fetch:
        c.start()
    slices = []
    for number, (k, lo, size, target) in enumerate(
        [(1, 0, n, to_l), (2, 0, n, to_r), (3, 0, h, to_oa), (3, h, h, to_ob)]
    ):
        for kind, source in enumerate((t.at[k], u.at[k - 1])):
            slices.append(
                pltpu.make_async_copy(
                    source.at[pl.ds(lo, size)], target.at[kind], ssem.at[number * 2 + kind]
                )
            )
    for k in range(4):
        for c in [row_c[k]] + gate_c[k] + up_c[k]:
            c.wait()
        term = dot(t[k], w[k])
        if k == 0:
            acc[...] = term
        else:
            acc[...] += term
    for c in fetch:
        c.wait()
    for c in slices:
        c.start()
    pre_gate, pre_up = acc[:, :width], acc[:, width:]
    s = jax.nn.sigmoid(pre_gate)
    act = pre_gate * s
    hid[...] = (act * pre_up).astype(BF)
    silu[...] = act
    slope[...] = pre_up * (s * (1.0 + pre_gate * (1.0 - s)))
    for c in slices:
        c.wait()


def hand_out(value, k, spot, o, own, sib, sem):
    n = own.shape[1]
    o[k] = value.astype(BF)
    copies = [
        pltpu.make_async_copy(o.at[k, pl.ds(i * n, n)], target.at[spot], sem.at[k * 2 + i])
        for i, target in enumerate((own, sib))
    ]
    for c in copies:
        c.start()
    return copies


def down_kernel(x, hid, slope, silu, rows, *refs):
    down_parts = refs[0:5]
    own, sib, grads = refs[5:8]
    wd, u, o, dsem, usem, osem = refs[8:]
    width = hid.shape[1]
    spots = [lax.rem(x[0] + s, 4) for s in SHIFTS]
    down_c = gather_copies(down_parts, wd, dsem, pl.ds(0, u.shape[2]), 0)
    row_c = [pltpu.make_async_copy(rows.at[spots[k], 1], u.at[k], usem.at[k]) for k in range(4)]
    for k in range(4):
        for c in [row_c[k]] + down_c[k]:
            c.start()
    sent = []
    back = jnp.zeros(hid.shape, F32)
    for k in range(4):
        for c in [row_c[k]] + down_c[k]:
            c.wait()
        sent += hand_out(dot(hid[...], wd[k]), k, spots[k], o, own, sib, osem)
        back = back + dot_t(u[k], wd[k])
    grads[:, 0:width] = hid[...]
    grads[:, width : 2 * width] = (back * slope[...]).astype(BF)
    grads[:, 2 * width :] = (back * silu[...]).astype(BF)
    for c in sent:
        c.wait()


def input_kernel(x, grads, *refs):
    gate_parts, up_parts = refs[0:5], refs[5:10]
    own, sib = refs[10:12]
    w, o, sem, osem = refs[12:]
    width = w.shape[2] // 2
    gate_c = gather_copies(gate_parts, w, sem, pl.ds(0, width), 0)
    up_c = gather_copies(up_parts, w, sem, pl.ds(width, width), 5)
    for k in range(4):
        for c in gate_c[k] + up_c[k]:
            c.start()
    sent = []
    for k in range(4):
        for c in gate_c[k] + up_c[k]:
            c.wait()
        spot = lax.rem(x[0] + SHIFTS[k], 4)
        sent += hand_out(dot_t(grads[:, width:], w[k]), k, spot, o, own, sib, osem)
    for c in sent:
        c.wait()


def weight_kernel(x, rows, *refs):
    mine, theirs = refs[0:4], refs[4:8]
    parts = refs[8:13]
    d_gate, d_up, d_down = refs[13:16]
    t, g, tsem, gsem = refs[16:]
    n = rows.shape[2] // 2
    h = n // 2
    width = d_gate.shape[1]
    copies = [pltpu.make_async_copy(rows.at[x[0]], t.at[:, pl.ds(0, 2 * n)], tsem.at[8])]
    for number, group in enumerate((mine, theirs)):
        base = number * n
        spots = [
            (1, base, n),
            (2, base, n),
            (3, base, h),
            (3, base + h, h),
        ]
        for i, (piece, (k, start, size)) in enumerate(zip(group, spots)):
            copies.append(
                pltpu.make_async_copy(
                    piece, t.at[:, pl.ds(k * 2 * n + start, size)], tsem.at[number * 4 + i]
                )
            )
    spots = [(0, 2 * n), (2 * n, 2 * n), (4 * n, 2 * n), (6 * n, n), (7 * n, n)]
    for i, (piece, (start, size)) in enumerate(zip(parts, spots)):
        copies.append(pltpu.make_async_copy(piece, g.at[pl.ds(start, size)], gsem.at[i]))
    for c in copies:
        c.start()
    for c in copies:
        c.wait()
    both = tdot(t[0], g[:, width:]).astype(BF)
    d_gate[...] = both[:, :width]
    d_up[...] = both[:, width:]
    d_down[...] = tdot(g[:, :width], t[1]).astype(BF)


def vmem():
    return pl.BlockSpec(memory_space=pltpu.VMEM)


def hbm():
    return pl.BlockSpec(memory_space=pl.ANY)


def smem():
    return pl.BlockSpec(memory_space=pltpu.SMEM)


def call(kernel, outs, ins, in_specs, out_specs, scratch=(), grid=(), aliases=None, flops=0, name=None):
    size = flops // 512
    return pl.pallas_call(
        kernel,
        out_shape=outs,
        grid=grid,
        input_output_aliases=aliases or {},
        in_specs=in_specs,
        out_specs=out_specs,
        scratch_shapes=list(scratch),
        compiler_params=pltpu.CompilerParams(vmem_limit_bytes=LIMIT),
        cost_estimate=pl.CostEstimate(flops=flops, bytes_accessed=size, transcendentals=0),
        name=name,
    )(*ins)


def shape(*dims, dtype=BF):
    return jax.ShapeDtypeStruct(dims, dtype)


def shift(v, k):
    n = lax.axis_size("dp")
    return lax.ppermute(v, "dp", [(i, (i + k) % n) for i in range(n)])


def sibling(v):
    return lax.ppermute(v, "expert", [(i, i ^ 1) for i in range(lax.axis_size("expert"))])


def near(v):
    return (v, shift(v, 1), shift(v, -1))


def far(parts):
    half = parts[0].shape[0] // 2
    return parts + (shift(parts[1][:half], 1), shift(parts[2][half:], -1))


def ring(v):
    return far(near(v))


def after(values, *earlier):
    return lax.optimization_barrier((values, earlier))[0]


def exchange(v):
    devices = lax.axis_size("expert")
    groups = [[2 * i + c for i in range(devices // 2)] for c in range(2)]
    cut = v.reshape(devices // 2, 8, v.shape[1])
    cut = lax.all_to_all(
        cut, "expert", split_axis=0, concat_axis=0, axis_index_groups=groups, tiled=True
    )
    return cut.reshape(v.shape)


def body(tokens, expert_ids, gate_values, w_gate, w_up, w_down, cotangent):
    experts = lax.axis_size("expert") // 2
    micro, toks, features = tokens.shape
    q = features // 4
    width = w_gate.shape[1]
    wire = experts * 8
    n = experts * 6
    x = lax.axis_index("dp").astype(jnp.int32).reshape(1)
    gate_near, up_near, down_near = near(w_gate), near(w_up), near(w_down)

    ids = jnp.transpose(expert_ids, (0, 2, 1))
    gates = jnp.transpose(gate_values, (0, 2, 1))
    packed, place = call(
        pack_kernel,
        [shape(wire, 6 * q), shape(1, micro * toks, dtype=jnp.int32)],
        [ids, gates, tokens.reshape(-1, features), cotangent.reshape(-1, features)],
        [vmem()] * 4,
        [vmem()] * 2,
        flops=2 * 6 * wire * wire * q,
        name="pack",
    )
    arrived = exchange(packed)
    arrived, gate_parts, up_near, down_near = lax.optimization_barrier(
        (arrived, far(gate_near), up_near, down_near)
    )
    up_parts, down_parts = far(up_near), far(down_near)
    arrived_sib = sibling(arrived)
    rows = call(
        compact_kernel,
        [shape(4, 2, 2 * n, q)],
        [arrived, arrived_sib],
        [vmem()] * 2,
        [vmem()],
        name="compact",
    )[0]
    dma = pltpu.SemaphoreType.DMA
    hid, slope, silu, to_l, to_r, to_oa, to_ob = call(
        forward_kernel,
        [shape(2 * n, width)]
        + [shape(2 * n, width, dtype=F32)] * 2
        + [shape(2, n, q)] * 2
        + [shape(2, n // 2, q)] * 2,
        [x, rows, *gate_parts, *up_parts],
        [smem()] + [hbm()] * 11,
        [vmem()] * 3 + [hbm()] * 4,
        scratch=[
            pltpu.VMEM((4, q, 2 * width), BF),
            pltpu.VMEM((4, 2 * n, q), BF),
            pltpu.VMEM((3, n, q), BF),
            pltpu.VMEM((2 * n, 2 * width), F32),
            dma((10,)),
            dma((4,)),
            dma((3,)),
            dma((8,)),
        ],
        flops=32 * 2 * n * features * width,
        name="forward",
    )
    to_l, to_r, to_oa, to_ob, down_parts = lax.optimization_barrier(
        (to_l, to_r, to_oa, to_ob, down_parts)
    )
    from_r, from_l = shift(to_l, -1), shift(to_r, 1)
    half_a, half_b = shift(to_oa, 1), shift(to_ob, -1)

    own_out, sib_out, grads = call(
        down_kernel,
        [shape(4, n, q)] * 2 + [shape(2 * n, 3 * width)],
        [x, hid, slope, silu, rows, *down_parts],
        [smem()] + [vmem()] * 3 + [hbm()] * 6,
        [hbm()] * 2 + [vmem()],
        scratch=[
            pltpu.VMEM((4, width, q), BF),
            pltpu.VMEM((4, 2 * n, q), BF),
            pltpu.VMEM((4, 2 * n, q), BF),
            dma((5,)),
            dma((4,)),
            dma((8,)),
        ],
        name="down",
    )
    own_grad, sib_grad = call(
        input_kernel,
        [shape(4, n, q)] * 2,
        [x, grads, *gate_parts, *up_parts],
        [smem()] + [vmem()] + [hbm()] * 10,
        [hbm()] * 2,
        scratch=[
            pltpu.VMEM((4, q, 2 * width), BF),
            pltpu.VMEM((4, 2 * n, q), BF),
            dma((10,)),
            dma((8,)),
        ],
        name="inputs",
    )
    parts = [
        pl.BlockSpec((1, n, q), lambda j: (j, 0, 0)),
        pl.BlockSpec((1, n, q), lambda j: (3, 0, 0)),
    ] * 2
    out_sib = sibling(sib_out)
    sib_grad, from_l, from_r = lax.optimization_barrier((sib_grad, from_l, from_r))
    grad_sib = sibling(sib_grad)
    sent = call(
        expand_kernel,
        [shape(wire, 6 * q)],
        [own_out, own_out, out_sib, out_sib],
        parts,
        [pl.BlockSpec((wire, q), lambda j: (0, j))],
        grid=(3,),
        name="expand_out",
    )[0]
    sent = call(
        lambda _, *refs: expand_kernel(*refs),
        [shape(wire, 6 * q)],
        [sent, own_grad, own_grad, grad_sib, grad_sib],
        [hbm()] + parts,
        [pl.BlockSpec((wire, q), lambda j: (0, 3 + j))],
        grid=(3,),
        aliases={0: 0},
        name="expand_grad",
    )[0]
    sent, half_a, half_b = lax.optimization_barrier((sent, half_a, half_b))
    came = exchange(sent)

    from_oa, from_ob = shift(half_a, 1), shift(half_b, -1)
    grad_parts = ring(grads)
    mine = (from_l, from_r, from_oa, from_ob)
    theirs = tuple(sibling(v) for v in mine)
    d_gate, d_up, d_down = call(
        weight_kernel,
        [shape(q, width)] * 2 + [shape(width, q)],
        [x, rows, *mine, *theirs, *grad_parts],
        [smem()] + [hbm()] * 14,
        [vmem()] * 3,
        scratch=[
            pltpu.VMEM((2, 8 * n, q), BF),
            pltpu.VMEM((8 * n, 3 * width), BF),
            dma((9,)),
            dma((5,)),
        ],
        flops=6 * 8 * n * q * width,
        name="weights",
    )
    layer_out, tokens_grad = call(
        unpack_kernel,
        [shape(micro * toks, features)] * 2,
        [place, gates, came],
        [vmem()] * 3,
        [vmem()] * 2,
        flops=2 * 6 * wire * wire * q,
        name="unpack",
    )
    return (
        layer_out.reshape(tokens.shape),
        tokens_grad.reshape(tokens.shape),
        d_gate,
        d_up,
        d_down,
    )


def solution(mesh):
    rows = P(None, ("dp", "expert"), None)
    return jax.shard_map(
        body,
        mesh=mesh,
        in_specs=(rows, rows, rows, P("dp", "expert"), P("dp", "expert"), P("expert", "dp"), rows),
        out_specs=(rows, rows, P("dp", "expert"), P("dp", "expert"), P("expert", "dp")),
        check_vma=False,
    )
```

```python
import functools

import jax
import jax.numpy as jnp
from jax import lax
from jax.experimental import pallas as pl
from jax.experimental.pallas import tpu as pltpu
from jax.sharding import PartitionSpec as P

BF = jnp.bfloat16
F32 = jnp.float32
LIMIT = 56 * 1024 * 1024


def dot(a, b):
    return jnp.dot(a, b, preferred_element_type=F32)


def dot_t(a, b):
    return lax.dot_general(a, b, (((1,), (1,)), ((), ())), preferred_element_type=F32)


def tdot(a, b):
    return lax.dot_general(a, b, (((0,), (0,)), ((), ())), preferred_element_type=F32)


def onehot(cond):
    return jnp.where(cond, 1.0, 0.0).astype(BF)


def iota(shape, dim):
    return lax.broadcasted_iota(jnp.int32, shape, dim)


def as_column(row):
    n = row.shape[1]
    return jnp.sum(jnp.where(iota((n, n), 0) == iota((n, n), 1), row, 0), axis=1, keepdims=True)


def slot_matrices(place, rows):
    n = place.shape[1]
    at = iota((rows, n), 0)
    base = place // 8 * 8
    slot = place - base
    main = onehot(at == place)
    tail = base + 6 + slot % 2
    return [
        jnp.concatenate([main, onehot((at == tail) & (slot // 2 == j))], axis=1) for j in range(3)
    ]


def as_row(ref):
    return jnp.concatenate([ref[m] for m in range(ref.shape[0])], axis=1)


def pack_kernel(ids_ref, gate_ref, tokens, cot, out, place_out):
    ids, gate = as_row(ids_ref), as_row(gate_ref)
    n = ids.shape[1]
    half = n // 2
    q = tokens.shape[1] // 4
    earlier, later = iota((n, n), 0), iota((n, n), 1)
    same = (as_column(ids) == ids) & (earlier < later) & (earlier // half == later // half)
    rank = jnp.sum(jnp.where(same, 1, 0), axis=0, keepdims=True)
    place = ids * 8 + iota((1, n), 1) // half * 3 + rank
    place_out[...] = place
    choose = slot_matrices(place, out.shape[0])
    weight = as_column(gate)
    for kind in range(2):
        def part(j):
            rows = (tokens if kind == 0 else cot)[:, j * q : (j + 1) * q]
            return rows if kind == 0 else (weight * rows.astype(F32)).astype(BF)
        last = part(3)
        for j in range(3):
            both = jnp.concatenate([part(j), last], axis=0)
            lo = (kind * 3 + j) * q
            out[:, lo : lo + q] = dot(choose[j], both).astype(BF)


def unpack_kernel(place, gate, back, layer, grad):
    n = place.shape[1]
    q = layer.shape[1] // 4
    choose = slot_matrices(place[...], back.shape[0])
    weight = as_column(as_row(gate))
    for kind in range(2):
        def put(j, rows):
            if kind == 0:
                layer[:, j * q : (j + 1) * q] = (weight * rows.astype(BF).astype(F32)).astype(BF)
            else:
                grad[:, j * q : (j + 1) * q] = rows.astype(BF)
        last = jnp.zeros((n, q), F32)
        for j in range(3):
            lo = (kind * 3 + j) * q
            got = tdot(choose[j], back[:, lo : lo + q])
            put(j, got[:n])
            last = last + got[n:]
        put(3, last)


def wire_places(shape_, dim):
    r = iota(shape_, dim)
    base, slot = r // 6 * 8, r % 6
    return base + slot, base + 6 + slot % 2, slot // 2


def compact_kernel(own, sib, out):
    n = out.shape[2] // 2
    q = out.shape[3]
    p = iota((n, own.shape[0]), 1)
    row, tail, part = wire_places((n, 1), 0)
    main = onehot(p == row)
    choose = [
        jnp.concatenate([main, onehot(p == jnp.where(part == j, tail, -1))], axis=0)
        for j in range(3)
    ]
    for place, source in enumerate((own, sib)):
        last = jnp.zeros((n, q), F32)
        for j in range(3):
            got = dot(choose[j], source[:, j * q : (j + 1) * q])
            out[j, 0, place * n : (place + 1) * n] = got[:n].astype(BF)
            last = last + got[n:]
        out[3, 0, place * n : (place + 1) * n] = last.astype(BF)


def expand_kernel(own, own_last, sib, sib_last, out):
    n = own.shape[1]
    p = iota((out.shape[0], n), 0)
    row, tail, part = wire_places((1, n), 1)
    tail = jnp.where(part == pl.program_id(0), tail, -1)
    choose = jnp.concatenate([onehot(p == row), onehot(p == tail)], axis=1)

    def total(a, b):
        return (a[0].astype(F32) + b[0].astype(F32)).astype(BF)

    both = jnp.concatenate([total(own, sib), total(own_last, sib_last)], axis=0)
    out[...] = dot(choose, both).astype(BF)


def gather_copies(pieces, buf, sem, lanes, first):
    half = pieces[3].shape[0]
    views = [
        (buf.at[0, :, lanes], 0),
        (buf.at[1, :, lanes], 1),
        (buf.at[2, :, lanes], 2),
        (buf.at[3, pl.ds(0, half), lanes], 3),
        (buf.at[3, pl.ds(half, half), lanes], 3),
    ]
    return [
        [
            pltpu.make_async_copy(piece, view, sem.at[first + n])
            for n, (piece, (view, at)) in enumerate(zip(pieces, views))
            if at == k
        ]
        for k in range(4)
    ]


SHIFTS = (0, 3, 1, 2)


def forward_kernel(x, rows, *refs):
    gate_parts, up_parts = refs[0:5], refs[5:10]
    hid, slope, silu, to_l, to_r, to_oa, to_ob = refs[10:17]
    w, t, u, acc, sem, tsem, usem, ssem = refs[17:]
    me = x[0]
    n = rows.shape[2] // 2
    spots = [lax.rem(me + s, 4) for s in SHIFTS]
    width = hid.shape[1]
    gate_c = gather_copies(gate_parts, w, sem, pl.ds(0, width), 0)
    up_c = gather_copies(up_parts, w, sem, pl.ds(width, width), 5)
    row_c = [
        pltpu.make_async_copy(rows.at[spots[k], 0], t.at[k], tsem.at[k]) for k in range(4)
    ]
    for k in range(4):
        for c in [row_c[k]] + gate_c[k] + up_c[k]:
            c.start()
    h = n // 2
    fetch = [
        pltpu.make_async_copy(rows.at[spots[k], 1, pl.ds(0, n)], u.at[k - 1], usem.at[k - 1])
        for k in (1, 2, 3)
    ]
    for c in fetch:
        c.start()
    slices = []
    for number, (k, lo, size, target) in enumerate(
        [(1, 0, n, to_l), (2, 0, n, to_r), (3, 0, h, to_oa), (3, h, h, to_ob)]
    ):
        for kind, source in enumerate((t.at[k], u.at[k - 1])):
            slices.append(
                pltpu.make_async_copy(
                    source.at[pl.ds(lo, size)], target.at[kind], ssem.at[number * 2 + kind]
                )
            )
    for k in range(4):
        for c in [row_c[k]] + gate_c[k] + up_c[k]:
            c.wait()
        term = dot(t[k], w[k])
        if k == 0:
            acc[...] = term
        else:
            acc[...] += term
    for c in fetch:
        c.wait()
    for c in slices:
        c.start()
    pre_gate, pre_up = acc[:, :width], acc[:, width:]
    s = jax.nn.sigmoid(pre_gate)
    act = pre_gate * s
    hid[...] = (act * pre_up).astype(BF)
    silu[...] = act
    slope[...] = pre_up * (s * (1.0 + pre_gate * (1.0 - s)))
    for c in slices:
        c.wait()


def hand_out(value, k, spot, o, own, sib, sem):
    n = own.shape[1]
    o[k] = value.astype(BF)
    copies = [
        pltpu.make_async_copy(o.at[k, pl.ds(i * n, n)], target.at[spot], sem.at[k * 2 + i])
        for i, target in enumerate((own, sib))
    ]
    for c in copies:
        c.start()
    return copies


def down_kernel(x, hid, slope, silu, rows, *refs):
    down_parts = refs[0:5]
    own, sib, grads = refs[5:8]
    wd, u, o, dsem, usem, osem = refs[8:]
    width = hid.shape[1]
    spots = [lax.rem(x[0] + s, 4) for s in SHIFTS]
    down_c = gather_copies(down_parts, wd, dsem, pl.ds(0, u.shape[2]), 0)
    row_c = [pltpu.make_async_copy(rows.at[spots[k], 1], u.at[k], usem.at[k]) for k in range(4)]
    for k in range(4):
        for c in [row_c[k]] + down_c[k]:
            c.start()
    sent = []
    back = jnp.zeros(hid.shape, F32)
    for k in range(4):
        for c in [row_c[k]] + down_c[k]:
            c.wait()
        sent += hand_out(dot(hid[...], wd[k]), k, spots[k], o, own, sib, osem)
        back = back + dot_t(u[k], wd[k])
    grads[:, 0:width] = hid[...]
    grads[:, width : 2 * width] = (back * slope[...]).astype(BF)
    grads[:, 2 * width :] = (back * silu[...]).astype(BF)
    for c in sent:
        c.wait()


def input_kernel(x, grads, *refs):
    gate_parts, up_parts = refs[0:5], refs[5:10]
    own, sib = refs[10:12]
    w, o, sem, osem = refs[12:]
    width = w.shape[2] // 2
    gate_c = gather_copies(gate_parts, w, sem, pl.ds(0, width), 0)
    up_c = gather_copies(up_parts, w, sem, pl.ds(width, width), 5)
    for k in range(4):
        for c in gate_c[k] + up_c[k]:
            c.start()
    sent = []
    for k in range(4):
        for c in gate_c[k] + up_c[k]:
            c.wait()
        spot = lax.rem(x[0] + SHIFTS[k], 4)
        sent += hand_out(dot_t(grads[:, width:], w[k]), k, spot, o, own, sib, osem)
    for c in sent:
        c.wait()


def weight_kernel(x, rows, *refs):
    mine, theirs = refs[0:4], refs[4:8]
    parts = refs[8:13]
    d_gate, d_up, d_down = refs[13:16]
    t, g, tsem, gsem = refs[16:]
    n = rows.shape[2] // 2
    h = n // 2
    width = d_gate.shape[1]
    copies = [pltpu.make_async_copy(rows.at[x[0]], t.at[:, pl.ds(0, 2 * n)], tsem.at[8])]
    for number, group in enumerate((mine, theirs)):
        base = number * n
        spots = [
            (1, base, n),
            (2, base, n),
            (3, base, h),
            (3, base + h, h),
        ]
        for i, (piece, (k, start, size)) in enumerate(zip(group, spots)):
            copies.append(
                pltpu.make_async_copy(
                    piece, t.at[:, pl.ds(k * 2 * n + start, size)], tsem.at[number * 4 + i]
                )
            )
    spots = [(0, 2 * n), (2 * n, 2 * n), (4 * n, 2 * n), (6 * n, n), (7 * n, n)]
    for i, (piece, (start, size)) in enumerate(zip(parts, spots)):
        copies.append(pltpu.make_async_copy(piece, g.at[pl.ds(start, size)], gsem.at[i]))
    for c in copies:
        c.start()
    for c in copies:
        c.wait()
    both = tdot(t[0], g[:, width:]).astype(BF)
    d_gate[...] = both[:, :width]
    d_up[...] = both[:, width:]
    d_down[...] = tdot(g[:, :width], t[1]).astype(BF)


def vmem():
    return pl.BlockSpec(memory_space=pltpu.VMEM)


def hbm():
    return pl.BlockSpec(memory_space=pl.ANY)


def smem():
    return pl.BlockSpec(memory_space=pltpu.SMEM)


def call(kernel, outs, ins, in_specs, out_specs, scratch=(), grid=(), aliases=None, flops=0, name=None):
    size = flops // 512
    return pl.pallas_call(
        kernel,
        out_shape=outs,
        grid=grid,
        input_output_aliases=aliases or {},
        in_specs=in_specs,
        out_specs=out_specs,
        scratch_shapes=list(scratch),
        compiler_params=pltpu.CompilerParams(vmem_limit_bytes=LIMIT),
        cost_estimate=pl.CostEstimate(flops=flops, bytes_accessed=size, transcendentals=0),
        name=name,
    )(*ins)


def shape(*dims, dtype=BF):
    return jax.ShapeDtypeStruct(dims, dtype)


def shift(v, k):
    n = lax.axis_size("dp")
    return lax.ppermute(v, "dp", [(i, (i + k) % n) for i in range(n)])


def sibling(v):
    return lax.ppermute(v, "expert", [(i, i ^ 1) for i in range(lax.axis_size("expert"))])


def near(v):
    return (v, shift(v, 1), shift(v, -1))


def halves(parts):
    half = parts[0].shape[0] // 2
    return parts + (parts[1][:half], parts[2][half:])


def far(parts):
    return parts[:3] + (shift(parts[3], 1), shift(parts[4], -1))


def ring(v):
    return far(halves(near(v)))


def exchange(v):
    devices = lax.axis_size("expert")
    groups = [[2 * i + c for i in range(devices // 2)] for c in range(2)]
    cut = v.reshape(devices // 2, 8, v.shape[1])
    cut = lax.all_to_all(
        cut, "expert", split_axis=0, concat_axis=0, axis_index_groups=groups, tiled=True
    )
    return cut.reshape(v.shape)


def body(tokens, expert_ids, gate_values, w_gate, w_up, w_down, cotangent):
    experts = lax.axis_size("expert") // 2
    micro, toks, features = tokens.shape
    q = features // 4
    width = w_gate.shape[1]
    wire = experts * 8
    n = experts * 6
    x = lax.axis_index("dp").astype(jnp.int32).reshape(1)
    gate_near, up_near, down_near = near(w_gate), near(w_up), near(w_down)

    ids = jnp.transpose(expert_ids, (0, 2, 1))
    gates = jnp.transpose(gate_values, (0, 2, 1))
    packed, place = call(
        pack_kernel,
        [shape(wire, 6 * q), shape(1, micro * toks, dtype=jnp.int32)],
        [ids, gates, tokens.reshape(-1, features), cotangent.reshape(-1, features)],
        [vmem()] * 4,
        [vmem()] * 2,
        flops=2 * 6 * wire * wire * q,
        name="pack",
    )
    arrived = exchange(packed)
    arrived, gate_parts, up_near, down_near = lax.optimization_barrier(
        (arrived, far(halves(gate_near)), halves(up_near), halves(down_near))
    )
    up_parts, down_parts = far(up_near), far(down_near)
    arrived_sib = sibling(arrived)
    rows = call(
        compact_kernel,
        [shape(4, 2, 2 * n, q)],
        [arrived, arrived_sib],
        [pl.BlockSpec((wire, 3 * q), lambda kind: (0, kind))] * 2,
        [pl.BlockSpec((4, 1, 2 * n, q), lambda kind: (0, kind, 0, 0))],
        grid=(2,),
        name="compact",
    )[0]
    dma = pltpu.SemaphoreType.DMA
    hid, slope, silu, to_l, to_r, to_oa, to_ob = call(
        forward_kernel,
        [shape(2 * n, width)]
        + [shape(2 * n, width, dtype=F32)] * 2
        + [shape(2, n, q)] * 2
        + [shape(2, n // 2, q)] * 2,
        [x, rows, *gate_parts, *up_parts],
        [smem()] + [hbm()] * 11,
        [vmem()] * 3 + [hbm()] * 4,
        scratch=[
            pltpu.VMEM((4, q, 2 * width), BF),
            pltpu.VMEM((4, 2 * n, q), BF),
            pltpu.VMEM((3, n, q), BF),
            pltpu.VMEM((2 * n, 2 * width), F32),
            dma((10,)),
            dma((4,)),
            dma((3,)),
            dma((8,)),
        ],
        flops=32 * 2 * n * features * width,
        name="forward",
    )
    to_l, to_r, to_oa, to_ob, down_parts = lax.optimization_barrier(
        (to_l, to_r, to_oa, to_ob, down_parts)
    )
    from_r, from_l = shift(to_l, -1), shift(to_r, 1)
    half_a, half_b = shift(to_oa, 1), shift(to_ob, -1)

    own_out, sib_out, grads = call(
        down_kernel,
        [shape(4, n, q)] * 2 + [shape(2 * n, 3 * width)],
        [x, hid, slope, silu, rows, *down_parts],
        [smem()] + [vmem()] * 3 + [hbm()] * 6,
        [hbm()] * 2 + [vmem()],
        scratch=[
            pltpu.VMEM((4, width, q), BF),
            pltpu.VMEM((4, 2 * n, q), BF),
            pltpu.VMEM((4, 2 * n, q), BF),
            dma((5,)),
            dma((4,)),
            dma((8,)),
        ],
        name="down",
    )
    own_grad, sib_grad = call(
        input_kernel,
        [shape(4, n, q)] * 2,
        [x, grads, *gate_parts, *up_parts],
        [smem()] + [vmem()] + [hbm()] * 10,
        [hbm()] * 2,
        scratch=[
            pltpu.VMEM((4, q, 2 * width), BF),
            pltpu.VMEM((4, 2 * n, q), BF),
            dma((10,)),
            dma((8,)),
        ],
        name="inputs",
    )
    parts = [
        pl.BlockSpec((1, n, q), lambda j: (j, 0, 0)),
        pl.BlockSpec((1, n, q), lambda j: (3, 0, 0)),
    ] * 2
    out_sib = sibling(sib_out)
    sib_grad, from_l, from_r = lax.optimization_barrier((sib_grad, from_l, from_r))
    grad_sib = sibling(sib_grad)
    sent = call(
        expand_kernel,
        [shape(wire, 6 * q)],
        [own_out, own_out, out_sib, out_sib],
        parts,
        [pl.BlockSpec((wire, q), lambda j: (0, j))],
        grid=(3,),
        name="expand_out",
    )[0]
    sent = call(
        lambda _, *refs: expand_kernel(*refs),
        [shape(wire, 6 * q)],
        [sent, own_grad, own_grad, grad_sib, grad_sib],
        [hbm()] + parts,
        [pl.BlockSpec((wire, q), lambda j: (0, 3 + j))],
        grid=(3,),
        aliases={0: 0},
        name="expand_grad",
    )[0]
    sent, half_a, half_b = lax.optimization_barrier((sent, half_a, half_b))
    came = exchange(sent)

    from_oa, from_ob = shift(half_a, 1), shift(half_b, -1)
    grad_parts = ring(grads)
    mine = (from_l, from_r, from_oa, from_ob)
    theirs = tuple(sibling(v) for v in mine)
    d_gate, d_up, d_down = call(
        weight_kernel,
        [shape(q, width)] * 2 + [shape(width, q)],
        [x, rows, *mine, *theirs, *grad_parts],
        [smem()] + [hbm()] * 14,
        [vmem()] * 3,
        scratch=[
            pltpu.VMEM((2, 8 * n, q), BF),
            pltpu.VMEM((8 * n, 3 * width), BF),
            dma((9,)),
            dma((5,)),
        ],
        flops=6 * 8 * n * q * width,
        name="weights",
    )
    layer_out, tokens_grad = call(
        unpack_kernel,
        [shape(micro * toks, features)] * 2,
        [place, gates, came],
        [vmem()] * 3,
        [vmem()] * 2,
        flops=2 * 6 * wire * wire * q,
        name="unpack",
    )
    return (
        layer_out.reshape(tokens.shape),
        tokens_grad.reshape(tokens.shape),
        d_gate,
        d_up,
        d_down,
    )


def solution(mesh):
    rows = P(None, ("dp", "expert"), None)
    return jax.shard_map(
        body,
        mesh=mesh,
        in_specs=(rows, rows, rows, P("dp", "expert"), P("dp", "expert"), P("expert", "dp"), rows),
        out_specs=(rows, rows, P("dp", "expert"), P("dp", "expert"), P("expert", "dp")),
        check_vma=False,
    )
```

```python
import functools

import jax
import jax.numpy as jnp
from jax import lax
from jax.experimental import pallas as pl
from jax.experimental.pallas import tpu as pltpu
from jax.sharding import PartitionSpec as P

BF = jnp.bfloat16
F32 = jnp.float32
LIMIT = 56 * 1024 * 1024


def dot(a, b):
    return jnp.dot(a, b, preferred_element_type=F32)


def dot_t(a, b):
    return lax.dot_general(a, b, (((1,), (1,)), ((), ())), preferred_element_type=F32)


def tdot(a, b):
    return lax.dot_general(a, b, (((0,), (0,)), ((), ())), preferred_element_type=F32)


def onehot(cond):
    return jnp.where(cond, 1.0, 0.0).astype(BF)


def iota(shape, dim):
    return lax.broadcasted_iota(jnp.int32, shape, dim)


def as_column(row):
    n = row.shape[1]
    return jnp.sum(jnp.where(iota((n, n), 0) == iota((n, n), 1), row, 0), axis=1, keepdims=True)


def slot_matrices(place, rows):
    n = place.shape[1]
    at = iota((rows, n), 0)
    base = place // 8 * 8
    slot = place - base
    main = onehot(at == place)
    tail = base + 6 + slot % 2
    return [
        jnp.concatenate([main, onehot((at == tail) & (slot // 2 == j))], axis=1) for j in range(3)
    ]


def as_row(ref):
    return jnp.concatenate([ref[m] for m in range(ref.shape[0])], axis=1)


def pack_kernel(ids_ref, gate_ref, tokens, cot, out, place_out):
    ids, gate = as_row(ids_ref), as_row(gate_ref)
    n = ids.shape[1]
    half = n // 2
    q = tokens.shape[1] // 4
    earlier, later = iota((n, n), 0), iota((n, n), 1)
    same = (as_column(ids) == ids) & (earlier < later) & (earlier // half == later // half)
    rank = jnp.sum(jnp.where(same, 1, 0), axis=0, keepdims=True)
    place = ids * 8 + iota((1, n), 1) // half * 3 + rank
    place_out[...] = place
    choose = slot_matrices(place, out.shape[0])
    weight = as_column(gate)
    for kind in range(2):
        def part(j):
            rows = (tokens if kind == 0 else cot)[:, j * q : (j + 1) * q]
            return rows if kind == 0 else (weight * rows.astype(F32)).astype(BF)
        last = part(3)
        for j in range(3):
            both = jnp.concatenate([part(j), last], axis=0)
            lo = (kind * 3 + j) * q
            out[:, lo : lo + q] = dot(choose[j], both).astype(BF)


def unpack_kernel(place, gate, back, layer, grad):
    n = place.shape[1]
    q = layer.shape[1] // 4
    choose = slot_matrices(place[...], back.shape[0])
    weight = as_column(as_row(gate))
    for kind in range(2):
        def put(j, rows):
            if kind == 0:
                layer[:, j * q : (j + 1) * q] = (weight * rows.astype(BF).astype(F32)).astype(BF)
            else:
                grad[:, j * q : (j + 1) * q] = rows.astype(BF)
        last = jnp.zeros((n, q), F32)
        for j in range(3):
            lo = (kind * 3 + j) * q
            got = tdot(choose[j], back[:, lo : lo + q])
            put(j, got[:n])
            last = last + got[n:]
        put(3, last)


def wire_places(shape_, dim):
    r = iota(shape_, dim)
    base, slot = r // 6 * 8, r % 6
    return base + slot, base + 6 + slot % 2, slot // 2


def compact_kernel(own, sib, out):
    n = out.shape[2] // 2
    q = out.shape[3]
    p = iota((n, own.shape[0]), 1)
    row, tail, part = wire_places((n, 1), 0)
    main = onehot(p == row)
    choose = [
        jnp.concatenate([main, onehot(p == jnp.where(part == j, tail, -1))], axis=0)
        for j in range(3)
    ]
    for place, source in enumerate((own, sib)):
        last = jnp.zeros((n, q), F32)
        for j in range(3):
            got = dot(choose[j], source[:, j * q : (j + 1) * q])
            out[j, 0, place * n : (place + 1) * n] = got[:n].astype(BF)
            last = last + got[n:]
        out[3, 0, place * n : (place + 1) * n] = last.astype(BF)


def expand_kernel(own, own_last, sib, sib_last, out):
    n = own.shape[1]
    p = iota((out.shape[0], n), 0)
    row, tail, part = wire_places((1, n), 1)
    tail = jnp.where(part == pl.program_id(0), tail, -1)
    choose = jnp.concatenate([onehot(p == row), onehot(p == tail)], axis=1)

    def total(a, b):
        return (a[0].astype(F32) + b[0].astype(F32)).astype(BF)

    both = jnp.concatenate([total(own, sib), total(own_last, sib_last)], axis=0)
    out[...] = dot(choose, both).astype(BF)


def gather_copies(pieces, buf, sem, lanes, first):
    half = pieces[3].shape[0]
    views = [
        (buf.at[0, :, lanes], 0),
        (buf.at[1, :, lanes], 1),
        (buf.at[2, :, lanes], 2),
        (buf.at[3, pl.ds(0, half), lanes], 3),
        (buf.at[3, pl.ds(half, half), lanes], 3),
    ]
    return [
        [
            pltpu.make_async_copy(piece, view, sem.at[first + n])
            for n, (piece, (view, at)) in enumerate(zip(pieces, views))
            if at == k
        ]
        for k in range(4)
    ]


SHIFTS = (0, 3, 1, 2)


def forward_kernel(x, rows, *refs):
    gate_all, up_parts = refs[0], refs[1:6]
    hid, slope, silu, to_l, to_r, to_oa, to_ob = refs[6:13]
    w, t, u, acc, sem, tsem, usem, ssem = refs[13:]
    me = x[0]
    n = rows.shape[2] // 2
    spots = [lax.rem(me + s, 4) for s in SHIFTS]
    width = hid.shape[1]
    gate_c = [
        [pltpu.make_async_copy(gate_all.at[spots[k]], w.at[k, :, pl.ds(0, width)], sem.at[k])]
        for k in range(4)
    ]
    up_c = gather_copies(up_parts, w, sem, pl.ds(width, width), 5)
    row_c = [
        pltpu.make_async_copy(rows.at[spots[k], 0], t.at[k], tsem.at[k]) for k in range(4)
    ]
    for k in range(4):
        for c in [row_c[k]] + gate_c[k] + up_c[k]:
            c.start()
    h = n // 2
    fetch = [
        pltpu.make_async_copy(rows.at[spots[k], 1, pl.ds(0, n)], u.at[k - 1], usem.at[k - 1])
        for k in (1, 2, 3)
    ]
    for c in fetch:
        c.start()
    slices = []
    for number, (k, lo, size, target) in enumerate(
        [(1, 0, n, to_l), (2, 0, n, to_r), (3, 0, h, to_oa), (3, h, h, to_ob)]
    ):
        for kind, source in enumerate((t.at[k], u.at[k - 1])):
            slices.append(
                pltpu.make_async_copy(
                    source.at[pl.ds(lo, size)], target.at[kind], ssem.at[number * 2 + kind]
                )
            )
    for k in range(4):
        for c in [row_c[k]] + gate_c[k] + up_c[k]:
            c.wait()
        term = dot(t[k], w[k])
        if k == 0:
            acc[...] = term
        else:
            acc[...] += term
    for c in fetch:
        c.wait()
    for c in slices:
        c.start()
    pre_gate, pre_up = acc[:, :width], acc[:, width:]
    s = jax.nn.sigmoid(pre_gate)
    act = pre_gate * s
    hid[...] = (act * pre_up).astype(BF)
    silu[...] = act
    slope[...] = pre_up * (s * (1.0 + pre_gate * (1.0 - s)))
    for c in slices:
        c.wait()


def hand_out(value, k, spot, o, own, sib, sem):
    n = own.shape[1]
    o[k] = value.astype(BF)
    copies = [
        pltpu.make_async_copy(o.at[k, pl.ds(i * n, n)], target.at[spot], sem.at[k * 2 + i])
        for i, target in enumerate((own, sib))
    ]
    for c in copies:
        c.start()
    return copies


def down_kernel(x, hid, slope, silu, rows, *refs):
    down_parts = refs[0:5]
    own, sib, grads = refs[5:8]
    wd, u, o, dsem, usem, osem = refs[8:]
    width = hid.shape[1]
    spots = [lax.rem(x[0] + s, 4) for s in SHIFTS]
    down_c = gather_copies(down_parts, wd, dsem, pl.ds(0, u.shape[2]), 0)
    row_c = [pltpu.make_async_copy(rows.at[spots[k], 1], u.at[k], usem.at[k]) for k in range(4)]
    for k in range(4):
        for c in [row_c[k]] + down_c[k]:
            c.start()
    sent = []
    back = jnp.zeros(hid.shape, F32)
    for k in range(4):
        for c in [row_c[k]] + down_c[k]:
            c.wait()
        sent += hand_out(dot(hid[...], wd[k]), k, spots[k], o, own, sib, osem)
        back = back + dot_t(u[k], wd[k])
    grads[:, 0:width] = hid[...]
    grads[:, width : 2 * width] = (back * slope[...]).astype(BF)
    grads[:, 2 * width :] = (back * silu[...]).astype(BF)
    for c in sent:
        c.wait()


def input_kernel(x, grads, *refs):
    gate_all, up_parts = refs[0], refs[1:6]
    own, sib = refs[6:8]
    w, o, sem, osem = refs[8:]
    width = w.shape[2] // 2
    spots = [lax.rem(x[0] + s, 4) for s in SHIFTS]
    gate_c = [
        [pltpu.make_async_copy(gate_all.at[spots[k]], w.at[k, :, pl.ds(0, width)], sem.at[k])]
        for k in range(4)
    ]
    up_c = gather_copies(up_parts, w, sem, pl.ds(width, width), 5)
    for k in range(4):
        for c in gate_c[k] + up_c[k]:
            c.start()
    sent = []
    for k in range(4):
        for c in gate_c[k] + up_c[k]:
            c.wait()
        sent += hand_out(dot_t(grads[:, width:], w[k]), k, spots[k], o, own, sib, osem)
    for c in sent:
        c.wait()


def weight_kernel(x, rows, *refs):
    mine, theirs = refs[0:4], refs[4:8]
    parts = refs[8:13]
    d_gate, d_up, d_down = refs[13:16]
    t, g, tsem, gsem = refs[16:]
    n = rows.shape[2] // 2
    h = n // 2
    width = d_gate.shape[1]
    copies = [pltpu.make_async_copy(rows.at[x[0]], t.at[:, pl.ds(0, 2 * n)], tsem.at[8])]
    for number, group in enumerate((mine, theirs)):
        base = number * n
        spots = [
            (1, base, n),
            (2, base, n),
            (3, base, h),
            (3, base + h, h),
        ]
        for i, (piece, (k, start, size)) in enumerate(zip(group, spots)):
            copies.append(
                pltpu.make_async_copy(
                    piece, t.at[:, pl.ds(k * 2 * n + start, size)], tsem.at[number * 4 + i]
                )
            )
    spots = [(0, 2 * n), (2 * n, 2 * n), (4 * n, 2 * n), (6 * n, n), (7 * n, n)]
    for i, (piece, (start, size)) in enumerate(zip(parts, spots)):
        copies.append(pltpu.make_async_copy(piece, g.at[pl.ds(start, size)], gsem.at[i]))
    for c in copies:
        c.start()
    for c in copies:
        c.wait()
    both = tdot(t[0], g[:, width:]).astype(BF)
    d_gate[...] = both[:, :width]
    d_up[...] = both[:, width:]
    d_down[...] = tdot(g[:, :width], t[1]).astype(BF)


def vmem():
    return pl.BlockSpec(memory_space=pltpu.VMEM)


def hbm():
    return pl.BlockSpec(memory_space=pl.ANY)


def smem():
    return pl.BlockSpec(memory_space=pltpu.SMEM)


def call(kernel, outs, ins, in_specs, out_specs, scratch=(), grid=(), aliases=None, flops=0, name=None):
    size = flops // 512
    return pl.pallas_call(
        kernel,
        out_shape=outs,
        grid=grid,
        input_output_aliases=aliases or {},
        in_specs=in_specs,
        out_specs=out_specs,
        scratch_shapes=list(scratch),
        compiler_params=pltpu.CompilerParams(vmem_limit_bytes=LIMIT),
        cost_estimate=pl.CostEstimate(flops=flops, bytes_accessed=size, transcendentals=0),
        name=name,
    )(*ins)


def shape(*dims, dtype=BF):
    return jax.ShapeDtypeStruct(dims, dtype)


def shift(v, k):
    n = lax.axis_size("dp")
    return lax.ppermute(v, "dp", [(i, (i + k) % n) for i in range(n)])


def sibling(v):
    return lax.ppermute(v, "expert", [(i, i ^ 1) for i in range(lax.axis_size("expert"))])


def near(v):
    return (v, shift(v, 1), shift(v, -1))


def halves(parts):
    half = parts[0].shape[0] // 2
    return parts + (parts[1][:half], parts[2][half:])


def far(parts):
    return parts[:3] + (shift(parts[3], 1), shift(parts[4], -1))


def ring(v):
    return far(halves(near(v)))


def exchange(v):
    devices = lax.axis_size("expert")
    groups = [[2 * i + c for i in range(devices // 2)] for c in range(2)]
    cut = v.reshape(devices // 2, 8, v.shape[1])
    cut = lax.all_to_all(
        cut, "expert", split_axis=0, concat_axis=0, axis_index_groups=groups, tiled=True
    )
    return cut.reshape(v.shape)


def body(tokens, expert_ids, gate_values, w_gate, w_up, w_down, cotangent):
    experts = lax.axis_size("expert") // 2
    micro, toks, features = tokens.shape
    q = features // 4
    width = w_gate.shape[1]
    wire = experts * 8
    n = experts * 6
    x = lax.axis_index("dp").astype(jnp.int32).reshape(1)
    gate_all = lax.all_gather(w_gate, "dp")
    up_parts, down_parts = ring(w_up), ring(w_down)

    ids = jnp.transpose(expert_ids, (0, 2, 1))
    gates = jnp.transpose(gate_values, (0, 2, 1))
    packed, place = call(
        pack_kernel,
        [shape(wire, 6 * q), shape(1, micro * toks, dtype=jnp.int32)],
        [ids, gates, tokens.reshape(-1, features), cotangent.reshape(-1, features)],
        [vmem()] * 4,
        [vmem()] * 2,
        flops=2 * 6 * wire * wire * q,
        name="pack",
    )
    arrived = exchange(packed)
    arrived, up_parts, down_parts = lax.optimization_barrier((arrived, up_parts, down_parts))
    arrived_sib = sibling(arrived)
    rows = call(
        compact_kernel,
        [shape(4, 2, 2 * n, q)],
        [arrived, arrived_sib],
        [pl.BlockSpec((wire, 3 * q), lambda kind: (0, kind))] * 2,
        [pl.BlockSpec((4, 1, 2 * n, q), lambda kind: (0, kind, 0, 0))],
        grid=(2,),
        name="compact",
    )[0]
    dma = pltpu.SemaphoreType.DMA
    hid, slope, silu, to_l, to_r, to_oa, to_ob = call(
        forward_kernel,
        [shape(2 * n, width)]
        + [shape(2 * n, width, dtype=F32)] * 2
        + [shape(2, n, q)] * 2
        + [shape(2, n // 2, q)] * 2,
        [x, rows, gate_all, *up_parts],
        [smem()] + [hbm()] * 7,
        [vmem()] * 3 + [hbm()] * 4,
        scratch=[
            pltpu.VMEM((4, q, 2 * width), BF),
            pltpu.VMEM((4, 2 * n, q), BF),
            pltpu.VMEM((3, n, q), BF),
            pltpu.VMEM((2 * n, 2 * width), F32),
            dma((10,)),
            dma((4,)),
            dma((3,)),
            dma((8,)),
        ],
        flops=32 * 2 * n * features * width,
        name="forward",
    )
    to_l, to_r, to_oa, to_ob, down_parts = lax.optimization_barrier(
        (to_l, to_r, to_oa, to_ob, down_parts)
    )
    from_r, from_l = shift(to_l, -1), shift(to_r, 1)
    half_a, half_b = shift(to_oa, 1), shift(to_ob, -1)

    own_out, sib_out, grads = call(
        down_kernel,
        [shape(4, n, q)] * 2 + [shape(2 * n, 3 * width)],
        [x, hid, slope, silu, rows, *down_parts],
        [smem()] + [vmem()] * 3 + [hbm()] * 6,
        [hbm()] * 2 + [vmem()],
        scratch=[
            pltpu.VMEM((4, width, q), BF),
            pltpu.VMEM((4, 2 * n, q), BF),
            pltpu.VMEM((4, 2 * n, q), BF),
            dma((5,)),
            dma((4,)),
            dma((8,)),
        ],
        name="down",
    )
    own_grad, sib_grad = call(
        input_kernel,
        [shape(4, n, q)] * 2,
        [x, grads, gate_all, *up_parts],
        [smem()] + [vmem()] + [hbm()] * 6,
        [hbm()] * 2,
        scratch=[
            pltpu.VMEM((4, q, 2 * width), BF),
            pltpu.VMEM((4, 2 * n, q), BF),
            dma((10,)),
            dma((8,)),
        ],
        flops=32 * 2 * n * features * width,
        name="inputs",
    )
    parts = [
        pl.BlockSpec((1, n, q), lambda j: (j, 0, 0)),
        pl.BlockSpec((1, n, q), lambda j: (3, 0, 0)),
    ] * 2
    out_sib = sibling(sib_out)
    sib_grad, out_sib, from_l, from_r = lax.optimization_barrier(
        (sib_grad, out_sib, from_l, from_r)
    )
    grad_sib = sibling(sib_grad)
    sent = call(
        expand_kernel,
        [shape(wire, 6 * q)],
        [own_out, own_out, out_sib, out_sib],
        parts,
        [pl.BlockSpec((wire, q), lambda j: (0, j))],
        grid=(3,),
        name="expand_out",
    )[0]
    sent = call(
        lambda _, *refs: expand_kernel(*refs),
        [shape(wire, 6 * q)],
        [sent, own_grad, own_grad, grad_sib, grad_sib],
        [hbm()] + parts,
        [pl.BlockSpec((wire, q), lambda j: (0, 3 + j))],
        grid=(3,),
        aliases={0: 0},
        name="expand_grad",
    )[0]
    sent, half_a, half_b = lax.optimization_barrier((sent, half_a, half_b))
    came = exchange(sent)

    from_oa, from_ob = shift(half_a, 1), shift(half_b, -1)
    grad_parts = ring(grads)
    mine = (from_l, from_r, from_oa, from_ob)
    theirs = tuple(sibling(v) for v in mine)
    d_gate, d_up, d_down = call(
        weight_kernel,
        [shape(q, width)] * 2 + [shape(width, q)],
        [x, rows, *mine, *theirs, *grad_parts],
        [smem()] + [hbm()] * 14,
        [vmem()] * 3,
        scratch=[
            pltpu.VMEM((2, 8 * n, q), BF),
            pltpu.VMEM((8 * n, 3 * width), BF),
            dma((9,)),
            dma((5,)),
        ],
        flops=6 * 8 * n * q * width,
        name="weights",
    )
    layer_out, tokens_grad = call(
        unpack_kernel,
        [shape(micro * toks, features)] * 2,
        [place, gates, came],
        [vmem()] * 3,
        [vmem()] * 2,
        flops=2 * 6 * wire * wire * q,
        name="unpack",
    )
    return (
        layer_out.reshape(tokens.shape),
        tokens_grad.reshape(tokens.shape),
        d_gate,
        d_up,
        d_down,
    )


def solution(mesh):
    rows = P(None, ("dp", "expert"), None)
    return jax.shard_map(
        body,
        mesh=mesh,
        in_specs=(rows, rows, rows, P("dp", "expert"), P("dp", "expert"), P("expert", "dp"), rows),
        out_specs=(rows, rows, P("dp", "expert"), P("dp", "expert"), P("expert", "dp")),
        check_vma=False,
    )
```

```python
import functools

import jax
import jax.numpy as jnp
from jax import lax
from jax.experimental import pallas as pl
from jax.experimental.pallas import tpu as pltpu
from jax.sharding import PartitionSpec as P

BF = jnp.bfloat16
F32 = jnp.float32
LIMIT = 56 * 1024 * 1024


def dot(a, b):
    return jnp.dot(a, b, preferred_element_type=F32)


def dot_t(a, b):
    return lax.dot_general(a, b, (((1,), (1,)), ((), ())), preferred_element_type=F32)


def tdot(a, b):
    return lax.dot_general(a, b, (((0,), (0,)), ((), ())), preferred_element_type=F32)


def onehot(cond):
    return jnp.where(cond, 1.0, 0.0).astype(BF)


def iota(shape, dim):
    return lax.broadcasted_iota(jnp.int32, shape, dim)


def as_column(row):
    n = row.shape[1]
    return jnp.sum(jnp.where(iota((n, n), 0) == iota((n, n), 1), row, 0), axis=1, keepdims=True)


def slot_matrices(place, rows):
    n = place.shape[1]
    at = iota((rows, n), 0)
    base = place // 8 * 8
    slot = place - base
    main = onehot(at == place)
    tail = base + 6 + slot % 2
    return [
        jnp.concatenate([main, onehot((at == tail) & (slot // 2 == j))], axis=1) for j in range(3)
    ]


def as_row(ref):
    return jnp.concatenate([ref[m] for m in range(ref.shape[0])], axis=1)


def pack_kernel(ids_ref, gate_ref, tokens, cot, out, place_out):
    ids, gate = as_row(ids_ref), as_row(gate_ref)
    n = ids.shape[1]
    half = n // 2
    q = tokens.shape[1] // 4
    earlier, later = iota((n, n), 0), iota((n, n), 1)
    same = (as_column(ids) == ids) & (earlier < later) & (earlier // half == later // half)
    rank = jnp.sum(jnp.where(same, 1, 0), axis=0, keepdims=True)
    place = ids * 8 + iota((1, n), 1) // half * 3 + rank
    place_out[...] = place
    choose = slot_matrices(place, out.shape[0])
    weight = as_column(gate)
    for kind in range(2):
        def part(j):
            rows = (tokens if kind == 0 else cot)[:, j * q : (j + 1) * q]
            return rows if kind == 0 else (weight * rows.astype(F32)).astype(BF)
        last = part(3)
        for j in range(3):
            both = jnp.concatenate([part(j), last], axis=0)
            lo = (kind * 3 + j) * q
            out[:, lo : lo + q] = dot(choose[j], both).astype(BF)


def unpack_kernel(place, gate, back, layer, grad):
    n = place.shape[1]
    q = layer.shape[1] // 4
    choose = slot_matrices(place[...], back.shape[0])
    weight = as_column(as_row(gate))
    for kind in range(2):
        def put(j, rows):
            if kind == 0:
                layer[:, j * q : (j + 1) * q] = (weight * rows.astype(BF).astype(F32)).astype(BF)
            else:
                grad[:, j * q : (j + 1) * q] = rows.astype(BF)
        last = jnp.zeros((n, q), F32)
        for j in range(3):
            lo = (kind * 3 + j) * q
            got = tdot(choose[j], back[:, lo : lo + q])
            put(j, got[:n])
            last = last + got[n:]
        put(3, last)


def wire_places(shape_, dim):
    r = iota(shape_, dim)
    base, slot = r // 6 * 8, r % 6
    return base + slot, base + 6 + slot % 2, slot // 2


def compact_kernel(own, sib, out):
    n = out.shape[2] // 2
    q = out.shape[3]
    p = iota((n, own.shape[0]), 1)
    row, tail, part = wire_places((n, 1), 0)
    main = onehot(p == row)
    choose = [
        jnp.concatenate([main, onehot(p == jnp.where(part == j, tail, -1))], axis=0)
        for j in range(3)
    ]
    for place, source in enumerate((own, sib)):
        last = jnp.zeros((n, q), F32)
        for j in range(3):
            got = dot(choose[j], source[:, j * q : (j + 1) * q])
            out[j, 0, place * n : (place + 1) * n] = got[:n].astype(BF)
            last = last + got[n:]
        out[3, 0, place * n : (place + 1) * n] = last.astype(BF)


def expand_kernel(own, own_last, sib, sib_last, out):
    n = own.shape[1]
    p = iota((out.shape[0], n), 0)
    row, tail, part = wire_places((1, n), 1)
    tail = jnp.where(part == pl.program_id(0), tail, -1)
    choose = jnp.concatenate([onehot(p == row), onehot(p == tail)], axis=1)

    def total(a, b):
        return (a[0].astype(F32) + b[0].astype(F32)).astype(BF)

    both = jnp.concatenate([total(own, sib), total(own_last, sib_last)], axis=0)
    out[...] = dot(choose, both).astype(BF)


def gather_copies(pieces, buf, sem, lanes, first):
    half = buf.shape[1] // 2
    split = len(pieces) == 7
    spots = [0] + ([1, 1, 2, 2] if split else [1, 2]) + [3, 3]
    copies = [[] for _ in range(4)]
    for i, (piece, k) in enumerate(zip(pieces, spots)):
        low = half if i and spots[i - 1] == k else 0
        view = buf.at[k, pl.ds(low, piece.shape[0]), lanes]
        copies[k].append(pltpu.make_async_copy(piece, view, sem.at[first + i]))
    return copies


SHIFTS = (0, 3, 1, 2)


def forward_kernel(x, rows, *refs):
    gate_parts, up_parts = refs[0:5], refs[5:10]
    hid, slope, silu, to_l, to_r, to_oa, to_ob = refs[10:17]
    w, t, u, acc, sem, tsem, usem, ssem = refs[17:]
    me = x[0]
    n = rows.shape[2] // 2
    spots = [lax.rem(me + s, 4) for s in SHIFTS]
    width = hid.shape[1]
    gate_c = gather_copies(gate_parts, w, sem, pl.ds(0, width), 0)
    up_c = gather_copies(up_parts, w, sem, pl.ds(width, width), 5)
    row_c = [
        pltpu.make_async_copy(rows.at[spots[k], 0], t.at[k], tsem.at[k]) for k in range(4)
    ]
    for k in range(4):
        for c in [row_c[k]] + gate_c[k] + up_c[k]:
            c.start()
    h = n // 2
    fetch = [
        pltpu.make_async_copy(rows.at[spots[k], 1, pl.ds(0, n)], u.at[k - 1], usem.at[k - 1])
        for k in (1, 2, 3)
    ]
    for c in fetch:
        c.start()
    slices = []
    for number, (k, lo, size, target) in enumerate(
        [(1, 0, n, to_l), (2, 0, n, to_r), (3, 0, h, to_oa), (3, h, h, to_ob)]
    ):
        for kind, source in enumerate((t.at[k], u.at[k - 1])):
            slices.append(
                pltpu.make_async_copy(
                    source.at[pl.ds(lo, size)], target.at[kind], ssem.at[number * 2 + kind]
                )
            )
    for k in range(4):
        for c in [row_c[k]] + gate_c[k] + up_c[k]:
            c.wait()
        term = dot(t[k], w[k])
        if k == 0:
            acc[...] = term
        else:
            acc[...] += term
    for c in fetch:
        c.wait()
    for c in slices:
        c.start()
    pre_gate, pre_up = acc[:, :width], acc[:, width:]
    s = jax.nn.sigmoid(pre_gate)
    act = pre_gate * s
    hid[...] = (act * pre_up).astype(BF)
    silu[...] = act
    slope[...] = pre_up * (s * (1.0 + pre_gate * (1.0 - s)))
    for c in slices:
        c.wait()


def hand_out(value, k, spot, o, own, sib, sem):
    n = own.shape[1]
    o[k] = value.astype(BF)
    copies = [
        pltpu.make_async_copy(o.at[k, pl.ds(i * n, n)], target.at[spot], sem.at[k * 2 + i])
        for i, target in enumerate((own, sib))
    ]
    for c in copies:
        c.start()
    return copies


def down_kernel(x, hid, slope, silu, rows, *refs):
    down_parts = refs[0:7]
    own, sib, grads = refs[7:10]
    wd, u, o, dsem, usem, osem = refs[10:]
    width = hid.shape[1]
    spots = [lax.rem(x[0] + s, 4) for s in SHIFTS]
    down_c = gather_copies(down_parts, wd, dsem, pl.ds(0, u.shape[2]), 0)
    row_c = [pltpu.make_async_copy(rows.at[spots[k], 1], u.at[k], usem.at[k]) for k in range(4)]
    for k in range(4):
        for c in [row_c[k]] + down_c[k]:
            c.start()
    sent = []
    back = jnp.zeros(hid.shape, F32)
    for k in range(4):
        for c in [row_c[k]] + down_c[k]:
            c.wait()
        sent += hand_out(dot(hid[...], wd[k]), k, spots[k], o, own, sib, osem)
        back = back + dot_t(u[k], wd[k])
    grads[:, 0:width] = hid[...]
    grads[:, width : 2 * width] = (back * slope[...]).astype(BF)
    grads[:, 2 * width :] = (back * silu[...]).astype(BF)
    for c in sent:
        c.wait()


def input_kernel(x, grads, *refs):
    gate_parts, up_parts = refs[0:5], refs[5:10]
    own, sib = refs[10:12]
    w, o, sem, osem = refs[12:]
    width = w.shape[2] // 2
    gate_c = gather_copies(gate_parts, w, sem, pl.ds(0, width), 0)
    up_c = gather_copies(up_parts, w, sem, pl.ds(width, width), 5)
    for k in range(4):
        for c in gate_c[k] + up_c[k]:
            c.start()
    sent = []
    for k in range(4):
        for c in gate_c[k] + up_c[k]:
            c.wait()
        spot = lax.rem(x[0] + SHIFTS[k], 4)
        sent += hand_out(dot_t(grads[:, width:], w[k]), k, spot, o, own, sib, osem)
    for c in sent:
        c.wait()


def weight_kernel(x, rows, *refs):
    mine, theirs = refs[0:4], refs[4:8]
    parts = refs[8:13]
    d_gate, d_up, d_down = refs[13:16]
    t, g, tsem, gsem = refs[16:]
    n = rows.shape[2] // 2
    h = n // 2
    width = d_gate.shape[1]
    copies = [pltpu.make_async_copy(rows.at[x[0]], t.at[:, pl.ds(0, 2 * n)], tsem.at[8])]
    for number, group in enumerate((mine, theirs)):
        base = number * n
        spots = [
            (1, base, n),
            (2, base, n),
            (3, base, h),
            (3, base + h, h),
        ]
        for i, (piece, (k, start, size)) in enumerate(zip(group, spots)):
            copies.append(
                pltpu.make_async_copy(
                    piece, t.at[:, pl.ds(k * 2 * n + start, size)], tsem.at[number * 4 + i]
                )
            )
    spots = [(0, 2 * n), (2 * n, 2 * n), (4 * n, 2 * n), (6 * n, n), (7 * n, n)]
    for i, (piece, (start, size)) in enumerate(zip(parts, spots)):
        copies.append(pltpu.make_async_copy(piece, g.at[pl.ds(start, size)], gsem.at[i]))
    for c in copies:
        c.start()
    for c in copies:
        c.wait()
    both = tdot(t[0], g[:, width:]).astype(BF)
    d_gate[...] = both[:, :width]
    d_up[...] = both[:, width:]
    d_down[...] = tdot(g[:, :width], t[1]).astype(BF)


def vmem():
    return pl.BlockSpec(memory_space=pltpu.VMEM)


def hbm():
    return pl.BlockSpec(memory_space=pl.ANY)


def smem():
    return pl.BlockSpec(memory_space=pltpu.SMEM)


def call(kernel, outs, ins, in_specs, out_specs, scratch=(), grid=(), aliases=None, flops=0, name=None):
    size = flops // 512
    return pl.pallas_call(
        kernel,
        out_shape=outs,
        grid=grid,
        input_output_aliases=aliases or {},
        in_specs=in_specs,
        out_specs=out_specs,
        scratch_shapes=list(scratch),
        compiler_params=pltpu.CompilerParams(vmem_limit_bytes=LIMIT),
        cost_estimate=pl.CostEstimate(flops=flops, bytes_accessed=size, transcendentals=0),
        name=name,
    )(*ins)


def shape(*dims, dtype=BF):
    return jax.ShapeDtypeStruct(dims, dtype)


def shift(v, k):
    n = lax.axis_size("dp")
    return lax.ppermute(v, "dp", [(i, (i + k) % n) for i in range(n)])


def sibling(v):
    return lax.ppermute(v, "expert", [(i, i ^ 1) for i in range(lax.axis_size("expert"))])


def near(v):
    return (v, shift(v, 1), shift(v, -1))


def halves(parts):
    half = parts[0].shape[0] // 2
    return parts + (parts[1][:half], parts[2][half:])


def far(parts):
    return parts[:3] + (shift(parts[3], 1), shift(parts[4], -1))


def ring(v):
    return far(halves(near(v)))


def exchange(v):
    devices = lax.axis_size("expert")
    groups = [[2 * i + c for i in range(devices // 2)] for c in range(2)]
    cut = v.reshape(devices // 2, 8, v.shape[1])
    cut = lax.all_to_all(
        cut, "expert", split_axis=0, concat_axis=0, axis_index_groups=groups, tiled=True
    )
    return cut.reshape(v.shape)


def body(tokens, expert_ids, gate_values, w_gate, w_up, w_down, cotangent):
    experts = lax.axis_size("expert") // 2
    micro, toks, features = tokens.shape
    q = features // 4
    width = w_gate.shape[1]
    wire = experts * 8
    n = experts * 6
    x = lax.axis_index("dp").astype(jnp.int32).reshape(1)
    gate_near = near(w_gate)
    up_near, w_down = lax.optimization_barrier((near(w_up), w_down))
    middle = w_down.shape[0] // 2
    gate_parts, up_parts = far(halves(gate_near)), far(halves(up_near))
    down_a = near(w_down[:middle])

    ids = jnp.transpose(expert_ids, (0, 2, 1))
    gates = jnp.transpose(gate_values, (0, 2, 1))
    packed, place = call(
        pack_kernel,
        [shape(wire, 6 * q), shape(1, micro * toks, dtype=jnp.int32)],
        [ids, gates, tokens.reshape(-1, features), cotangent.reshape(-1, features)],
        [vmem()] * 4,
        [vmem()] * 2,
        flops=2 * 6 * wire * wire * q,
        name="pack",
    )
    arrived = exchange(packed)
    arrived, gate_parts, up_parts, down_a, w_down = lax.optimization_barrier(
        (arrived, gate_parts, up_parts, down_a, w_down)
    )
    down_b = near(w_down[middle:])
    down_parts = (
        w_down, down_a[1], down_b[1], down_a[2], down_b[2], shift(down_a[1], 1), shift(down_b[2], -1)
    )
    arrived_sib = sibling(arrived)
    rows = call(
        compact_kernel,
        [shape(4, 2, 2 * n, q)],
        [arrived, arrived_sib],
        [pl.BlockSpec((wire, 3 * q), lambda kind: (0, kind))] * 2,
        [pl.BlockSpec((4, 1, 2 * n, q), lambda kind: (0, kind, 0, 0))],
        grid=(2,),
        name="compact",
    )[0]
    dma = pltpu.SemaphoreType.DMA
    hid, slope, silu, to_l, to_r, to_oa, to_ob = call(
        forward_kernel,
        [shape(2 * n, width)]
        + [shape(2 * n, width, dtype=F32)] * 2
        + [shape(2, n, q)] * 2
        + [shape(2, n // 2, q)] * 2,
        [x, rows, *gate_parts, *up_parts],
        [smem()] + [hbm()] * 11,
        [vmem()] * 3 + [hbm()] * 4,
        scratch=[
            pltpu.VMEM((4, q, 2 * width), BF),
            pltpu.VMEM((4, 2 * n, q), BF),
            pltpu.VMEM((3, n, q), BF),
            pltpu.VMEM((2 * n, 2 * width), F32),
            dma((10,)),
            dma((4,)),
            dma((3,)),
            dma((8,)),
        ],
        flops=32 * 2 * n * features * width,
        name="forward",
    )
    to_l, to_r, to_oa, to_ob, down_parts = lax.optimization_barrier(
        (to_l, to_r, to_oa, to_ob, down_parts)
    )
    from_r, from_l = shift(to_l, -1), shift(to_r, 1)
    half_a, half_b = shift(to_oa, 1), shift(to_ob, -1)

    own_out, sib_out, grads = call(
        down_kernel,
        [shape(4, n, q)] * 2 + [shape(2 * n, 3 * width)],
        [x, hid, slope, silu, rows, *down_parts],
        [smem()] + [vmem()] * 3 + [hbm()] * 8,
        [hbm()] * 2 + [vmem()],
        scratch=[
            pltpu.VMEM((4, width, q), BF),
            pltpu.VMEM((4, 2 * n, q), BF),
            pltpu.VMEM((4, 2 * n, q), BF),
            dma((7,)),
            dma((4,)),
            dma((8,)),
        ],
        name="down",
    )
    own_grad, sib_grad = call(
        input_kernel,
        [shape(4, n, q)] * 2,
        [x, grads, *gate_parts, *up_parts],
        [smem()] + [vmem()] + [hbm()] * 10,
        [hbm()] * 2,
        scratch=[
            pltpu.VMEM((4, q, 2 * width), BF),
            pltpu.VMEM((4, 2 * n, q), BF),
            dma((10,)),
            dma((8,)),
        ],
        name="inputs",
    )
    parts = [
        pl.BlockSpec((1, n, q), lambda j: (j, 0, 0)),
        pl.BlockSpec((1, n, q), lambda j: (3, 0, 0)),
    ] * 2
    sib_out, half_a, half_b = lax.optimization_barrier((sib_out, half_a, half_b))
    out_sib = sibling(sib_out)
    sib_grad, out_sib = lax.optimization_barrier((sib_grad, out_sib))
    grad_sib = sibling(sib_grad)
    sent = call(
        expand_kernel,
        [shape(wire, 6 * q)],
        [own_out, own_out, out_sib, out_sib],
        parts,
        [pl.BlockSpec((wire, q), lambda j: (0, j))],
        grid=(3,),
        name="expand_out",
    )[0]
    sent = call(
        lambda _, *refs: expand_kernel(*refs),
        [shape(wire, 6 * q)],
        [sent, own_grad, own_grad, grad_sib, grad_sib],
        [hbm()] + parts,
        [pl.BlockSpec((wire, q), lambda j: (0, 3 + j))],
        grid=(3,),
        aliases={0: 0},
        name="expand_grad",
    )[0]
    sent, from_l, from_r = lax.optimization_barrier((sent, from_l, from_r))
    came = exchange(sent)

    from_oa, from_ob = shift(half_a, 1), shift(half_b, -1)
    grad_parts = ring(grads)
    mine = (from_l, from_r, from_oa, from_ob)
    theirs = tuple(sibling(v) for v in mine)
    d_gate, d_up, d_down = call(
        weight_kernel,
        [shape(q, width)] * 2 + [shape(width, q)],
        [x, rows, *mine, *theirs, *grad_parts],
        [smem()] + [hbm()] * 14,
        [vmem()] * 3,
        scratch=[
            pltpu.VMEM((2, 8 * n, q), BF),
            pltpu.VMEM((8 * n, 3 * width), BF),
            dma((9,)),
            dma((5,)),
        ],
        flops=6 * 8 * n * q * width,
        name="weights",
    )
    layer_out, tokens_grad = call(
        unpack_kernel,
        [shape(micro * toks, features)] * 2,
        [place, gates, came],
        [vmem()] * 3,
        [vmem()] * 2,
        flops=2 * 6 * wire * wire * q,
        name="unpack",
    )
    return (
        layer_out.reshape(tokens.shape),
        tokens_grad.reshape(tokens.shape),
        d_gate,
        d_up,
        d_down,
    )


def solution(mesh):
    rows = P(None, ("dp", "expert"), None)
    return jax.shard_map(
        body,
        mesh=mesh,
        in_specs=(rows, rows, rows, P("dp", "expert"), P("dp", "expert"), P("expert", "dp"), rows),
        out_specs=(rows, rows, P("dp", "expert"), P("dp", "expert"), P("expert", "dp")),
        check_vma=False,
    )
```

```python
import functools

import jax
import jax.numpy as jnp
from jax import lax
from jax.experimental import pallas as pl
from jax.experimental.pallas import tpu as pltpu
from jax.sharding import PartitionSpec as P

BF = jnp.bfloat16
F32 = jnp.float32
LIMIT = 62 * 1024 * 1024


def dot(a, b):
    return jnp.dot(a, b, preferred_element_type=F32)


def dot_t(a, b):
    return lax.dot_general(a, b, (((1,), (1,)), ((), ())), preferred_element_type=F32)


def tdot(a, b):
    return lax.dot_general(a, b, (((0,), (0,)), ((), ())), preferred_element_type=F32)


def onehot(cond):
    return jnp.where(cond, 1.0, 0.0).astype(BF)


def iota(shape, dim):
    return lax.broadcasted_iota(jnp.int32, shape, dim)


def as_column(row):
    n = row.shape[1]
    return jnp.sum(jnp.where(iota((n, n), 0) == iota((n, n), 1), row, 0), axis=1, keepdims=True)


def slot_matrices(place, rows):
    n = place.shape[1]
    at = iota((rows, n), 0)
    base = place // 8 * 8
    slot = place - base
    main = onehot(at == place)
    tail = base + 6 + slot % 2
    return [
        jnp.concatenate([main, onehot((at == tail) & (slot // 2 == j))], axis=1) for j in range(3)
    ]


def as_row(ref):
    return jnp.concatenate([ref[m] for m in range(ref.shape[0])], axis=1)


def pack_kernel(ids_ref, gate_ref, tokens, cot, out, place_out):
    ids, gate = as_row(ids_ref), as_row(gate_ref)
    n = ids.shape[1]
    half = n // 2
    q = tokens.shape[1] // 4
    earlier, later = iota((n, n), 0), iota((n, n), 1)
    same = (as_column(ids) == ids) & (earlier < later) & (earlier // half == later // half)
    rank = jnp.sum(jnp.where(same, 1, 0), axis=0, keepdims=True)
    place = ids * 8 + iota((1, n), 1) // half * 3 + rank
    place_out[...] = place
    choose = slot_matrices(place, out.shape[0])
    weight = as_column(gate)
    for kind in range(2):
        def part(j):
            rows = (tokens if kind == 0 else cot)[:, j * q : (j + 1) * q]
            return rows if kind == 0 else (weight * rows.astype(F32)).astype(BF)
        last = part(3)
        for j in range(3):
            both = jnp.concatenate([part(j), last], axis=0)
            lo = (kind * 3 + j) * q
            out[:, lo : lo + q] = dot(choose[j], both).astype(BF)


def unpack_kernel(place, gate, back, layer, grad):
    n = place.shape[1]
    q = layer.shape[1] // 4
    choose = slot_matrices(place[...], back.shape[0])
    weight = as_column(as_row(gate))
    for kind in range(2):
        def put(j, rows):
            if kind == 0:
                layer[:, j * q : (j + 1) * q] = (weight * rows.astype(BF).astype(F32)).astype(BF)
            else:
                grad[:, j * q : (j + 1) * q] = rows.astype(BF)
        last = jnp.zeros((n, q), F32)
        for j in range(3):
            lo = (kind * 3 + j) * q
            got = tdot(choose[j], back[:, lo : lo + q])
            put(j, got[:n])
            last = last + got[n:]
        put(3, last)


def wire_places(shape_, dim):
    r = iota(shape_, dim)
    base, slot = r // 6 * 8, r % 6
    return base + slot, base + 6 + slot % 2, slot // 2


def compact_kernel(own, sib, out):
    n = out.shape[2] // 2
    q = out.shape[3]
    p = iota((n, own.shape[0]), 1)
    row, tail, part = wire_places((n, 1), 0)
    main = onehot(p == row)
    choose = [
        jnp.concatenate([main, onehot(p == jnp.where(part == j, tail, -1))], axis=0)
        for j in range(3)
    ]
    for place, source in enumerate((own, sib)):
        last = jnp.zeros((n, q), F32)
        for j in range(3):
            got = dot(choose[j], source[:, j * q : (j + 1) * q])
            out[j, 0, place * n : (place + 1) * n] = got[:n].astype(BF)
            last = last + got[n:]
        out[3, 0, place * n : (place + 1) * n] = last.astype(BF)


def expand_kernel(own, own_last, sib, sib_last, out):
    n = own.shape[1]
    p = iota((out.shape[0], n), 0)
    row, tail, part = wire_places((1, n), 1)
    tail = jnp.where(part == pl.program_id(0), tail, -1)
    choose = jnp.concatenate([onehot(p == row), onehot(p == tail)], axis=1)

    def total(a, b):
        return (a[0].astype(F32) + b[0].astype(F32)).astype(BF)

    both = jnp.concatenate([total(own, sib), total(own_last, sib_last)], axis=0)
    out[...] = dot(choose, both).astype(BF)


def gather_copies(pieces, buf, sem, lanes, first):
    half = pieces[3].shape[0]
    views = [
        (buf.at[0, :, lanes], 0),
        (buf.at[1, :, lanes], 1),
        (buf.at[2, :, lanes], 2),
        (buf.at[3, pl.ds(0, half), lanes], 3),
        (buf.at[3, pl.ds(half, half), lanes], 3),
    ]
    return [
        [
            pltpu.make_async_copy(piece, view, sem.at[first + n])
            for n, (piece, (view, at)) in enumerate(zip(pieces, views))
            if at == k
        ]
        for k in range(4)
    ]


SHIFTS = (0, 3, 1, 2)


def forward_kernel(x, rows, *refs):
    gate_parts, up_parts = refs[0:5], refs[5:10]
    hid, slope, silu, to_l, to_r, to_oa, to_ob = refs[10:17]
    w, t, u, acc, sem, tsem, usem, ssem = refs[17:]
    me = x[0]
    n = rows.shape[2] // 2
    spots = [lax.rem(me + s, 4) for s in SHIFTS]
    width = hid.shape[1]
    gate_c = gather_copies(gate_parts, w, sem, pl.ds(0, width), 0)
    up_c = gather_copies(up_parts, w, sem, pl.ds(width, width), 5)
    row_c = [
        pltpu.make_async_copy(rows.at[spots[k], 0], t.at[k], tsem.at[k]) for k in range(4)
    ]
    for k in range(4):
        for c in [row_c[k]] + gate_c[k] + up_c[k]:
            c.start()
    h = n // 2
    fetch = [
        pltpu.make_async_copy(rows.at[spots[k], 1, pl.ds(0, n)], u.at[k - 1], usem.at[k - 1])
        for k in (1, 2, 3)
    ]
    for c in fetch:
        c.start()
    slices = []
    for number, (k, lo, size, target) in enumerate(
        [(1, 0, n, to_l), (2, 0, n, to_r), (3, 0, h, to_oa), (3, h, h, to_ob)]
    ):
        for kind, source in enumerate((t.at[k], u.at[k - 1])):
            slices.append(
                pltpu.make_async_copy(
                    source.at[pl.ds(lo, size)], target.at[kind], ssem.at[number * 2 + kind]
                )
            )
    for k in range(4):
        for c in [row_c[k]] + gate_c[k] + up_c[k]:
            c.wait()
        term = dot(t[k], w[k])
        if k == 0:
            acc[...] = term
        else:
            acc[...] += term
    for c in fetch:
        c.wait()
    for c in slices:
        c.start()
    pre_gate, pre_up = acc[:, :width], acc[:, width:]
    s = jax.nn.sigmoid(pre_gate)
    act = pre_gate * s
    hid[...] = (act * pre_up).astype(BF)
    silu[...] = act
    slope[...] = pre_up * (s * (1.0 + pre_gate * (1.0 - s)))
    for c in slices:
        c.wait()


def hand_out(value, k, spot, o, own, sib, sem):
    n = own.shape[1]
    o[k] = value.astype(BF)
    copies = [
        pltpu.make_async_copy(o.at[k, pl.ds(i * n, n)], target.at[spot], sem.at[k * 2 + i])
        for i, target in enumerate((own, sib))
    ]
    for c in copies:
        c.start()
    return copies


def down_kernel(x, hid, slope, silu, rows, *refs):
    down_parts = refs[0:5]
    own, sib, grads = refs[5:8]
    wd, u, o, dsem, usem, osem = refs[8:]
    width = hid.shape[1]
    spots = [lax.rem(x[0] + s, 4) for s in SHIFTS]
    down_c = gather_copies(down_parts, wd, dsem, pl.ds(0, u.shape[2]), 0)
    row_c = [pltpu.make_async_copy(rows.at[spots[k], 1], u.at[k], usem.at[k]) for k in range(4)]
    for k in range(4):
        for c in [row_c[k]] + down_c[k]:
            c.start()
    sent = []
    back = jnp.zeros(hid.shape, F32)
    for k in range(4):
        for c in [row_c[k]] + down_c[k]:
            c.wait()
        sent += hand_out(dot(hid[...], wd[k]), k, spots[k], o, own, sib, osem)
        back = back + dot_t(u[k], wd[k])
    grads[:, 0:width] = hid[...]
    grads[:, width : 2 * width] = (back * slope[...]).astype(BF)
    grads[:, 2 * width :] = (back * silu[...]).astype(BF)
    for c in sent:
        c.wait()


def input_kernel(x, grads, *refs):
    gate_parts, up_parts = refs[0:5], refs[5:10]
    own, sib = refs[10:12]
    w, o, sem, osem = refs[12:]
    width = w.shape[2] // 2
    gate_c = gather_copies(gate_parts, w, sem, pl.ds(0, width), 0)
    up_c = gather_copies(up_parts, w, sem, pl.ds(width, width), 5)
    for k in range(4):
        for c in gate_c[k] + up_c[k]:
            c.start()
    sent = []
    for k in range(4):
        for c in gate_c[k] + up_c[k]:
            c.wait()
        spot = lax.rem(x[0] + SHIFTS[k], 4)
        sent += hand_out(dot_t(grads[:, width:], w[k]), k, spot, o, own, sib, osem)
    for c in sent:
        c.wait()


def weight_kernel(x, rows, *refs):
    mine, theirs = refs[0:4], refs[4:8]
    parts = refs[8:13]
    d_gate, d_up, d_down = refs[13:16]
    t, g, tsem, gsem = refs[16:]
    n = rows.shape[2] // 2
    h = n // 2
    width = d_gate.shape[1]
    copies = [pltpu.make_async_copy(rows.at[x[0]], t.at[:, pl.ds(0, 2 * n)], tsem.at[8])]
    for number, group in enumerate((mine, theirs)):
        base = number * n
        spots = [
            (1, base, n),
            (2, base, n),
            (3, base, h),
            (3, base + h, h),
        ]
        for i, (piece, (k, start, size)) in enumerate(zip(group, spots)):
            copies.append(
                pltpu.make_async_copy(
                    piece, t.at[:, pl.ds(k * 2 * n + start, size)], tsem.at[number * 4 + i]
                )
            )
    spots = [(0, 2 * n), (2 * n, 2 * n), (4 * n, 2 * n), (6 * n, n), (7 * n, n)]
    for i, (piece, (start, size)) in enumerate(zip(parts, spots)):
        copies.append(pltpu.make_async_copy(piece, g.at[pl.ds(start, size)], gsem.at[i]))
    for c in copies:
        c.start()
    for c in copies:
        c.wait()
    both = tdot(t[0], g[:, width:]).astype(BF)
    d_gate[...] = both[:, :width]
    d_up[...] = both[:, width:]
    d_down[...] = tdot(g[:, :width], t[1]).astype(BF)


def vmem():
    return pl.BlockSpec(memory_space=pltpu.VMEM)


def hbm():
    return pl.BlockSpec(memory_space=pl.ANY)


def smem():
    return pl.BlockSpec(memory_space=pltpu.SMEM)


def call(kernel, outs, ins, in_specs, out_specs, scratch=(), grid=(), aliases=None, flops=0, name=None):
    size = flops // 512
    return pl.pallas_call(
        kernel,
        out_shape=outs,
        grid=grid,
        input_output_aliases=aliases or {},
        in_specs=in_specs,
        out_specs=out_specs,
        scratch_shapes=list(scratch),
        compiler_params=pltpu.CompilerParams(vmem_limit_bytes=LIMIT),
        cost_estimate=pl.CostEstimate(flops=flops, bytes_accessed=size, transcendentals=0),
        name=name,
    )(*ins)


def shape(*dims, dtype=BF):
    return jax.ShapeDtypeStruct(dims, dtype)


def shift(v, k):
    n = lax.axis_size("dp")
    return lax.ppermute(v, "dp", [(i, (i + k) % n) for i in range(n)])


def sibling(v):
    return lax.ppermute(v, "expert", [(i, i ^ 1) for i in range(lax.axis_size("expert"))])


def near(v):
    return (v, shift(v, 1), shift(v, -1))


def halves(parts):
    half = parts[0].shape[0] // 2
    return parts + (parts[1][:half], parts[2][half:])


def far(parts):
    return parts[:3] + (shift(parts[3], 1), shift(parts[4], -1))


def ring(v):
    return far(halves(near(v)))


def exchange(v):
    devices = lax.axis_size("expert")
    groups = [[2 * i + c for i in range(devices // 2)] for c in range(2)]
    cut = v.reshape(devices // 2, 8, v.shape[1])
    cut = lax.all_to_all(
        cut, "expert", split_axis=0, concat_axis=0, axis_index_groups=groups, tiled=True
    )
    return cut.reshape(v.shape)


def body(tokens, expert_ids, gate_values, w_gate, w_up, w_down, cotangent):
    experts = lax.axis_size("expert") // 2
    micro, toks, features = tokens.shape
    q = features // 4
    width = w_gate.shape[1]
    wire = experts * 8
    n = experts * 6
    x = lax.axis_index("dp").astype(jnp.int32).reshape(1)
    gate_near, up_near, down_near = near(w_gate), near(w_up), near(w_down)

    ids = jnp.transpose(expert_ids, (0, 2, 1))
    gates = jnp.transpose(gate_values, (0, 2, 1))
    packed, place = call(
        pack_kernel,
        [shape(wire, 6 * q), shape(1, micro * toks, dtype=jnp.int32)],
        [ids, gates, tokens.reshape(-1, features), cotangent.reshape(-1, features)],
        [vmem()] * 4,
        [vmem()] * 2,
        flops=2 * 6 * wire * wire * q,
        name="pack",
    )
    arrived = exchange(packed)
    arrived, gate_parts, up_near, down_near = lax.optimization_barrier(
        (arrived, far(halves(gate_near)), halves(up_near), halves(down_near))
    )
    up_parts, down_parts = far(up_near), far(down_near)
    arrived_sib = sibling(arrived)
    rows = call(
        compact_kernel,
        [shape(4, 2, 2 * n, q)],
        [arrived, arrived_sib],
        [pl.BlockSpec((wire, 3 * q), lambda kind: (0, kind))] * 2,
        [pl.BlockSpec((4, 1, 2 * n, q), lambda kind: (0, kind, 0, 0))],
        grid=(2,),
        name="compact",
    )[0]
    dma = pltpu.SemaphoreType.DMA
    hid, slope, silu, to_l, to_r, to_oa, to_ob = call(
        forward_kernel,
        [shape(2 * n, width)]
        + [shape(2 * n, width, dtype=F32)] * 2
        + [shape(2, n, q)] * 2
        + [shape(2, n // 2, q)] * 2,
        [x, rows, *gate_parts, *up_parts],
        [smem()] + [hbm()] * 11,
        [vmem()] * 3 + [hbm()] * 4,
        scratch=[
            pltpu.VMEM((4, q, 2 * width), BF),
            pltpu.VMEM((4, 2 * n, q), BF),
            pltpu.VMEM((3, n, q), BF),
            pltpu.VMEM((2 * n, 2 * width), F32),
            dma((10,)),
            dma((4,)),
            dma((3,)),
            dma((8,)),
        ],
        flops=32 * 2 * n * features * width,
        name="forward",
    )
    to_l, to_r, to_oa, to_ob, down_parts = lax.optimization_barrier(
        (to_l, to_r, to_oa, to_ob, down_parts)
    )
    from_r, from_l = shift(to_l, -1), shift(to_r, 1)
    half_a, half_b = shift(to_oa, 1), shift(to_ob, -1)

    own_out, sib_out, grads = call(
        down_kernel,
        [shape(4, n, q)] * 2 + [shape(2 * n, 3 * width)],
        [x, hid, slope, silu, rows, *down_parts],
        [smem()] + [vmem()] * 3 + [hbm()] * 6,
        [hbm()] * 2 + [vmem()],
        scratch=[
            pltpu.VMEM((4, width, q), BF),
            pltpu.VMEM((4, 2 * n, q), BF),
            pltpu.VMEM((4, 2 * n, q), BF),
            dma((5,)),
            dma((4,)),
            dma((8,)),
        ],
        name="down",
    )
    own_grad, sib_grad = call(
        input_kernel,
        [shape(4, n, q)] * 2,
        [x, grads, *gate_parts, *up_parts],
        [smem()] + [vmem()] + [hbm()] * 10,
        [hbm()] * 2,
        scratch=[
            pltpu.VMEM((4, q, 2 * width), BF),
            pltpu.VMEM((4, 2 * n, q), BF),
            dma((10,)),
            dma((8,)),
        ],
        name="inputs",
    )
    parts = [
        pl.BlockSpec((1, n, q), lambda j: (j, 0, 0)),
        pl.BlockSpec((1, n, q), lambda j: (3, 0, 0)),
    ] * 2
    out_sib = sibling(sib_out)
    sib_grad, from_l, from_r = lax.optimization_barrier((sib_grad, from_l, from_r))
    grad_sib = sibling(sib_grad)
    sent = call(
        expand_kernel,
        [shape(wire, 6 * q)],
        [own_out, own_out, out_sib, out_sib],
        parts,
        [pl.BlockSpec((wire, q), lambda j: (0, j))],
        grid=(3,),
        name="expand_out",
    )[0]
    sent = call(
        lambda _, *refs: expand_kernel(*refs),
        [shape(wire, 6 * q)],
        [sent, own_grad, own_grad, grad_sib, grad_sib],
        [hbm()] + parts,
        [pl.BlockSpec((wire, q), lambda j: (0, 3 + j))],
        grid=(3,),
        aliases={0: 0},
        name="expand_grad",
    )[0]
    sent, half_a, half_b = lax.optimization_barrier((sent, half_a, half_b))
    came = exchange(sent)

    from_oa, from_ob = shift(half_a, 1), shift(half_b, -1)
    grad_parts = ring(grads)
    mine = (from_l, from_r, from_oa, from_ob)
    theirs = tuple(sibling(v) for v in mine)
    d_gate, d_up, d_down = call(
        weight_kernel,
        [shape(q, width)] * 2 + [shape(width, q)],
        [x, rows, *mine, *theirs, *grad_parts],
        [smem()] + [hbm()] * 14,
        [vmem()] * 3,
        scratch=[
            pltpu.VMEM((2, 8 * n, q), BF),
            pltpu.VMEM((8 * n, 3 * width), BF),
            dma((9,)),
            dma((5,)),
        ],
        flops=6 * 8 * n * q * width,
        name="weights",
    )
    layer_out, tokens_grad = call(
        unpack_kernel,
        [shape(micro * toks, features)] * 2,
        [place, gates, came],
        [vmem()] * 3,
        [vmem()] * 2,
        flops=2 * 6 * wire * wire * q,
        name="unpack",
    )
    return (
        layer_out.reshape(tokens.shape),
        tokens_grad.reshape(tokens.shape),
        d_gate,
        d_up,
        d_down,
    )


def solution(mesh):
    rows = P(None, ("dp", "expert"), None)
    return jax.shard_map(
        body,
        mesh=mesh,
        in_specs=(rows, rows, rows, P("dp", "expert"), P("dp", "expert"), P("expert", "dp"), rows),
        out_specs=(rows, rows, P("dp", "expert"), P("dp", "expert"), P("expert", "dp")),
        check_vma=False,
    )
```

```python
import functools

import jax
import jax.numpy as jnp
from jax import lax
from jax.experimental import pallas as pl
from jax.experimental.pallas import tpu as pltpu
from jax.sharding import PartitionSpec as P

BF = jnp.bfloat16
F32 = jnp.float32
LIMIT = 63 * 1024 * 1024


def dot(a, b):
    return jnp.dot(a, b, preferred_element_type=F32)


def dot_t(a, b):
    return lax.dot_general(a, b, (((1,), (1,)), ((), ())), preferred_element_type=F32)


def tdot(a, b):
    return lax.dot_general(a, b, (((0,), (0,)), ((), ())), preferred_element_type=F32)


def onehot(cond):
    return jnp.where(cond, 1.0, 0.0).astype(BF)


def iota(shape, dim):
    return lax.broadcasted_iota(jnp.int32, shape, dim)


def as_column(row):
    n = row.shape[1]
    return jnp.sum(jnp.where(iota((n, n), 0) == iota((n, n), 1), row, 0), axis=1, keepdims=True)


def slot_matrices(place, rows):
    n = place.shape[1]
    at = iota((rows, n), 0)
    base = place // 8 * 8
    slot = place - base
    main = onehot(at == place)
    tail = base + 6 + slot % 2
    return [
        jnp.concatenate([main, onehot((at == tail) & (slot // 2 == j))], axis=1) for j in range(3)
    ]


def as_row(ref):
    return jnp.concatenate([ref[m] for m in range(ref.shape[0])], axis=1)


def pack_kernel(ids_ref, gate_ref, tokens, cot, out, place_out):
    ids, gate = as_row(ids_ref), as_row(gate_ref)
    n = ids.shape[1]
    half = n // 2
    q = tokens.shape[1] // 4
    earlier, later = iota((n, n), 0), iota((n, n), 1)
    same = (as_column(ids) == ids) & (earlier < later) & (earlier // half == later // half)
    rank = jnp.sum(jnp.where(same, 1, 0), axis=0, keepdims=True)
    place = ids * 8 + iota((1, n), 1) // half * 3 + rank
    place_out[...] = place
    choose = slot_matrices(place, out.shape[0])
    weight = as_column(gate)
    for kind in range(2):
        def part(j):
            rows = (tokens if kind == 0 else cot)[:, j * q : (j + 1) * q]
            return rows if kind == 0 else (weight * rows.astype(F32)).astype(BF)
        last = part(3)
        for j in range(3):
            both = jnp.concatenate([part(j), last], axis=0)
            lo = (kind * 3 + j) * q
            out[:, lo : lo + q] = dot(choose[j], both).astype(BF)


def unpack_kernel(place, gate, back, layer, grad):
    n = place.shape[1]
    q = layer.shape[1] // 4
    choose = slot_matrices(place[...], back.shape[0])
    weight = as_column(as_row(gate))
    for kind in range(2):
        def put(j, rows):
            if kind == 0:
                layer[:, j * q : (j + 1) * q] = (weight * rows.astype(BF).astype(F32)).astype(BF)
            else:
                grad[:, j * q : (j + 1) * q] = rows.astype(BF)
        last = jnp.zeros((n, q), F32)
        for j in range(3):
            lo = (kind * 3 + j) * q
            got = tdot(choose[j], back[:, lo : lo + q])
            put(j, got[:n])
            last = last + got[n:]
        put(3, last)


def wire_places(shape_, dim):
    r = iota(shape_, dim)
    base, slot = r // 6 * 8, r % 6
    return base + slot, base + 6 + slot % 2, slot // 2


def compact_kernel(own, sib, out):
    n = out.shape[2] // 2
    q = out.shape[3]
    p = iota((n, own.shape[0]), 1)
    row, tail, part = wire_places((n, 1), 0)
    main = onehot(p == row)
    choose = [
        jnp.concatenate([main, onehot(p == jnp.where(part == j, tail, -1))], axis=0)
        for j in range(3)
    ]
    for place, source in enumerate((own, sib)):
        last = jnp.zeros((n, q), F32)
        for j in range(3):
            got = dot(choose[j], source[:, j * q : (j + 1) * q])
            out[j, 0, place * n : (place + 1) * n] = got[:n].astype(BF)
            last = last + got[n:]
        out[3, 0, place * n : (place + 1) * n] = last.astype(BF)


def expand_kernel(own, own_last, sib, sib_last, out):
    n = own.shape[1]
    p = iota((out.shape[0], n), 0)
    row, tail, part = wire_places((1, n), 1)
    tail = jnp.where(part == pl.program_id(0), tail, -1)
    choose = jnp.concatenate([onehot(p == row), onehot(p == tail)], axis=1)

    def total(a, b):
        return (a[0].astype(F32) + b[0].astype(F32)).astype(BF)

    both = jnp.concatenate([total(own, sib), total(own_last, sib_last)], axis=0)
    out[...] = dot(choose, both).astype(BF)


def gather_copies(pieces, buf, sem, lanes, first):
    half = pieces[3].shape[0]
    views = [
        (buf.at[0, :, lanes], 0),
        (buf.at[1, :, lanes], 1),
        (buf.at[2, :, lanes], 2),
        (buf.at[3, pl.ds(0, half), lanes], 3),
        (buf.at[3, pl.ds(half, half), lanes], 3),
    ]
    return [
        [
            pltpu.make_async_copy(piece, view, sem.at[first + n])
            for n, (piece, (view, at)) in enumerate(zip(pieces, views))
            if at == k
        ]
        for k in range(4)
    ]


SHIFTS = (0, 3, 1, 2)


def forward_kernel(x, rows, *refs):
    gate_parts, up_parts = refs[0:5], refs[5:10]
    hid, slope, silu, to_l, to_r, to_oa, to_ob = refs[10:17]
    w, t, u, acc, sem, tsem, usem, ssem = refs[17:]
    me = x[0]
    n = rows.shape[2] // 2
    spots = [lax.rem(me + s, 4) for s in SHIFTS]
    width = hid.shape[1]
    gate_c = gather_copies(gate_parts, w, sem, pl.ds(0, width), 0)
    up_c = gather_copies(up_parts, w, sem, pl.ds(width, width), 5)
    row_c = [
        pltpu.make_async_copy(rows.at[spots[k], 0], t.at[k], tsem.at[k]) for k in range(4)
    ]
    for k in range(4):
        for c in [row_c[k]] + gate_c[k] + up_c[k]:
            c.start()
    h = n // 2
    fetch = [
        pltpu.make_async_copy(rows.at[spots[k], 1, pl.ds(0, n)], u.at[k - 1], usem.at[k - 1])
        for k in (1, 2, 3)
    ]
    for c in fetch:
        c.start()
    slices = []
    for number, (k, lo, size, target) in enumerate(
        [(1, 0, n, to_l), (2, 0, n, to_r), (3, 0, h, to_oa), (3, h, h, to_ob)]
    ):
        for kind, source in enumerate((t.at[k], u.at[k - 1])):
            slices.append(
                pltpu.make_async_copy(
                    source.at[pl.ds(lo, size)], target.at[kind], ssem.at[number * 2 + kind]
                )
            )
    for k in range(4):
        for c in [row_c[k]] + gate_c[k] + up_c[k]:
            c.wait()
        term = dot(t[k], w[k])
        if k == 0:
            acc[...] = term
        else:
            acc[...] += term
    for c in fetch:
        c.wait()
    for c in slices:
        c.start()
    pre_gate, pre_up = acc[:, :width], acc[:, width:]
    s = jax.nn.sigmoid(pre_gate)
    act = pre_gate * s
    hid[...] = (act * pre_up).astype(BF)
    silu[...] = act
    slope[...] = pre_up * (s * (1.0 + pre_gate * (1.0 - s)))
    for c in slices:
        c.wait()


def hand_out(value, k, spot, o, own, sib, sem):
    n = own.shape[1]
    o[k] = value.astype(BF)
    copies = [
        pltpu.make_async_copy(o.at[k, pl.ds(i * n, n)], target.at[spot], sem.at[k * 2 + i])
        for i, target in enumerate((own, sib))
    ]
    for c in copies:
        c.start()
    return copies


def down_kernel(x, hid, slope, silu, rows, *refs):
    down_parts = refs[0:5]
    own, sib, grads = refs[5:8]
    wd, u, o, dsem, usem, osem = refs[8:]
    width = hid.shape[1]
    spots = [lax.rem(x[0] + s, 4) for s in SHIFTS]
    down_c = gather_copies(down_parts, wd, dsem, pl.ds(0, u.shape[2]), 0)
    row_c = [pltpu.make_async_copy(rows.at[spots[k], 1], u.at[k], usem.at[k]) for k in range(4)]
    for k in range(4):
        for c in [row_c[k]] + down_c[k]:
            c.start()
    sent = []
    back = jnp.zeros(hid.shape, F32)
    for k in range(4):
        for c in [row_c[k]] + down_c[k]:
            c.wait()
        sent += hand_out(dot(hid[...], wd[k]), k, spots[k], o, own, sib, osem)
        back = back + dot_t(u[k], wd[k])
    grads[:, 0:width] = hid[...]
    grads[:, width : 2 * width] = (back * slope[...]).astype(BF)
    grads[:, 2 * width :] = (back * silu[...]).astype(BF)
    for c in sent:
        c.wait()


def input_kernel(x, grads, *refs):
    gate_parts, up_parts = refs[0:5], refs[5:10]
    own, sib = refs[10:12]
    w, o, sem, osem = refs[12:]
    width = w.shape[2] // 2
    gate_c = gather_copies(gate_parts, w, sem, pl.ds(0, width), 0)
    up_c = gather_copies(up_parts, w, sem, pl.ds(width, width), 5)
    for k in range(4):
        for c in gate_c[k] + up_c[k]:
            c.start()
    sent = []
    for k in range(4):
        for c in gate_c[k] + up_c[k]:
            c.wait()
        spot = lax.rem(x[0] + SHIFTS[k], 4)
        sent += hand_out(dot_t(grads[:, width:], w[k]), k, spot, o, own, sib, osem)
    for c in sent:
        c.wait()


def weight_kernel(x, rows, *refs):
    mine, theirs = refs[0:4], refs[4:8]
    parts = refs[8:13]
    d_gate, d_up, d_down = refs[13:16]
    t, g, tsem, gsem = refs[16:]
    n = rows.shape[2] // 2
    h = n // 2
    width = d_gate.shape[1]
    copies = [pltpu.make_async_copy(rows.at[x[0]], t.at[:, pl.ds(0, 2 * n)], tsem.at[8])]
    for number, group in enumerate((mine, theirs)):
        base = number * n
        spots = [
            (1, base, n),
            (2, base, n),
            (3, base, h),
            (3, base + h, h),
        ]
        for i, (piece, (k, start, size)) in enumerate(zip(group, spots)):
            copies.append(
                pltpu.make_async_copy(
                    piece, t.at[:, pl.ds(k * 2 * n + start, size)], tsem.at[number * 4 + i]
                )
            )
    spots = [(0, 2 * n), (2 * n, 2 * n), (4 * n, 2 * n), (6 * n, n), (7 * n, n)]
    for i, (piece, (start, size)) in enumerate(zip(parts, spots)):
        copies.append(pltpu.make_async_copy(piece, g.at[pl.ds(start, size)], gsem.at[i]))
    for c in copies:
        c.start()
    for c in copies:
        c.wait()
    both = tdot(t[0], g[:, width:]).astype(BF)
    d_gate[...] = both[:, :width]
    d_up[...] = both[:, width:]
    d_down[...] = tdot(g[:, :width], t[1]).astype(BF)


def vmem():
    return pl.BlockSpec(memory_space=pltpu.VMEM)


def hbm():
    return pl.BlockSpec(memory_space=pl.ANY)


def smem():
    return pl.BlockSpec(memory_space=pltpu.SMEM)


def call(kernel, outs, ins, in_specs, out_specs, scratch=(), grid=(), aliases=None, flops=0, name=None):
    size = flops // 512
    return pl.pallas_call(
        kernel,
        out_shape=outs,
        grid=grid,
        input_output_aliases=aliases or {},
        in_specs=in_specs,
        out_specs=out_specs,
        scratch_shapes=list(scratch),
        compiler_params=pltpu.CompilerParams(vmem_limit_bytes=LIMIT),
        cost_estimate=pl.CostEstimate(flops=flops, bytes_accessed=size, transcendentals=0),
        name=name,
    )(*ins)


def shape(*dims, dtype=BF):
    return jax.ShapeDtypeStruct(dims, dtype)


def shift(v, k):
    n = lax.axis_size("dp")
    return lax.ppermute(v, "dp", [(i, (i + k) % n) for i in range(n)])


def sibling(v):
    return lax.ppermute(v, "expert", [(i, i ^ 1) for i in range(lax.axis_size("expert"))])


def near(v):
    return (v, shift(v, 1), shift(v, -1))


def halves(parts):
    half = parts[0].shape[0] // 2
    return parts + (parts[1][:half], parts[2][half:])


def far(parts):
    return parts[:3] + (shift(parts[3], 1), shift(parts[4], -1))


def ring(v):
    return far(halves(near(v)))


def exchange(v):
    devices = lax.axis_size("expert")
    groups = [[2 * i + c for i in range(devices // 2)] for c in range(2)]
    cut = v.reshape(devices // 2, 8, v.shape[1])
    cut = lax.all_to_all(
        cut, "expert", split_axis=0, concat_axis=0, axis_index_groups=groups, tiled=True
    )
    return cut.reshape(v.shape)


def body(tokens, expert_ids, gate_values, w_gate, w_up, w_down, cotangent):
    experts = lax.axis_size("expert") // 2
    micro, toks, features = tokens.shape
    q = features // 4
    width = w_gate.shape[1]
    wire = experts * 8
    n = experts * 6
    x = lax.axis_index("dp").astype(jnp.int32).reshape(1)
    gate_near, up_near, down_near = near(w_gate), near(w_up), near(w_down)

    ids = jnp.transpose(expert_ids, (0, 2, 1))
    gates = jnp.transpose(gate_values, (0, 2, 1))
    packed, place = call(
        pack_kernel,
        [shape(wire, 6 * q), shape(1, micro * toks, dtype=jnp.int32)],
        [ids, gates, tokens.reshape(-1, features), cotangent.reshape(-1, features)],
        [vmem()] * 4,
        [vmem()] * 2,
        flops=2 * 6 * wire * wire * q,
        name="pack",
    )
    arrived = exchange(packed)
    arrived, gate_near, up_near, down_near = lax.optimization_barrier(
        (arrived, halves(gate_near), halves(up_near), halves(down_near))
    )
    gate_parts, up_parts, down_parts = far(gate_near), far(up_near), far(down_near)
    arrived_sib = sibling(arrived)
    rows = call(
        compact_kernel,
        [shape(4, 2, 2 * n, q)],
        [arrived, arrived_sib],
        [pl.BlockSpec((wire, 3 * q), lambda kind: (0, kind))] * 2,
        [pl.BlockSpec((4, 1, 2 * n, q), lambda kind: (0, kind, 0, 0))],
        grid=(2,),
        name="compact",
    )[0]
    dma = pltpu.SemaphoreType.DMA
    hid, slope, silu, to_l, to_r, to_oa, to_ob = call(
        forward_kernel,
        [shape(2 * n, width)]
        + [shape(2 * n, width, dtype=F32)] * 2
        + [shape(2, n, q)] * 2
        + [shape(2, n // 2, q)] * 2,
        [x, rows, *gate_parts, *up_parts],
        [smem()] + [hbm()] * 11,
        [vmem()] * 3 + [hbm()] * 4,
        scratch=[
            pltpu.VMEM((4, q, 2 * width), BF),
            pltpu.VMEM((4, 2 * n, q), BF),
            pltpu.VMEM((3, n, q), BF),
            pltpu.VMEM((2 * n, 2 * width), F32),
            dma((10,)),
            dma((4,)),
            dma((3,)),
            dma((8,)),
        ],
        flops=32 * 2 * n * features * width,
        name="forward",
    )
    to_l, to_r, to_oa, to_ob, down_parts = lax.optimization_barrier(
        (to_l, to_r, to_oa, to_ob, down_parts)
    )
    from_r, from_l = shift(to_l, -1), shift(to_r, 1)
    half_a, half_b = shift(to_oa, 1), shift(to_ob, -1)

    own_out, sib_out, grads = call(
        down_kernel,
        [shape(4, n, q)] * 2 + [shape(2 * n, 3 * width)],
        [x, hid, slope, silu, rows, *down_parts],
        [smem()] + [vmem()] * 3 + [hbm()] * 6,
        [hbm()] * 2 + [vmem()],
        scratch=[
            pltpu.VMEM((4, width, q), BF),
            pltpu.VMEM((4, 2 * n, q), BF),
            pltpu.VMEM((4, 2 * n, q), BF),
            dma((5,)),
            dma((4,)),
            dma((8,)),
        ],
        name="down",
    )
    own_grad, sib_grad = call(
        input_kernel,
        [shape(4, n, q)] * 2,
        [x, grads, *gate_parts, *up_parts],
        [smem()] + [vmem()] + [hbm()] * 10,
        [hbm()] * 2,
        scratch=[
            pltpu.VMEM((4, q, 2 * width), BF),
            pltpu.VMEM((4, 2 * n, q), BF),
            dma((10,)),
            dma((8,)),
        ],
        name="inputs",
    )
    parts = [
        pl.BlockSpec((1, n, q), lambda j: (j, 0, 0)),
        pl.BlockSpec((1, n, q), lambda j: (3, 0, 0)),
    ] * 2
    out_sib = sibling(sib_out)
    sib_grad, from_l, from_r = lax.optimization_barrier((sib_grad, from_l, from_r))
    grad_sib = sibling(sib_grad)
    sent = call(
        expand_kernel,
        [shape(wire, 6 * q)],
        [own_out, own_out, out_sib, out_sib],
        parts,
        [pl.BlockSpec((wire, q), lambda j: (0, j))],
        grid=(3,),
        name="expand_out",
    )[0]
    sent = call(
        lambda _, *refs: expand_kernel(*refs),
        [shape(wire, 6 * q)],
        [sent, own_grad, own_grad, grad_sib, grad_sib],
        [hbm()] + parts,
        [pl.BlockSpec((wire, q), lambda j: (0, 3 + j))],
        grid=(3,),
        aliases={0: 0},
        name="expand_grad",
    )[0]
    sent, half_a, half_b = lax.optimization_barrier((sent, half_a, half_b))
    came = exchange(sent)

    from_oa, from_ob = shift(half_a, 1), shift(half_b, -1)
    grad_parts = ring(grads)
    mine = (from_l, from_r, from_oa, from_ob)
    theirs = tuple(sibling(v) for v in mine)
    d_gate, d_up, d_down = call(
        weight_kernel,
        [shape(q, width)] * 2 + [shape(width, q)],
        [x, rows, *mine, *theirs, *grad_parts],
        [smem()] + [hbm()] * 14,
        [vmem()] * 3,
        scratch=[
            pltpu.VMEM((2, 8 * n, q), BF),
            pltpu.VMEM((8 * n, 3 * width), BF),
            dma((9,)),
            dma((5,)),
        ],
        flops=6 * 8 * n * q * width,
        name="weights",
    )
    layer_out, tokens_grad = call(
        unpack_kernel,
        [shape(micro * toks, features)] * 2,
        [place, gates, came],
        [vmem()] * 3,
        [vmem()] * 2,
        flops=2 * 6 * wire * wire * q,
        name="unpack",
    )
    return (
        layer_out.reshape(tokens.shape),
        tokens_grad.reshape(tokens.shape),
        d_gate,
        d_up,
        d_down,
    )


def solution(mesh):
    rows = P(None, ("dp", "expert"), None)
    return jax.shard_map(
        body,
        mesh=mesh,
        in_specs=(rows, rows, rows, P("dp", "expert"), P("dp", "expert"), P("expert", "dp"), rows),
        out_specs=(rows, rows, P("dp", "expert"), P("dp", "expert"), P("expert", "dp")),
        check_vma=False,
    )
```

```python
import functools

import jax
import jax.numpy as jnp
from jax import lax
from jax.experimental import pallas as pl
from jax.experimental.pallas import tpu as pltpu
from jax.sharding import PartitionSpec as P

BF = jnp.bfloat16
F32 = jnp.float32
LIMIT = 63 * 1024 * 1024


def dot(a, b):
    return jnp.dot(a, b, preferred_element_type=F32)


def dot_t(a, b):
    return lax.dot_general(a, b, (((1,), (1,)), ((), ())), preferred_element_type=F32)


def tdot(a, b):
    return lax.dot_general(a, b, (((0,), (0,)), ((), ())), preferred_element_type=F32)


def onehot(cond):
    return jnp.where(cond, 1.0, 0.0).astype(BF)


def iota(shape, dim):
    return lax.broadcasted_iota(jnp.int32, shape, dim)


def as_column(row):
    n = row.shape[1]
    return jnp.sum(jnp.where(iota((n, n), 0) == iota((n, n), 1), row, 0), axis=1, keepdims=True)


def slot_matrices(place, rows):
    n = place.shape[1]
    at = iota((rows, n), 0)
    base = place // 8 * 8
    slot = place - base
    main = onehot(at == place)
    tail = base + 6 + slot % 2
    return [
        jnp.concatenate([main, onehot((at == tail) & (slot // 2 == j))], axis=1) for j in range(3)
    ]


def as_row(ref):
    return jnp.concatenate([ref[m] for m in range(ref.shape[0])], axis=1)


def pack_kernel(ids_ref, gate_ref, tokens, cot, out, place_out):
    ids, gate = as_row(ids_ref), as_row(gate_ref)
    n = ids.shape[1]
    half = n // 2
    q = tokens.shape[1] // 4
    earlier, later = iota((n, n), 0), iota((n, n), 1)
    same = (as_column(ids) == ids) & (earlier < later) & (earlier // half == later // half)
    rank = jnp.sum(jnp.where(same, 1, 0), axis=0, keepdims=True)
    place = ids * 8 + iota((1, n), 1) // half * 3 + rank
    place_out[...] = place
    choose = slot_matrices(place, out.shape[0])
    weight = as_column(gate)
    for kind in range(2):
        def part(j):
            rows = (tokens if kind == 0 else cot)[:, j * q : (j + 1) * q]
            return rows if kind == 0 else (weight * rows.astype(F32)).astype(BF)
        last = part(3)
        for j in range(3):
            both = jnp.concatenate([part(j), last], axis=0)
            lo = (kind * 3 + j) * q
            out[:, lo : lo + q] = dot(choose[j], both).astype(BF)


def unpack_kernel(place, gate, back, layer, grad):
    n = place.shape[1]
    q = layer.shape[1] // 4
    choose = slot_matrices(place[...], back.shape[0])
    weight = as_column(as_row(gate))
    for kind in range(2):
        def put(j, rows):
            if kind == 0:
                layer[:, j * q : (j + 1) * q] = (weight * rows.astype(BF).astype(F32)).astype(BF)
            else:
                grad[:, j * q : (j + 1) * q] = rows.astype(BF)
        last = jnp.zeros((n, q), F32)
        for j in range(3):
            lo = (kind * 3 + j) * q
            got = tdot(choose[j], back[:, lo : lo + q])
            put(j, got[:n])
            last = last + got[n:]
        put(3, last)


def wire_places(shape_, dim):
    r = iota(shape_, dim)
    base, slot = r // 6 * 8, r % 6
    return base + slot, base + 6 + slot % 2, slot // 2


def compact_kernel(own, sib, out):
    n = out.shape[2] // 2
    q = out.shape[3]
    p = iota((n, own.shape[0]), 1)
    row, tail, part = wire_places((n, 1), 0)
    main = onehot(p == row)
    choose = [
        jnp.concatenate([main, onehot(p == jnp.where(part == j, tail, -1))], axis=0)
        for j in range(3)
    ]
    for place, source in enumerate((own, sib)):
        last = jnp.zeros((n, q), F32)
        for j in range(3):
            got = dot(choose[j], source[:, j * q : (j + 1) * q])
            out[j, 0, place * n : (place + 1) * n] = got[:n].astype(BF)
            last = last + got[n:]
        out[3, 0, place * n : (place + 1) * n] = last.astype(BF)


def expand_kernel(own, own_last, sib, sib_last, out):
    n = own.shape[1]
    p = iota((out.shape[0], n), 0)
    row, tail, part = wire_places((1, n), 1)
    tail = jnp.where(part == pl.program_id(0), tail, -1)
    choose = jnp.concatenate([onehot(p == row), onehot(p == tail)], axis=1)

    def total(a, b):
        return (a[0].astype(F32) + b[0].astype(F32)).astype(BF)

    both = jnp.concatenate([total(own, sib), total(own_last, sib_last)], axis=0)
    out[...] = dot(choose, both).astype(BF)


def gather_copies(pieces, buf, sem, lanes, first):
    half = pieces[3].shape[0]
    views = [
        (buf.at[0, :, lanes], 0),
        (buf.at[1, :, lanes], 1),
        (buf.at[2, :, lanes], 2),
        (buf.at[3, pl.ds(0, half), lanes], 3),
        (buf.at[3, pl.ds(half, half), lanes], 3),
    ]
    return [
        [
            pltpu.make_async_copy(piece, view, sem.at[first + n])
            for n, (piece, (view, at)) in enumerate(zip(pieces, views))
            if at == k
        ]
        for k in range(4)
    ]


SHIFTS = (0, 3, 1, 2)


def forward_kernel(x, rows, *refs):
    gate_parts, up_parts = refs[0:5], refs[5:10]
    hid, slope, silu, to_l, to_r, to_oa, to_ob = refs[10:17]
    w, t, u, acc, sem, tsem, usem, ssem = refs[17:]
    me = x[0]
    n = rows.shape[2] // 2
    spots = [lax.rem(me + s, 4) for s in SHIFTS]
    width = hid.shape[1]
    gate_c = gather_copies(gate_parts, w, sem, pl.ds(0, width), 0)
    up_c = gather_copies(up_parts, w, sem, pl.ds(width, width), 5)
    row_c = [
        pltpu.make_async_copy(rows.at[spots[k], 0], t.at[k], tsem.at[k]) for k in range(4)
    ]
    for k in range(4):
        for c in [row_c[k]] + gate_c[k] + up_c[k]:
            c.start()
    h = n // 2
    fetch = [
        pltpu.make_async_copy(rows.at[spots[k], 1, pl.ds(0, n)], u.at[k - 1], usem.at[k - 1])
        for k in (1, 2, 3)
    ]
    for c in fetch:
        c.start()
    slices = []
    for number, (k, lo, size, target) in enumerate(
        [(1, 0, n, to_l), (2, 0, n, to_r), (3, 0, h, to_oa), (3, h, h, to_ob)]
    ):
        for kind, source in enumerate((t.at[k], u.at[k - 1])):
            slices.append(
                pltpu.make_async_copy(
                    source.at[pl.ds(lo, size)], target.at[kind], ssem.at[number * 2 + kind]
                )
            )
    for k in range(4):
        for c in [row_c[k]] + gate_c[k] + up_c[k]:
            c.wait()
        term = dot(t[k], w[k])
        if k == 0:
            acc[...] = term
        else:
            acc[...] += term
    for c in fetch:
        c.wait()
    for c in slices:
        c.start()
    pre_gate, pre_up = acc[:, :width], acc[:, width:]
    s = jax.nn.sigmoid(pre_gate)
    act = pre_gate * s
    hid[...] = (act * pre_up).astype(BF)
    silu[...] = act
    slope[...] = pre_up * (s * (1.0 + pre_gate * (1.0 - s)))
    for c in slices:
        c.wait()


def hand_out(value, k, spot, o, own, sib, sem):
    n = own.shape[1]
    o[k] = value.astype(BF)
    copies = [
        pltpu.make_async_copy(o.at[k, pl.ds(i * n, n)], target.at[spot], sem.at[k * 2 + i])
        for i, target in enumerate((own, sib))
    ]
    for c in copies:
        c.start()
    return copies


def down_kernel(x, hid, slope, silu, rows, *refs):
    down_parts = refs[0:5]
    own, sib, grads = refs[5:8]
    wd, u, o, dsem, usem, osem = refs[8:]
    width = hid.shape[1]
    spots = [lax.rem(x[0] + s, 4) for s in SHIFTS]
    down_c = gather_copies(down_parts, wd, dsem, pl.ds(0, u.shape[2]), 0)
    row_c = [pltpu.make_async_copy(rows.at[spots[k], 1], u.at[k], usem.at[k]) for k in range(4)]
    for k in range(4):
        for c in [row_c[k]] + down_c[k]:
            c.start()
    sent = []
    back = jnp.zeros(hid.shape, F32)
    for k in range(4):
        for c in [row_c[k]] + down_c[k]:
            c.wait()
        sent += hand_out(dot(hid[...], wd[k]), k, spots[k], o, own, sib, osem)
        back = back + dot_t(u[k], wd[k])
    grads[:, 0:width] = hid[...]
    grads[:, width : 2 * width] = (back * slope[...]).astype(BF)
    grads[:, 2 * width :] = (back * silu[...]).astype(BF)
    for c in sent:
        c.wait()


def input_kernel(x, grads, *refs):
    gate_parts, up_parts = refs[0:5], refs[5:10]
    own, sib = refs[10:12]
    w, o, sem, osem = refs[12:]
    width = w.shape[2] // 2
    gate_c = gather_copies(gate_parts, w, sem, pl.ds(0, width), 0)
    up_c = gather_copies(up_parts, w, sem, pl.ds(width, width), 5)
    for k in range(4):
        for c in gate_c[k] + up_c[k]:
            c.start()
    sent = []
    for k in range(4):
        for c in gate_c[k] + up_c[k]:
            c.wait()
        spot = lax.rem(x[0] + SHIFTS[k], 4)
        sent += hand_out(dot_t(grads[:, width:], w[k]), k, spot, o, own, sib, osem)
    for c in sent:
        c.wait()


def weight_kernel(x, rows, *refs):
    mine, theirs = refs[0:4], refs[4:8]
    parts = refs[8:13]
    d_gate, d_up, d_down = refs[13:16]
    t, g, tsem, gsem = refs[16:]
    n = rows.shape[2] // 2
    h = n // 2
    width = d_gate.shape[1]
    copies = [pltpu.make_async_copy(rows.at[x[0]], t.at[:, pl.ds(0, 2 * n)], tsem.at[8])]
    for number, group in enumerate((mine, theirs)):
        base = number * n
        spots = [
            (1, base, n),
            (2, base, n),
            (3, base, h),
            (3, base + h, h),
        ]
        for i, (piece, (k, start, size)) in enumerate(zip(group, spots)):
            copies.append(
                pltpu.make_async_copy(
                    piece, t.at[:, pl.ds(k * 2 * n + start, size)], tsem.at[number * 4 + i]
                )
            )
    spots = [(0, 2 * n), (2 * n, 2 * n), (4 * n, 2 * n), (6 * n, n), (7 * n, n)]
    for i, (piece, (start, size)) in enumerate(zip(parts, spots)):
        copies.append(pltpu.make_async_copy(piece, g.at[pl.ds(start, size)], gsem.at[i]))
    for c in copies:
        c.start()
    for c in copies:
        c.wait()
    both = tdot(t[0], g[:, width:]).astype(BF)
    d_gate[...] = both[:, :width]
    d_up[...] = both[:, width:]
    d_down[...] = tdot(g[:, :width], t[1]).astype(BF)


def vmem():
    return pl.BlockSpec(memory_space=pltpu.VMEM)


def hbm():
    return pl.BlockSpec(memory_space=pl.ANY)


def smem():
    return pl.BlockSpec(memory_space=pltpu.SMEM)


def call(kernel, outs, ins, in_specs, out_specs, scratch=(), grid=(), aliases=None, flops=0, name=None):
    size = flops // 512
    return pl.pallas_call(
        kernel,
        out_shape=outs,
        grid=grid,
        input_output_aliases=aliases or {},
        in_specs=in_specs,
        out_specs=out_specs,
        scratch_shapes=list(scratch),
        compiler_params=pltpu.CompilerParams(vmem_limit_bytes=LIMIT),
        cost_estimate=pl.CostEstimate(flops=flops, bytes_accessed=size, transcendentals=0),
        name=name,
    )(*ins)


def shape(*dims, dtype=BF):
    return jax.ShapeDtypeStruct(dims, dtype)


def shift(v, k):
    n = lax.axis_size("dp")
    return lax.ppermute(v, "dp", [(i, (i + k) % n) for i in range(n)])


def sibling(v):
    return lax.ppermute(v, "expert", [(i, i ^ 1) for i in range(lax.axis_size("expert"))])


def near(v):
    return (v, shift(v, 1), shift(v, -1))


def halves(parts):
    half = parts[0].shape[0] // 2
    return parts + (parts[1][:half], parts[2][half:])


def far(parts):
    return parts[:3] + (shift(parts[3], 1), shift(parts[4], -1))


def ring(v):
    return far(halves(near(v)))


def exchange(v):
    devices = lax.axis_size("expert")
    groups = [[2 * i + c for i in range(devices // 2)] for c in range(2)]
    cut = v.reshape(devices // 2, 8, v.shape[1])
    cut = lax.all_to_all(
        cut, "expert", split_axis=0, concat_axis=0, axis_index_groups=groups, tiled=True
    )
    return cut.reshape(v.shape)


def body(tokens, expert_ids, gate_values, w_gate, w_up, w_down, cotangent):
    experts = lax.axis_size("expert") // 2
    micro, toks, features = tokens.shape
    q = features // 4
    width = w_gate.shape[1]
    wire = experts * 8
    n = experts * 6
    x = lax.axis_index("dp").astype(jnp.int32).reshape(1)
    gate_near, up_near, down_near = near(w_gate), near(w_up), near(w_down)

    ids = jnp.transpose(expert_ids, (0, 2, 1))
    gates = jnp.transpose(gate_values, (0, 2, 1))
    packed, place = call(
        pack_kernel,
        [shape(wire, 6 * q), shape(1, micro * toks, dtype=jnp.int32)],
        [ids, gates, tokens.reshape(-1, features), cotangent.reshape(-1, features)],
        [vmem()] * 4,
        [vmem()] * 2,
        flops=2 * 6 * wire * wire * q,
        name="pack",
    )
    arrived = exchange(packed)
    arrived, gate_near, up_near, down_near = lax.optimization_barrier(
        (arrived, halves(gate_near), halves(up_near), halves(down_near))
    )
    gate_parts, up_parts = far(gate_near), far(up_near)
    arrived_sib = sibling(arrived)
    rows = call(
        compact_kernel,
        [shape(4, 2, 2 * n, q)],
        [arrived, arrived_sib],
        [pl.BlockSpec((wire, 3 * q), lambda kind: (0, kind))] * 2,
        [pl.BlockSpec((4, 1, 2 * n, q), lambda kind: (0, kind, 0, 0))],
        grid=(2,),
        name="compact",
    )[0]
    rows, down_near = lax.optimization_barrier((rows, down_near))
    down_parts = far(down_near)
    dma = pltpu.SemaphoreType.DMA
    hid, slope, silu, to_l, to_r, to_oa, to_ob = call(
        forward_kernel,
        [shape(2 * n, width)]
        + [shape(2 * n, width, dtype=F32)] * 2
        + [shape(2, n, q)] * 2
        + [shape(2, n // 2, q)] * 2,
        [x, rows, *gate_parts, *up_parts],
        [smem()] + [hbm()] * 11,
        [vmem()] * 3 + [hbm()] * 4,
        scratch=[
            pltpu.VMEM((4, q, 2 * width), BF),
            pltpu.VMEM((4, 2 * n, q), BF),
            pltpu.VMEM((3, n, q), BF),
            pltpu.VMEM((2 * n, 2 * width), F32),
            dma((10,)),
            dma((4,)),
            dma((3,)),
            dma((8,)),
        ],
        flops=32 * 2 * n * features * width,
        name="forward",
    )
    to_l, to_r, to_oa, to_ob, down_parts = lax.optimization_barrier(
        (to_l, to_r, to_oa, to_ob, down_parts)
    )
    from_r, from_l = shift(to_l, -1), shift(to_r, 1)
    half_a, half_b = shift(to_oa, 1), shift(to_ob, -1)

    own_out, sib_out, grads = call(
        down_kernel,
        [shape(4, n, q)] * 2 + [shape(2 * n, 3 * width)],
        [x, hid, slope, silu, rows, *down_parts],
        [smem()] + [vmem()] * 3 + [hbm()] * 6,
        [hbm()] * 2 + [vmem()],
        scratch=[
            pltpu.VMEM((4, width, q), BF),
            pltpu.VMEM((4, 2 * n, q), BF),
            pltpu.VMEM((4, 2 * n, q), BF),
            dma((5,)),
            dma((4,)),
            dma((8,)),
        ],
        name="down",
    )
    own_grad, sib_grad = call(
        input_kernel,
        [shape(4, n, q)] * 2,
        [x, grads, *gate_parts, *up_parts],
        [smem()] + [vmem()] + [hbm()] * 10,
        [hbm()] * 2,
        scratch=[
            pltpu.VMEM((4, q, 2 * width), BF),
            pltpu.VMEM((4, 2 * n, q), BF),
            dma((10,)),
            dma((8,)),
        ],
        name="inputs",
    )
    parts = [
        pl.BlockSpec((1, n, q), lambda j: (j, 0, 0)),
        pl.BlockSpec((1, n, q), lambda j: (3, 0, 0)),
    ] * 2
    out_sib = sibling(sib_out)
    sib_grad, from_l, from_r = lax.optimization_barrier((sib_grad, from_l, from_r))
    grad_sib = sibling(sib_grad)
    sent = call(
        expand_kernel,
        [shape(wire, 6 * q)],
        [own_out, own_out, out_sib, out_sib],
        parts,
        [pl.BlockSpec((wire, q), lambda j: (0, j))],
        grid=(3,),
        name="expand_out",
    )[0]
    sent = call(
        lambda _, *refs: expand_kernel(*refs),
        [shape(wire, 6 * q)],
        [sent, own_grad, own_grad, grad_sib, grad_sib],
        [hbm()] + parts,
        [pl.BlockSpec((wire, q), lambda j: (0, 3 + j))],
        grid=(3,),
        aliases={0: 0},
        name="expand_grad",
    )[0]
    sent, half_a, half_b = lax.optimization_barrier((sent, half_a, half_b))
    came = exchange(sent)

    from_oa, from_ob = shift(half_a, 1), shift(half_b, -1)
    grad_parts = ring(grads)
    mine = (from_l, from_r, from_oa, from_ob)
    theirs = tuple(sibling(v) for v in mine)
    d_gate, d_up, d_down = call(
        weight_kernel,
        [shape(q, width)] * 2 + [shape(width, q)],
        [x, rows, *mine, *theirs, *grad_parts],
        [smem()] + [hbm()] * 14,
        [vmem()] * 3,
        scratch=[
            pltpu.VMEM((2, 8 * n, q), BF),
            pltpu.VMEM((8 * n, 3 * width), BF),
            dma((9,)),
            dma((5,)),
        ],
        flops=6 * 8 * n * q * width,
        name="weights",
    )
    layer_out, tokens_grad = call(
        unpack_kernel,
        [shape(micro * toks, features)] * 2,
        [place, gates, came],
        [vmem()] * 3,
        [vmem()] * 2,
        flops=2 * 6 * wire * wire * q,
        name="unpack",
    )
    return (
        layer_out.reshape(tokens.shape),
        tokens_grad.reshape(tokens.shape),
        d_gate,
        d_up,
        d_down,
    )


def solution(mesh):
    rows = P(None, ("dp", "expert"), None)
    return jax.shard_map(
        body,
        mesh=mesh,
        in_specs=(rows, rows, rows, P("dp", "expert"), P("dp", "expert"), P("expert", "dp"), rows),
        out_specs=(rows, rows, P("dp", "expert"), P("dp", "expert"), P("expert", "dp")),
        check_vma=False,
    )
```
